32 devices in a mesh: tm: 4 (over x, core), batch: 8 (over z, y).
Axes of the slice: x: 2, y: 2, z: 4, core: 2. Of those that a mesh axis runs over, the one named last changes fastest.
Arguments:
- video: bfloat16 [64, 16, 7, 7, 192], P('batch', 'tm'), may hold values from -12 to 12
- video_ids: int32 [64], P('batch'), may hold values from 0 to 63, as said below
- crop_scales: int32 [64], P('batch'), may hold values from 0 to 3
- labels: int32 [64], P('batch'), may hold values from 0 to 399
- valid_clips: int32 [64], P('batch'), may hold values from 0 to 1, as said below
- stem_weight: float32 [2304, 192], P('batch'), may hold values from -0.4375 to 0.4375
- lateral_weight: float32 [512, 1280], P('batch'), may hold values from -0.15625 to 0.15625
- condense: float32 [512, 6144], P('batch'), may hold values from -0.078125 to 0.078125
- mixing: float32 [512, 4608], P('batch'), may hold values from -0.09375 to 0.09375
- restore: float32 [2048, 512], P('batch'), may hold values from -0.25 to 0.25
- squeeze: float32 [64, 768], P('batch'), may hold values from -0.21875 to 0.21875
- blending: float32 [64, 576], P('batch'), may hold values from -0.25 to 0.25
- recover: float32 [256, 64], P('batch'), may hold values from -0.75 to 0.75
- head_weight: float32 [2304, 400], P('batch'), may hold values from -0.125 to 0.125
- stem_velocity: float32 [2304, 192], P('batch'), may hold values from -1.9073486e-05 to 1.9073486e-05
- lateral_velocity: float32 [512, 1280], P('batch'), may hold values from -1.9073486e-05 to 1.9073486e-05
- condense_velocity: float32 [512, 6144], P('batch'), may hold values from -1.9073486e-05 to 1.9073486e-05
- mixing_velocity: float32 [512, 4608], P('batch'), may hold values from -1.9073486e-05 to 1.9073486e-05
- restore_velocity: float32 [2048, 512], P('batch'), may hold values from -1.9073486e-05 to 1.9073486e-05
- squeeze_velocity: float32 [64, 768], P('batch'), may hold values from -1.9073486e-05 to 1.9073486e-05
- blending_velocity: float32 [64, 576], P('batch'), may hold values from -1.9073486e-05 to 1.9073486e-05
- recover_velocity: float32 [256, 64], P('batch'), may hold values from -1.9073486e-05 to 1.9073486e-05
- head_moment: float32 [2304, 400], P('batch'), may hold values from -2.3841858e-06 to 2.3841858e-06
- head_square: float32 [2304, 400], P('batch'), may hold values from 1.1517234e-14 to 4.6068936e-14
- affine: float32 [7312], replicated, may hold values from -1 to 7, as said below
- affine_moment: float32 [7312], replicated, may hold values from -1.1444092e-05 to 1.1444092e-05
- affine_square: float32 [7312], replicated, may hold values from 2.8793087e-13 to 1.1517235e-12
Outputs:
- stem_carried: float32 [2304, 192], P('batch')
- lateral_carried: float32 [512, 1280], P('batch')
- condense_carried: float32 [512, 6144], P('batch')
- mixing_carried: float32 [512, 4608], P('batch')
- restore_carried: float32 [2048, 512], P('batch')
- squeeze_carried: float32 [64, 768], P('batch')
- blending_carried: float32 [64, 576], P('batch')
- recover_carried: float32 [256, 64], P('batch')
- stem_updated: float32 [2304, 192], P('batch')
- lateral_updated: float32 [512, 1280], P('batch')
- condense_updated: float32 [512, 6144], P('batch')
- mixing_updated: float32 [512, 4608], P('batch')
- restore_updated: float32 [2048, 512], P('batch')
- squeeze_updated: float32 [64, 768], P('batch')
- blending_updated: float32 [64, 576], P('batch')
- recover_updated: float32 [256, 64], P('batch')
- head_updated: float32 [2304, 400], P('batch')
- moment_head: float32 [2304, 400], P('batch')
- square_head: float32 [2304, 400], P('batch')
- affine_updated: float32 [7312], replicated
- moment_affine: float32 [7312], replicated
- square_affine: float32 [7312], replicated
- loss_total: float32 [], replicated
- clip_count: float32 [], replicated
- grad_norm: float32 [], replicated
The draws below stay inside these ranges and needn't reach their ends.
Inputs may be any that keep to these rules, and one draw needn't show every extreme that they name: `video_ids`: never falling; clips that share an id lie in one aligned block of 8 clips; the last clip of every block has id (block index + 1) * 8 - 1. `valid_clips`: zero or one. `affine`: gains are positive.
All inputs are finite; a program needn't handle non-finite values.
Results may differ from the reference program's by a relative error of at most 0.005.
Values may be sent and summed in bfloat16 or wider, within the bound.
No kernel may reach another device: no remote copies, remote signals or barrier semaphores. Data moves between devices by JAX's collectives and lax.ppermute only.
A program may use at most 256 MiB of HBM per device.

```python
import math
import jax
import jax.numpy as jnp
from jax import lax

CS = 2048
CSM = 512
CF = 256
CFM = 64
CLS = 400
PIX = 192
CLIP_DEV = 8
ALPHA = 4
SP = 7
NSCALE = 4
NS_STEPS = 3
STEP = 10
CLIPS = 64
TS = 4
TF = 16
AFF = 7312
PARAMS = 8682640


def draw_video(key, part):
    key = jax.random.fold_in(key, 11)
    shape = (CLIPS, TF, SP, SP, PIX)
    clip_place = jnp.arange(CLIPS).astype(jnp.float32) / max(CLIPS - 1, 1)
    frame_place = jnp.arange(TF).astype(jnp.float32) / max(TF - 1, 1)
    rise = 3.0
    base = jnp.clip(jax.random.normal(key, shape, jnp.float32), -4.0, 4.0)
    growth = rise ** (0.5 * (clip_place[:, None] + frame_place[None, :]))
    return (base * growth[:, :, None, None, None]).astype(jnp.bfloat16)


def draw_video_ids(key, part):
    key = jax.random.fold_in(key, 23)
    starts = jax.random.randint(key, (CLIPS,), 0, 2)
    within = jnp.arange(CLIPS) % CLIP_DEV
    starts = jnp.where(within == 0, 1, starts).reshape(CLIPS // CLIP_DEV, CLIP_DEV)
    later = jnp.sum(starts, axis=1, keepdims=True) - jnp.cumsum(starts, axis=1)
    blocks = jnp.arange(CLIPS // CLIP_DEV)[:, None] * CLIP_DEV
    return (blocks + CLIP_DEV - 1 - later).reshape(CLIPS).astype(jnp.int32)


def draw_valid_clips(key, part):
    key = jax.random.fold_in(key, 37)
    chance = 30 + 60 * jnp.arange(CLIPS) // max(CLIPS - 1, 1)
    rolled = jax.random.randint(key, (CLIPS,), 0, 100)
    return (rolled < chance).astype(jnp.int32)


def draw_affine(key, part):
    key = jax.random.fold_in(key, 41)
    first, second = jax.random.split(key, 2)
    widths = (CSM, CSM, CS, CFM, CFM, CF)
    place = jnp.concatenate([jnp.arange(width).astype(jnp.float32) / (width - 1) for width in widths])
    total = place.shape[0]
    rise = 3.0
    noise = jax.random.uniform(first, (total,), jnp.float32, 0.8, 1.2)
    shifts = jnp.clip(0.3 * jax.random.normal(second, (total + CLS,), jnp.float32), -1.0, 1.0)
    gains = rise ** place * noise
    return jnp.concatenate([gains, shifts])


def place_ends(drawn, own_key, least, high):
    index_at = [jax.random.randint(jax.random.fold_in(own_key, axis), (), 0, length) for axis, length in enumerate(drawn.shape)]
    main_axis = drawn.shape.index(max(drawn.shape))
    neighbour = index_at[:main_axis] + [(index_at[main_axis] + 1) % drawn.shape[main_axis]] + index_at[main_axis + 1:]
    return drawn.at[tuple(index_at)].set(least).at[tuple(neighbour)].set(high)


def shard_levels(rng, extent, cuts, least, top_value):
    def one(dim, shards_of):
        draws = jax.random.uniform(jax.random.fold_in(jax.random.fold_in(rng, 6), dim), (shards_of,), jnp.float32, least / len(cuts), top_value / len(cuts))
        return jnp.repeat(jnp.exp(draws), extent[dim] // shards_of).reshape((-1,) + (1,) * (len(extent) - dim - 1))

    level = one(*cuts[0])
    for cut in cuts[1:]:
        level = level * one(*cut)
    return level


def gaussian(own_key, extent, scale, reach, shards=(), kind=jnp.bfloat16):
    loudness = shard_levels(own_key, extent, shards, -0.22, 0.18) if shards else 1.0
    entries = jax.random.normal(own_key, extent, jnp.float32) * scale * loudness
    return jnp.minimum(jnp.maximum(entries, -reach), reach).astype(kind)


def setup_inputs(seed: int = 0) -> dict:
    keys = jax.random.split(jax.random.key(seed), 28)
    return {
        "video": draw_video(jax.random.fold_in(keys[27], 71), 0),
        "video_ids": draw_video_ids(jax.random.fold_in(keys[27], 71), 0),
        "crop_scales": place_ends(jax.random.randint(keys[2], (CLIPS,), 0, NSCALE), jax.random.fold_in(keys[2], 1), 0, NSCALE - 1).astype(jnp.int32),
        "labels": place_ends(jax.random.randint(keys[3], (CLIPS,), 0, CLS), jax.random.fold_in(keys[3], 1), 0, CLS - 1).astype(jnp.int32),
        "valid_clips": draw_valid_clips(jax.random.fold_in(keys[27], 71), 0),
        "stem_weight": gaussian(keys[5], (CS + CF, PIX), PIX ** -0.5, 0.4375, ((0, 8),), jnp.float32),
        "lateral_weight": gaussian(keys[6], (CSM, 5 * CF), (5 * CF) ** -0.5, 0.15625, ((0, 8),), jnp.float32),
        "condense": gaussian(keys[7], (CSM, 3 * CS), (3 * CS) ** -0.5, 0.078125, ((0, 8),), jnp.float32),
        "mixing": gaussian(keys[8], (CSM, 9 * CSM), (9 * CSM) ** -0.5, 0.09375, ((0, 8),), jnp.float32),
        "restore": gaussian(keys[9], (CS, CSM), CSM ** -0.5, 0.25, ((0, 8),), jnp.float32),
        "squeeze": gaussian(keys[10], (CFM, 3 * CF), (3 * CF) ** -0.5, 0.21875, ((0, 8),), jnp.float32),
        "blending": gaussian(keys[11], (CFM, 9 * CFM), (9 * CFM) ** -0.5, 0.25, ((0, 8),), jnp.float32),
        "recover": gaussian(keys[12], (CF, CFM), CFM ** -0.5, 0.75, ((0, 8),), jnp.float32),
        "head_weight": gaussian(keys[13], (CS + CF, CLS), (CS + CF) ** -0.5, 0.125, ((0, 8),), jnp.float32),
        "stem_velocity": gaussian(keys[14], (CS + CF, PIX), (0.01 * PARAMS ** -0.5), 1.9073486328125e-05, ((0, 8),), jnp.float32),
        "lateral_velocity": gaussian(keys[15], (CSM, 5 * CF), (0.01 * PARAMS ** -0.5), 1.9073486328125e-05, ((0, 8),), jnp.float32),
        "condense_velocity": gaussian(keys[16], (CSM, 3 * CS), (0.01 * PARAMS ** -0.5), 1.9073486328125e-05, ((0, 8),), jnp.float32),
        "mixing_velocity": gaussian(keys[17], (CSM, 9 * CSM), (0.01 * PARAMS ** -0.5), 1.9073486328125e-05, ((0, 8),), jnp.float32),
        "restore_velocity": gaussian(keys[18], (CS, CSM), (0.01 * PARAMS ** -0.5), 1.9073486328125e-05, ((0, 8),), jnp.float32),
        "squeeze_velocity": gaussian(keys[19], (CFM, 3 * CF), (0.01 * PARAMS ** -0.5), 1.9073486328125e-05, ((0, 8),), jnp.float32),
        "blending_velocity": gaussian(keys[20], (CFM, 9 * CFM), (0.01 * PARAMS ** -0.5), 1.9073486328125e-05, ((0, 8),), jnp.float32),
        "recover_velocity": gaussian(keys[21], (CF, CFM), (0.01 * PARAMS ** -0.5), 1.9073486328125e-05, ((0, 8),), jnp.float32),
        "head_moment": gaussian(keys[22], (CS + CF, CLS), (0.0011 * PARAMS ** -0.5), 2.384185791015625e-06, ((0, 8),), jnp.float32),
        "head_square": jnp.clip(jnp.exp(math.log(4.606893615503524e-14) - 1.3862944 * jax.random.uniform(keys[23], (CS + CF, CLS), jnp.float32) ** shard_levels(keys[23], (CS + CF, CLS), ((0, 8),), -0.2, 0.2)), 1.151723403875881e-14, 4.606893615503524e-14),
        "affine": draw_affine(jax.random.fold_in(keys[27], 71), 0),
        "affine_moment": gaussian(keys[25], (AFF,), (0.0055 * PARAMS ** -0.5), 1.1444091796875e-05, (), jnp.float32),
        "affine_square": jnp.clip(jnp.exp(jax.random.uniform(keys[26], (AFF,), jnp.float32, math.log(2.879308662155633e-13), math.log(1.1517234648622532e-12))), 2.879308662155633e-13, 1.1517234648622532e-12),
    }


HIGHEST = lax.Precision.HIGHEST
NORM_EPS = 1e-05
CLIP_AT = 0.01
MUON_RATE = 0.5
MUON_KEEP = 0.95
WEIGHT_DECAY = 0.01
ADAM_ONE = 0.9
ADAM_TWO = 0.999
ADAM_EPS = 1e-08
HEAD_RATE = 0.02
AFFINE_RATE = 0.1
NS_FIRST = 3.4445
NS_SECOND = -4.775
NS_THIRD = 2.0315

@jax.custom_vjp
def low(v):
    return lax.optimization_barrier(v.astype(jnp.bfloat16)).astype(jnp.float32)

@jax.custom_vjp
def low_back(v):
    return v

def low_keep(v):
    return (low(v), None)

def low_pass(kept, grad):
    return (grad,)

def back_keep(v):
    return (v, None)

def back_low(kept, grad):
    return (low(grad),)
low.defvjp(low_keep, low_pass)
low_back.defvjp(back_keep, back_low)

def split_affine(vector):
    widths = (CSM, CSM, CS, CFM, CFM, CF)
    gains = []
    shifts = []
    start = 0
    for width in widths:
        gains.append(vector[start:start + width])
        start = start + width
    for width in widths:
        shifts.append(vector[start:start + width])
        start = start + width
    return (gains, shifts, vector[start:start + CLS])

def project(inputs, weight):
    return lax.dot_general(inputs, weight, (((inputs.ndim - 1,), (1,)), ((), ())), precision=HIGHEST)

def temporal(inputs, weight):
    width = inputs.shape[-1]
    frames = inputs.shape[1]
    padded = jnp.pad(inputs, ((0, 0), (1, 1), (0, 0), (0, 0), (0, 0)))
    total = project(padded[:, 0:frames], weight[:, 0:width])
    for offset in range(1, 3):
        total = total + project(padded[:, offset:offset + frames], weight[:, offset * width:(offset + 1) * width])
    return total

def spatial(inputs, weight):
    width = inputs.shape[-1]
    height = inputs.shape[2]
    padded = jnp.pad(inputs, ((0, 0), (0, 0), (1, 1), (1, 1), (0, 0)))
    total = None
    for tap in range(9):
        down, across = (tap // 3, tap % 3)
        term = project(padded[:, :, down:down + height, across:across + height], weight[:, tap * width:(tap + 1) * width])
        total = term if total is None else total + term
    return total

def lateral(fast, weight):
    width = fast.shape[-1]
    slow_frames = fast.shape[1] // ALPHA
    padded = jnp.pad(fast, ((0, 0), (2, 2), (0, 0), (0, 0), (0, 0)))
    total = None
    for offset in range(5):
        picked = padded[:, offset:offset + ALPHA * slow_frames:ALPHA]
        term = project(picked, weight[:, offset * width:(offset + 1) * width])
        total = term if total is None else total + term
    return total

def normalize(values, gain, shift, mask, count):
    total = lax.optimization_barrier(jnp.sum(mask * values, axis=(0, 1, 2, 3)))
    squares = lax.optimization_barrier(jnp.sum(mask * values * values, axis=(0, 1, 2, 3)))
    mean = total / count
    spread = squares / count - mean * mean
    scaled = (values - mean) * lax.rsqrt(spread + NORM_EPS)
    return gain * scaled + shift

def branch(source, source_low, added, reduce_weight, middle_weight, expand_weight, gains, shifts, mask, count):
    first = low_back(temporal(source_low, reduce_weight) + added)
    act_one = low(jax.nn.silu(normalize(first, gains[0], shifts[0], mask, count)) * mask)
    second = low_back(spatial(act_one, middle_weight))
    act_two = low(jax.nn.silu(normalize(second, gains[1], shifts[1], mask, count)) * mask)
    third = low_back(project(act_two, expand_weight))
    output = jax.nn.silu(source + normalize(third, gains[2], shifts[2], mask, count)) * mask
    return lax.optimization_barrier(jnp.sum(output, axis=(1, 2, 3)))

def forward(mats, affine, frames, mask, area, average, onehot, valid):
    stem, side, condense, mixing, restore, squeeze, blending, recover, head = [low(item) for item in mats]
    gains, shifts, class_bias = split_affine(affine)
    slow_pre = low_back(project(frames[:, ::ALPHA], stem[0:CS]))
    fast_pre = low_back(project(frames, stem[CS:]))
    slow_x = jax.nn.silu(slow_pre) * mask
    fast_x = jax.nn.silu(fast_pre) * mask
    slow_low = low(slow_x)
    fast_low = low(fast_x)
    area_sum = jnp.sum(area)
    added = lateral(fast_low, side)
    slow_pool = jax.checkpoint(branch)(slow_x, slow_low, added, condense, mixing, restore, gains[0:3], shifts[0:3], mask, area_sum * TS)
    fast_pool = jax.checkpoint(branch)(fast_x, fast_low, jnp.float32(0.0), squeeze, blending, recover, gains[3:6], shifts[3:6], mask, area_sum * TF)
    features = jnp.concatenate([slow_pool / (TS * area)[:, None], fast_pool / (TF * area)[:, None]], axis=1)
    logits = low_back(jnp.dot(low(features), head, precision=HIGHEST) + class_bias)
    mean_logits = jnp.dot(average, logits, precision=HIGHEST)
    log_norm = jax.nn.logsumexp(mean_logits, axis=1)
    picked = lax.optimization_barrier(jnp.sum(onehot * mean_logits, axis=1))
    return jnp.sum(valid * (log_norm - picked))

def orthogonalize(matrix):
    rows, columns = matrix.shape
    wide = matrix.T if rows > columns else matrix
    wide = wide / (jnp.sqrt(jnp.sum(wide * wide)) + 1e-07)
    for step in range(NS_STEPS):
        gram = jnp.dot(wide, wide.T, precision=HIGHEST)
        poly = NS_SECOND * gram + NS_THIRD * jnp.dot(gram, gram, precision=HIGHEST)
        wide = NS_FIRST * wide + jnp.dot(poly, wide, precision=HIGHEST)
    return wide.T if rows > columns else wide

def adam(weight, moment, square, grad, rate, decay):
    moment = ADAM_ONE * moment + (1.0 - ADAM_ONE) * grad
    square = ADAM_TWO * square + (1.0 - ADAM_TWO) * grad * grad
    fixed_one = 1.0 - ADAM_ONE ** STEP
    fixed_two = 1.0 - ADAM_TWO ** STEP
    weight = weight - rate * (moment / fixed_one / (jnp.sqrt(square / fixed_two) + ADAM_EPS) + decay * weight)
    return (weight, moment, square)

def reference(video, video_ids, crop_scales, labels, valid_clips, stem_weight, lateral_weight, condense, mixing, restore, squeeze, blending, recover, head_weight, stem_velocity, lateral_velocity, condense_velocity, mixing_velocity, restore_velocity, squeeze_velocity, blending_velocity, recover_velocity, head_moment, head_square, affine, affine_moment, affine_square):
    mats = (stem_weight, lateral_weight, condense, mixing, restore, squeeze, blending, recover, head_weight)
    velocities = (stem_velocity, lateral_velocity, condense_velocity, mixing_velocity, restore_velocity, squeeze_velocity, blending_velocity, recover_velocity)
    side = (SP - crop_scales).astype(jnp.float32)
    places = jnp.arange(SP).astype(jnp.float32)
    inside = (places[None, :] < side[:, None]).astype(jnp.float32)
    mask = (inside[:, :, None] * inside[:, None, :])[:, None, :, :, None]
    area = side * side
    same = (video_ids[:, None] == video_ids[None, :]).astype(jnp.float32)
    average = same / lax.optimization_barrier(jnp.sum(same, axis=1, keepdims=True))
    onehot = (labels[:, None] == jnp.arange(CLS).astype(jnp.int32)[None, :]).astype(jnp.float32)
    valid = valid_clips.astype(jnp.float32)
    frames = video.astype(jnp.float32)

    def loss_of(weights, vector):
        return forward(weights, vector, frames, mask, area, average, onehot, valid)
    loss_total, pullback = jax.vjp(loss_of, mats, affine)
    grads, affine_grad = pullback(jnp.ones((), jnp.float32))
    clip_count = jnp.sum(valid)
    grads = [item / clip_count for item in grads]
    affine_grad = affine_grad / clip_count
    squares = jnp.sum(affine_grad * affine_grad)
    for item in grads:
        squares = squares + jnp.sum(item * item)
    grad_norm = jnp.sqrt(squares)
    factor = jnp.minimum(1.0, CLIP_AT / grad_norm)
    grads = [item * factor for item in grads]
    affine_grad = affine_grad * factor
    carried = []
    updated = []
    for weight, velocity, grad in zip(mats[0:8], velocities, grads[0:8]):
        moved = MUON_KEEP * velocity + grad
        ortho = low(orthogonalize(low(moved)))
        rows, columns = weight.shape
        carried.append(moved)
        updated.append(weight - MUON_RATE * (ortho * math.sqrt(max(1.0, rows / columns)) + WEIGHT_DECAY * weight))
    head_new, head_first, head_second = adam(head_weight, head_moment, head_square, grads[8], HEAD_RATE, WEIGHT_DECAY)
    affine_new, affine_first, affine_second = adam(affine, affine_moment, affine_square, affine_grad, AFFINE_RATE, 0.0)
    return (carried[0], carried[1], carried[2], carried[3], carried[4], carried[5], carried[6], carried[7], updated[0], updated[1], updated[2], updated[3], updated[4], updated[5], updated[6], updated[7], head_new, head_first, head_second, affine_new, affine_first, affine_second, loss_total, clip_count, grad_norm)
```

```python
import functools
import math

import jax
import jax.numpy as jnp
from jax import lax
from jax.experimental import pallas as pl
from jax.experimental.pallas import tpu as pltpu
from jax.sharding import PartitionSpec as P

CS = 2048
CSM = 512
CF = 256
CFM = 64
CLS = 400
ALPHA = 4
NS_STEPS = 3
STEP = 10


HIGHEST = lax.Precision.HIGHEST
NORM_EPS = 1e-05
CLIP_AT = 0.01
MUON_RATE = 0.5
MUON_KEEP = 0.95
WEIGHT_DECAY = 0.01
ADAM_ONE = 0.9
ADAM_TWO = 0.999
ADAM_EPS = 1e-08
HEAD_RATE = 0.02
AFFINE_RATE = 0.1
NS_FIRST = 3.4445
NS_SECOND = -4.775
NS_THIRD = 2.0315


F32 = jnp.float32
BF16 = jnp.bfloat16
VMEM = 61 * 1024 * 1024
SIDE_AT = 9 * CSM
CONDENSE_AT = SIDE_AT + 5 * CF
RESTORE_AT = CONDENSE_AT + 3 * CS
GRAM = BF16
SIX = (CSM, CSM, CS, CFM, CFM, CF)


def swap(values, axis, mask):
    count = lax.axis_size(axis)
    return lax.ppermute(values, axis, [(i, i ^ mask) for i in range(count)])


def shift(values, axis, step):
    count = lax.axis_size(axis)
    route = [(i, i + step) for i in range(count) if 0 <= i + step < count]
    return lax.ppermute(values, axis, route)


def spread_all(rows, axes):
    count = math.prod(lax.axis_size(axis) for axis in axes)
    copies = jnp.broadcast_to(rows[None], (count,) + rows.shape)
    return lax.all_to_all(copies, axes, 0, 0, tiled=True)


def all_sum(pieces, axes):
    flat = jnp.concatenate([piece.reshape(-1) for piece in pieces])
    length = flat.shape[0]
    wide = -(-length // 1024) * 128
    flat = jnp.pad(flat, (0, 8 * wide - length)).reshape(8, wide)
    total = jnp.sum(spread_all(flat, axes), axis=0).reshape(-1)
    parts = []
    start = 0
    for piece in pieces:
        parts.append(total[start : start + piece.size].reshape(piece.shape))
        start = start + piece.size
    return parts


def pick(values, dim, place):
    return lax.dynamic_index_in_dim(values, place, dim, keepdims=False)


def bits(axis, low):
    count = lax.axis_size(axis).bit_length() - 1
    return [(axis, bit) for bit in range(count - 1, low - 1, -1)]


def halve(view, live, order):
    live = list(live)
    for axis, bit in order:
        dim = live.index((axis, bit))
        flag = (lax.axis_index(axis) >> bit) & 1
        got = swap(pick(view, dim, 1 - flag).astype(BF16), axis, 1 << bit)
        view = pick(view, dim, flag) + got.astype(F32)
        live.remove((axis, bit))
    return view


def dot(left, right, dims):
    return lax.dot_general(left, right, ((dims[0], dims[1]), ((), ())), preferred_element_type=F32)


def rows_by_rows(left, right):
    return dot(left, right, ((1,), (1,)))


def rows_by_columns(left, right):
    return dot(left, right, ((1,), (0,)))


def over_rows(left, right):
    return dot(left, right, ((0,), (0,)))


def split_affine(vector):
    gains = []
    shifts = []
    start = 0
    for width in SIX:
        gains.append(vector[start : start + width])
        start = start + width
    for width in SIX:
        shifts.append(vector[start : start + width])
        start = start + width
    return (gains, shifts, vector[start : start + CLS])


def silu_grad(values):
    sigma = jax.nn.sigmoid(values)
    return sigma * (1.0 + values * (1.0 - sigma))


def call(kernel, outs, args, scratch=(), far=(), copies=0, micros=6, scalars=()):
    specs = [
        pl.BlockSpec(
            memory_space=pl.ANY
            if place in far
            else pltpu.SMEM
            if place in scalars
            else pltpu.VMEM
        )
        for place in range(len(args))
    ]
    shapes = [pltpu.VMEM(shape, kind) for shape, kind in scratch]
    if copies:
        shapes.append(pltpu.SemaphoreType.DMA((copies,)))
    return pl.pallas_call(
        kernel,
        in_specs=specs,
        out_shape=[jax.ShapeDtypeStruct(shape, kind) for shape, kind in outs],
        scratch_shapes=shapes,
        compiler_params=pltpu.CompilerParams(vmem_limit_bytes=VMEM),
        cost_estimate=pl.CostEstimate(
            flops=micros * 1150000000, bytes_accessed=micros * 3000000, transcendentals=0
        ),
    )(*args)


def fetch(source, target, flags, spans):
    started = []
    for place, (there, here, width) in enumerate(spans):
        copy = pltpu.make_async_copy(
            source.at[:, pl.ds(there, width)], target.at[:, pl.ds(here, width)], flags.at[place]
        )
        copy.start()
        started.append(copy)
    return started


def fetch_tall(source, target, flags, start):
    started = []
    count = flags.shape[0] // 4
    block = source.shape[0] // count
    for place in range(4 * count):
        b, k = (place // 4, place % 4)
        copy = pltpu.make_async_copy(
            source.at[pl.ds(b * block, block), pl.ds(start + k * CSM, CSM)],
            target.at[pl.ds(place * block, block), :],
            flags.at[place],
        )
        copy.start()
        started.append(copy)
    return started


def nt(left, right):
    return dot(left, right, ((1,), (1,)))


def nn(left, right):
    return dot(left, right, ((1,), (0,)))


def silu(values):
    return values * jax.nn.sigmoid(values)


def low(values):
    return values.astype(BF16)


def sums(held, other):
    return (
        jnp.sum(held, axis=0, keepdims=True),
        jnp.sum(held * other, axis=0, keepdims=True),
    )


def flat(values):
    return values.reshape(values.shape[0] * values.shape[1], values.shape[2])


def put_narrow(out, block, slow, fast, extra=()):
    block[...] = jnp.zeros_like(block)
    for place, vector in enumerate(slow):
        block[2 * place : 2 * place + 1, :] = vector[:, 0:256]
        block[2 * place + 1 : 2 * place + 2, :] = vector[:, 256:512]
    for place, vector in enumerate(fast):
        block[4 + place : 5 + place, 0:CFM] = vector
    for place, value in enumerate(extra):
        block[6 + place : 7 + place, 0:128] = jnp.broadcast_to(value, (1, 128))
    out[...] = jnp.broadcast_to(block[...][None], out.shape).astype(out.dtype)


def get_narrow(total):
    slow = [
        jnp.concatenate([total[2 * k : 2 * k + 1], total[2 * k + 1 : 2 * k + 2]], axis=1)
        for k in range(2)
    ]
    fast = [total[4 + k : 5 + k, 0:CFM] for k in range(2)]
    return slow, fast


def put_wide(out, slow, fast, extra=None):
    out[...] = jnp.zeros_like(out)
    for place, vector in enumerate(slow):
        for row in range(4):
            out[4 * place + row : 4 * place + row + 1, 0:512] = vector[:, 512 * row : 512 * row + 512]
    for place, vector in enumerate(fast):
        for row in range(2):
            spot = 2 * place + row
            out[spot : spot + 1, 512:640] = vector[:, 128 * row : 128 * row + 128]
    if extra is not None:
        for row in range(4, 7):
            part = low(jnp.broadcast_to(extra, (1, 128))).astype(F32)
            out[row : row + 1, 512:640] = part
            extra = extra - part


def get_wide(total):
    slow = [
        jnp.concatenate([total[4 * k + row : 4 * k + row + 1, 0:512] for row in range(4)], axis=1)
        for k in range(2)
    ]
    fast = [
        jnp.concatenate(
            [total[2 * k + row : 2 * k + row + 1, 512:640] for row in range(2)], axis=1
        )
        for k in range(2)
    ]
    return slow, fast


def moments(pair, count):
    mean = pair[0] / count
    spread = pair[1] / count - mean * mean
    return mean, lax.rsqrt(spread + NORM_EPS)


def counts(total, frames):
    count = total[6:7, 0:1]
    return count, count * frames


def in_relation(place, outs, values):
    for k, out in enumerate(outs):
        for p, value in enumerate(values):

            @pl.when(jnp.bitwise_xor(place, k) == p)
            def store(out=out, value=value):
                out[...] = value


def stem_kernel(
    near, place, slow_video, fast_video, weight, mask, slow_pre, fast_pre, slow_low, fast_low, *shares
):
    held = mask[...]
    for k in range(3):
        pre = nt(slow_video[k], weight[0:CS, :])
        if k == 1:
            slow_pre[...] = pre
        act = low(silu(pre) * held)
        slow_low[k] = act
        if k == 1 and near:
            width = CS // 4
            parts = [act[:, p * width : (p + 1) * width] for p in range(4)]
            in_relation(place[0], shares[0:4], parts)
        elif k == 1:
            count, _, width = shares[0].shape
            for p in range(count):
                shares[0][p] = act[:, p * width : (p + 1) * width]
    count = fast_video.shape[0]
    for k in range(count):
        pre = nt(fast_video[k], weight[CS:, :])
        if 2 <= k < count - 1:
            fast_pre[k - 2] = pre
        act = low(silu(pre) * held)
        fast_low[k] = act
        if near and k < 5:
            parts = [act[:, 0:128], act[:, 128:256]]
            in_relation(place[0] // 2, [side.at[k] for side in shares[4:6]], parts)


def first_kernel(
    slow_low, fast_low, weights, squeeze, mask, valid, h1, h4, out, block, first, flags
):
    spans = [(SIDE_AT, 0, 5 * CF)]
    spans += [(CONDENSE_AT + k * CS, 5 * CF + k * CS, CS) for k in range(3)]
    copies = fetch(weights, first, flags, spans)
    held = mask[...]
    copies[0].wait()
    total = None
    for k in range(5):
        term = nt(fast_low[k], first[:, k * CF : (k + 1) * CF])
        total = term if total is None else total + term
    for k in range(3):
        start = 5 * CF + k * CS
        copies[1 + k].wait()
        total = total + nt(slow_low[k], first[:, start : start + CS])
    h1[...] = total
    slow = sums(total * held, total)
    frames = h4.shape[0]
    fast = None
    for frame in range(frames):
        piece = None
        for k in range(3):
            term = nt(fast_low[1 + k + frame], squeeze[:, k * CF : (k + 1) * CF])
            piece = term if piece is None else piece + term
        h4[frame] = piece
        pair = sums(piece * held, piece)
        fast = pair if fast is None else tuple(a + b for a, b in zip(fast, pair))
    put_narrow(out, block, slow, fast, (jnp.sum(held), jnp.sum(valid[...])))


def fill(pad, values):
    side = pad.shape[0] - 2
    pad[1 : side + 1, 1 : side + 1] = values.reshape(side, side, pad.shape[2], pad.shape[3])


def tap_of(pad, down, right):
    side = pad.shape[0] - 2
    values = pad[down : down + side, right : right + side]
    return values.reshape(side * side * pad.shape[2], pad.shape[3])


def second_kernel(near, *refs):
    place, h1, h4, got, slow_par, fast_par, mask, weights, blending = refs[0:9]
    h2, h5, total_out, out = refs[9:13]
    shares = refs[13:17] if near else refs[13:14]
    pad, fast_pad, block, mixing, flags = refs[-5:]
    copies = fetch(weights, mixing, flags, [(tap * CSM, tap * CSM, CSM) for tap in range(9)])
    held = mask[...]
    frames = h4.shape[0]
    total = jnp.sum(got[...].astype(F32), axis=0)
    total_out[...] = total
    slow, fast = get_narrow(total)
    slow_count, fast_count = counts(total, frames)
    mean, inverse = moments(slow, slow_count)
    level = slow_par[0:1] * ((h1[...] - mean) * inverse) + slow_par[1:2]
    pad[...] = jnp.zeros_like(pad)
    act = low(silu(level) * held)
    if near:
        in_relation(place[0], shares, [act[:, p * 128 : (p + 1) * 128] for p in range(4)])
    else:
        shares[0][...] = act
    fill(pad, act.astype(F32))
    acc = None
    for tap in range(9):
        piece = low(tap_of(pad, tap // 3, tap % 3))
        copies[tap].wait()
        term = nt(piece, mixing[:, tap * CSM : (tap + 1) * CSM])
        acc = term if acc is None else acc + term
    h2[...] = acc
    slow_pair = sums(acc * held, acc)
    mean, inverse = moments(fast, fast_count)
    fast_pad[...] = jnp.zeros_like(fast_pad)
    fast_pair = None
    for frame in range(frames):
        level = fast_par[0:1] * ((h4[frame] - mean) * inverse) + fast_par[1:2]
        fill(fast_pad, low(silu(level) * held).astype(F32))
        acc = None
        for tap in range(9):
            piece = low(tap_of(fast_pad, tap // 3, tap % 3))
            term = nn(piece, blending[tap])
            acc = term if acc is None else acc + term
        h5[frame] = acc
        pair = sums(acc * held, acc)
        fast_pair = pair if fast_pair is None else tuple(a + b for a, b in zip(fast_pair, pair))
    put_narrow(out, block, slow_pair, fast_pair)


def third_kernel(
    h2, h5, before, got, slow_par, fast_par, mask, weights, recover, a2, a5, h3, h6, total_out, out,
    restore, flags,
):
    copies = fetch_tall(weights, restore, flags, RESTORE_AT)
    held = mask[...]
    frames = h5.shape[0]
    total = jnp.sum(got[...].astype(F32), axis=0)
    total_out[...] = total
    slow, fast = get_narrow(total)
    slow_count, fast_count = counts(before[...], frames)
    mean, inverse = moments(slow, slow_count)
    level = slow_par[0:1] * ((h2[...] - mean) * inverse) + slow_par[1:2]
    act = low(silu(level) * held)
    a2[...] = act
    for copy in copies:
        copy.wait()
    acc = nt(act, restore[...])
    h3[...] = acc
    slow_pair = sums(acc * held, acc)
    mean, inverse = moments(fast, fast_count)
    fast_pair = None
    for frame in range(frames):
        level = fast_par[0:1] * ((h5[frame] - mean) * inverse) + fast_par[1:2]
        act = low(silu(level) * held)
        a5[frame] = act
        acc = nt(act, recover[...])
        h6[frame] = acc
        pair = sums(acc * held, acc)
        fast_pair = pair if fast_pair is None else tuple(a + b for a, b in zip(fast_pair, pair))
    put_wide(out, slow_pair, fast_pair)


def by_clip(values, clips):
    return jnp.sum(values.reshape(-1, clips, values.shape[1]), axis=0)


def pool_kernel(
    h3, h6, slow_pre, fast_pre, before, got, slow_par, fast_par, mask, out, total_out
):
    held = mask[...]
    frames = h6.shape[0]
    clips = out.shape[0]
    total = jnp.sum(got[...].astype(F32), axis=0)
    total_out[...] = total
    slow, fast = get_wide(total)
    slow_count, fast_count = counts(before[...], frames)
    mean, inverse = moments(slow, slow_count)
    scaled = (h3[...] - mean) * inverse
    residual = silu(slow_pre[...]) * held + slow_par[0:1] * scaled + slow_par[1:2]
    out[:, 0:CS] = by_clip(silu(residual) * held, clips)
    mean, inverse = moments(fast, fast_count)
    pooled = None
    for frame in range(frames):
        scaled = (h6[frame] - mean) * inverse
        residual = silu(fast_pre[frame]) * held + fast_par[0:1] * scaled + fast_par[1:2]
        part = by_clip(silu(residual) * held, clips)
        pooled = part if pooled is None else pooled + part
    out[:, CS:] = pooled


def mixed(average, values):
    total = None
    for k in range(values.shape[0]):
        term = average[:, k : k + 1] * values[k : k + 1, :]
        total = term if total is None else total + term
    return total


def head_kernel(
    pools, head, bias, ids_down, ids_across, labels, valid, area, h3, h6, slow_pre, fast_pre,
    before, total_in, slow_par, fast_par, mask, features, logit_low, d3, d6, out,
):
    held = mask[...]
    frames = h6.shape[0]
    clips = features.shape[0]
    tm_count = pools.shape[0]
    parts = [pools[k] for k in range(tm_count)]
    while len(parts) > 1:
        parts = [parts[k] + parts[k + 1] for k in range(0, len(parts), 2)]
    (pool,) = parts
    slow_divide = area[...] * tm_count
    fast_divide = slow_divide * frames
    slow_feature = low(pool[:, 0:CS] / slow_divide)
    fast_feature = low(pool[:, CS:] / fast_divide)
    features[:, 0:CS] = slow_feature
    features[:, CS:] = fast_feature
    logits = nn(slow_feature, head[0:CS, :]) + nn(fast_feature, head[CS:, :]) + bias[...]
    same = (ids_down[...] == ids_across[...]).astype(F32)
    average = same / jnp.sum(same, axis=1, keepdims=True)
    mean_logits = mixed(average, logits)
    top = jnp.max(mean_logits, axis=1, keepdims=True)
    powers = jnp.exp(mean_logits - top)
    whole = jnp.sum(powers, axis=1, keepdims=True)
    classes = lax.broadcasted_iota(jnp.int32, mean_logits.shape, 1)
    onehot = (labels[...] == classes).astype(F32)
    picked = jnp.sum(onehot * mean_logits, axis=1, keepdims=True)
    loss = jnp.sum(valid[...] * (jnp.log(whole) + top - picked))
    mean_grad = valid[...] * (powers / whole - onehot)
    logit = low(mixed(average, mean_grad))
    logit_low[...] = logit
    slow_count, fast_count = counts(before[...], frames)
    slow, fast = get_wide(total_in[...])

    grad = nt(logit, head[0:CS, :]) / slow_divide
    mean, inverse = moments(slow, slow_count)
    scaled = (h3[...] - mean) * inverse
    residual = silu(slow_pre[...]) * held + slow_par[0:1] * scaled + slow_par[1:2]
    down = held * silu_grad(residual)
    down = (down.reshape(-1, clips, CS) * grad[None]).reshape(down.shape)
    d3[...] = down
    slow_pair = sums(down, scaled)

    grad = nt(logit, head[CS:, :]) / fast_divide
    mean, inverse = moments(fast, fast_count)
    fast_pair = None
    for frame in range(frames):
        scaled = (h6[frame] - mean) * inverse
        residual = silu(fast_pre[frame]) * held + fast_par[0:1] * scaled + fast_par[1:2]
        down = held * silu_grad(residual)
        down = (down.reshape(-1, clips, CF) * grad[None]).reshape(down.shape)
        d6[frame] = down
        pair = sums(down, scaled)
        fast_pair = pair if fast_pair is None else tuple(a + b for a, b in zip(fast_pair, pair))
    put_wide(out, slow_pair, fast_pair, loss)


def under(upstream, values, mean, inverse, gain, pair, count, held):
    scaled = (values - mean) * inverse
    return low(held * gain * inverse * (upstream - (pair[0] + scaled * pair[1]) / count))


def third_back_kernel(
    near, place, d3, d6, h3, h6, h2, h5, before, total3, total2, got, slow3, fast3, slow2, fast2, mask,
    weights, recover, u6, e2, e5, total_out, out, *rest
):
    u3 = rest[0:4] if near else rest[0:1]
    block, restore, flags = rest[-3:]
    copies = fetch_tall(weights, restore, flags, RESTORE_AT)
    held = mask[...]
    frames = h6.shape[0]
    total = jnp.sum(got[...].astype(F32), axis=0)
    total_out[...] = total
    slow_count, fast_count = counts(before[...], frames)
    slow_pair, fast_pair = get_wide(total)
    slow, fast = get_wide(total3[...])
    slow_two, fast_two = get_narrow(total2[...])
    mean, inverse = moments(slow, slow_count)
    upper = under(d3[...], h3[...], mean, inverse, slow3[0:1], slow_pair, slow_count, held)
    if near:
        wide = upper.astype(F32)
        tiles = [wide[:, k * 128 : (k + 1) * 128] for k in range(CS // 128)]
        turned = [pltpu.roll(tile, 64, 1) for tile in tiles]
        first_half = lax.broadcasted_iota(jnp.int32, tiles[0].shape, 1) < 64
        parts = []
        for p in range(4):
            held_tiles = []
            for k in range(4):
                one = 4 * k + p // 2
                two = one + 2
                if p % 2 == 0:
                    tile = jnp.where(first_half, tiles[one], turned[two])
                else:
                    tile = jnp.where(first_half, turned[one], tiles[two])
                held_tiles.append(low(tile))
            parts.append(jnp.concatenate(held_tiles, axis=1))
        in_relation(place[0], u3, parts)
    else:
        u3[0][...] = upper
    mean, inverse = moments(slow_two, slow_count)
    scaled = (h2[...] - mean) * inverse
    for copy in copies:
        copy.wait()
    down = nn(upper, restore[...]) * held * silu_grad(slow2[0:1] * scaled + slow2[1:2])
    e2[...] = down
    slow_out = sums(down, scaled)
    mean, inverse = moments(fast, fast_count)
    mean_two, inverse_two = moments(fast_two, fast_count)
    fast_out = None
    for frame in range(frames):
        upper = under(d6[frame], h6[frame], mean, inverse, fast3[0:1], fast_pair, fast_count, held)
        u6[frame] = upper
        scaled = (h5[frame] - mean_two) * inverse_two
        down = nn(upper, recover[...]) * held * silu_grad(fast2[0:1] * scaled + fast2[1:2])
        e5[frame] = down
        pair = sums(down, scaled)
        fast_out = pair if fast_out is None else tuple(a + b for a, b in zip(fast_out, pair))
    put_narrow(out, block, slow_out, fast_out)


def second_back_kernel(
    e2, e5, h2, h5, h1, h4, total2, total1, got, slow2, fast2, slow1, fast1, mask,
    weights, blending, u2, u5, e1, e4, blend_grad, total_out, out, pad, fast_pad, act_pad, block,
    mixing, flags,
):
    copies = fetch(weights, mixing, flags, [(tap * CSM, tap * CSM, CSM) for tap in range(9)])
    held = mask[...]
    frames = h5.shape[0]
    total = jnp.sum(got[...].astype(F32), axis=0)
    total_out[...] = total
    slow_count, fast_count = counts(total1[...], frames)
    slow_pair, fast_pair = get_narrow(total)
    slow_two, fast_two = get_narrow(total2[...])
    slow_one, fast_one = get_narrow(total1[...])
    mean, inverse = moments(slow_two, slow_count)
    upper = under(e2[...], h2[...], mean, inverse, slow2[0:1], slow_pair, slow_count, held)
    u2[...] = upper
    pad[...] = jnp.zeros_like(pad)
    fill(pad, upper.astype(F32))
    acc = None
    for tap in range(9):
        piece = low(tap_of(pad, 2 - tap // 3, 2 - tap % 3))
        copies[tap].wait()
        term = nn(piece, mixing[:, tap * CSM : (tap + 1) * CSM])
        acc = term if acc is None else acc + term
    mean, inverse = moments(slow_one, slow_count)
    scaled = (h1[...] - mean) * inverse
    down = acc * held * silu_grad(slow1[0:1] * scaled + slow1[1:2])
    e1[...] = down
    slow_out = sums(down, scaled)
    mean, inverse = moments(fast_two, fast_count)
    mean_one, inverse_one = moments(fast_one, fast_count)
    fast_pad[...] = jnp.zeros_like(fast_pad)
    act_pad[...] = jnp.zeros_like(act_pad)
    fast_out = None
    for frame in range(frames):
        upper = under(e5[frame], h5[frame], mean, inverse, fast2[0:1], fast_pair, fast_count, held)
        u5[frame] = upper
        scaled = (h4[frame] - mean_one) * inverse_one
        level = fast1[0:1] * scaled + fast1[1:2]
        fill(fast_pad, upper.astype(F32))
        fill(act_pad, low(silu(level) * held).astype(F32))
        turned = low(upper.astype(F32).T)
        acc = None
        for tap in range(9):
            down_by, right_by = (tap // 3, tap % 3)
            piece = low(tap_of(fast_pad, 2 - down_by, 2 - right_by))
            term = nt(piece, blending[tap])
            acc = term if acc is None else acc + term
            part = nn(turned, low(tap_of(act_pad, down_by, right_by)))
            blend_grad[tap] = part if frame == 0 else blend_grad[tap] + part
        down = acc * held * silu_grad(level)
        e4[frame] = down
        pair = sums(down, scaled)
        fast_out = pair if fast_out is None else tuple(a + b for a, b in zip(fast_out, pair))
    put_narrow(out, block, slow_out, fast_out)


def mixing_grad_kernel(acts, uppers, out, pad):
    count = acts.shape[0]
    pad[...] = jnp.zeros_like(pad)
    for place in range(count):
        fill(pad.at[place], acts[place].astype(F32))
    for tap in range(9):
        total = None
        for place in range(count):
            piece = low(tap_of(pad.at[place], tap // 3, tap % 3))
            term = dot(piece, uppers[place], ((0,), (0,)))
            total = term if total is None else total + term
        out[tap] = low(total)


def first_back_kernel(
    e1, e4, h1, h4, total1, got, slow1, fast1, mask, u1, u4, total_out
):
    held = mask[...]
    frames = h4.shape[0]
    total = jnp.sum(got[...].astype(F32), axis=0)
    total_out[...] = total
    slow_count, fast_count = counts(total1[...], frames)
    slow_pair, fast_pair = get_narrow(total)
    slow, fast = get_narrow(total1[...])
    mean, inverse = moments(slow, slow_count)
    u1[...] = under(e1[...], h1[...], mean, inverse, slow1[0:1], slow_pair, slow_count, held)
    mean, inverse = moments(fast, fast_count)
    for frame in range(frames):
        u4[frame] = under(
            e4[frame], h4[frame], mean, inverse, fast1[0:1], fast_pair, fast_count, held
        )


def by_frame(place, target, parts):
    target[0] = jnp.zeros_like(target[0])
    target[len(parts) + 1] = jnp.zeros_like(target[0])
    for k, part in enumerate(parts):
        target[jnp.bitwise_xor(place, k) + 1] = part


def turn(parts):
    own, across, others = parts
    return [own[...], others[0], across[...], others[1]]


def stem_grad_kernel(
    place, slow_up, fast_up, video, small, out_0, out_1, out_2, out_3, total
):
    total[0:CS, :] = dot(slow_up[...], video[0], ((0,), (0,)))
    fast = None
    for frame in range(fast_up.shape[0]):
        term = dot(fast_up[frame], video[frame], ((0,), (0,)))
        fast = term if fast is None else fast + term
    total[CS:, :] = fast
    size = total.shape[0] // 8
    for k, out in enumerate((out_0, out_1, out_2, out_3)):
        target = jnp.bitwise_xor(place[0], k)
        for b in range(8):
            start = pl.multiple_of(b * size + target * (size // 4), 8)
            rows = total[pl.ds(start, size // 4), :]
            out[b] = low(jnp.concatenate([rows, small[target, b]]))


def early_kernel(*refs):
    uppers, acts, out = refs[0:4], refs[4:7], refs[7]
    total = None
    for upper, act in zip(uppers, turn(acts)):
        term = dot(upper[...], act, ((0,), (0,)))
        total = term if total is None else total + term
    size = total.shape[0] // out.shape[0]
    for b in range(out.shape[0]):
        out[b] = low(total[b * size : (b + 1) * size])


def mixing_kernel(*refs):
    acts, uppers, restore, out, pad = refs[0:4], refs[4:7], refs[7], refs[8], refs[9]
    pad[...] = jnp.zeros_like(pad)
    for k, act in enumerate(acts):
        fill(pad.at[k], act[...].astype(F32))
    parts = turn(uppers)
    for tap in range(9):
        total = None
        for k, upper in enumerate(parts):
            term = dot(low(tap_of(pad.at[k], tap // 3, tap % 3)), upper, ((0,), (0,)))
            total = term if total is None else total + term
        if tap < 8:
            out[tap, 0:128, :] = low(total)
        else:
            for b in range(8):
                out[b, 128:144, :] = low(total[b * 16 : (b + 1) * 16])
    for b in range(8):
        out[b, 144:208, :] = restore[b]


def late_kernel(*refs):
    place, cells, sides, uppers = refs[0], refs[1:5], refs[5:8], refs[8:11]
    out, frames, side_total, side_rows = refs[11:15]
    here = place[0]
    by_frame(here, frames, [cell[...] for cell in cells])
    parts = turn(uppers)
    for tap in range(3):
        total = None
        for k, upper in enumerate(parts):
            cell = frames[jnp.bitwise_xor(here, k) + tap]
            term = dot(cell, upper, ((0,), (0,)))
            total = term if total is None else total + term
        for b in range(4):
            if tap < 2:
                out[tap * 4 + b, 0:128, :] = low(total[b * 128 : (b + 1) * 128])
            else:
                out[2 * b, 128:192, :] = low(total[b * 128 : b * 128 + 64])
                out[2 * b + 1, 128:192, :] = low(total[b * 128 + 64 : (b + 1) * 128])
    core = here % 2
    own, across, others = sides
    for tap in range(5):
        total = None
        turned = (own[tap], others[0, tap], across[tap], others[1, tap])
        for side, upper in zip(turned, parts):
            term = dot(side, upper, ((0,), (0,)))
            total = term if total is None else total + term
        side_total[...] = total
        side_rows[tap * 64 : (tap + 1) * 64, :] = side_total[
            pl.ds(pl.multiple_of(core * 64, 64), 64), :
        ]
    blank = jnp.zeros((8, CSM), F32)
    for b in range(8):
        rows = jnp.concatenate([side_rows[b * 40 : (b + 1) * 40, :], blank])
        out[b, 192:240, :] = low(rows)


def stem_back_kernel(near, place, *refs):
    u1_held = refs[0:3] if near else refs[0]
    (
        u4, u4_before, u4_after, weights, squeeze, d3, d6, slow_pre, fast_pre,
        mask, slow_up, fast_up, first, frames_held, flags,
    ) = refs[-15:]
    spans = [(CONDENSE_AT + k * CS, 5 * CF + k * CS, CS) for k in range(3)]
    copies = fetch(weights, first, flags, spans + [(SIDE_AT, 0, 5 * CF)])
    held = mask[...]
    frames = fast_up.shape[0]
    total = d3[...]
    if near:
        by_frame(place[0], frames_held, turn(u1_held))
        source = frames_held
    else:
        source = u1_held
    u1_before, u1, u1_after = [source[place[0] + k] for k in range(3)]
    for tap, piece in enumerate((u1_after, u1, u1_before)):
        start = 5 * CF + tap * CS
        copies[tap].wait()
        total = total + nn(piece, first[:, start : start + CS])
    copies[3].wait()
    slow_up[...] = low(total * held * silu_grad(slow_pre[...]))
    for frame in range(frames):
        total = d6[frame]
        pairs = [(frame + 2, u1)] if frame < 3 else []
        pairs = pairs + ([(frame - 2, u1_after)] if frame >= 2 else [])
        for tap, piece in pairs:
            total = total + nn(piece, first[:, tap * CF : (tap + 1) * CF])
        for tap in range(3):
            place = frame + 1 - tap
            if place < 0:
                piece = u4_before[...]
            elif place >= frames:
                piece = u4_after[...]
            else:
                piece = u4[place]
            total = total + nn(piece, squeeze[:, tap * CF : (tap + 1) * CF])
        fast_up[frame] = low(total * held * silu_grad(fast_pre[frame]))


def product(left, right):
    left_high = low(left)
    right_high = low(right)
    if left.shape[0] >= CSM:
        return nn(left_high, right_high)
    left_rest = low(left - left_high.astype(F32))
    right_rest = low(right - right_high.astype(F32))
    return nn(left_high, right_high) + (nn(left_high, right_rest) + nn(left_rest, right_high))


def shape_kernel(*refs):
    half = len(refs) // 2
    grams = []
    eyes = []
    scales = []
    totals = []
    for source in refs[:half]:
        size = source.shape[0]
        gram = source[...]
        rows = lax.broadcasted_iota(jnp.int32, (size, size), 0)
        columns = lax.broadcasted_iota(jnp.int32, (size, size), 1)
        eye = (rows == columns).astype(F32)
        diagonal = jnp.sum(gram * eye, axis=1, keepdims=True)
        diagonal = jnp.sum(diagonal, axis=0, keepdims=True)
        scale = 1.0 / (jnp.sqrt(diagonal) + 1e-07)
        grams.append(gram * (scale * scale))
        eyes.append(eye)
        scales.append(scale)
    for step in range(NS_STEPS):
        extras = [NS_SECOND * gram + NS_THIRD * product(gram, gram) for gram in grams]
        if step == 0:
            totals = [NS_FIRST * eye + extra for eye, extra in zip(eyes, extras)]
        else:
            totals = [
                NS_FIRST * total + product(extra, total) for total, extra in zip(totals, extras)
            ]
        if step + 1 < NS_STEPS:
            middles = [NS_FIRST * g + product(extra, g) for g, extra in zip(grams, extras)]
            grams = [NS_FIRST * m + product(extra, m) for m, extra in zip(middles, extras)]
    for target, total, scale in zip(refs[half:], totals, scales):
        target[...] = (total * scale).astype(target.dtype)


def block_shape_kernel(whole, *refs):
    small, outs = refs[0:3], refs[3:8]
    gram, stem = refs[8:10]
    for b in range(8):
        gram[b * 64 : (b + 1) * 64, :] = whole[b, 0:64, :].astype(F32)
        rows = whole[b, 64:80, :].astype(F32)
        stem[b * 24 : b * 24 + 16, :] = rows[:, 0:192]
        stem[b * 24 + 16 : b * 24 + 24, :] = rows[0:8, 256:448]
    shape_kernel(gram, stem, *small, *outs)


def gram_kernel(
    place, factor, speed, restore_speed, own, got, stem_speed, stem_grad, one, two, stem_out,
    keep, give, stem_gram, wide, tall, held,
):
    x = place[0] // 2
    core = place[0] % 2
    scale = factor[...]
    for spot, part in ((x, own), (1 - x, got)):
        held[pl.ds(pl.multiple_of(spot * 128, 128), 128), :] = part[0:128, :].astype(F32)
        held[pl.ds(pl.multiple_of(spot * 64 + 256, 64), 64), :] = part[128:192, :].astype(F32)
        held[pl.ds(pl.multiple_of(spot * 64 + 384, 64), 64), :] = part[192:256, :].astype(F32)
    speeds = jnp.concatenate([speed[b, 0:64, :].astype(F32) for b in range(8)]).T
    grads = held[...]
    speed_two = jnp.where(x == 0, restore_speed[...].astype(F32), speeds[384:512])
    moved_one = low(MUON_KEEP * speeds[0:384] + grads[0:384] * scale)
    moved_two = low(MUON_KEEP * speed_two + grads[384:512] * scale)
    one[...] = moved_one
    two[...] = moved_two
    gram_one = low(dot(moved_one, moved_one, ((0,), (0,))))
    gram_two = low(dot(moved_two, moved_two, ((0,), (0,))))
    keep[...] = jnp.where(core == 0, gram_one, gram_two)
    give[...] = jnp.where(core == 0, gram_two, gram_one)
    moved = low(MUON_KEEP * stem_speed[...] + stem_grad[...].astype(F32) * scale)
    stem_out[...] = moved
    gram = dot(moved, moved, ((0,), (0,)))
    stem_gram[...] = jnp.zeros_like(stem_gram)
    blank = jnp.zeros((8, 192), F32)
    for b in range(8):
        stem_gram[b, :, 0:192] = low(gram[b * 24 : b * 24 + 16])
        rest = jnp.concatenate([gram[b * 24 + 16 : b * 24 + 24], blank])
        stem_gram[b, :, 256:448] = low(rest)
    turned = low(grads.T)
    for b in range(8):
        wide[b] = turned[b * 64 : (b + 1) * 64]
    put_tall(tall, low(grads[384:512]))


def put_tall(out, values):
    for k in range(4):
        for h in range(2):
            out[2 * k + h] = values[h * 64 : (h + 1) * 64, k * 128 : (k + 1) * 128]


def ortho_kernel(place, shaped, other, one, two, wide, tall):
    core = place[0] % 2
    shape_one = jnp.where(core == 0, shaped[...], other[...])
    shape_two = jnp.where(core == 0, other[...], shaped[...])
    first = low(nt(shape_one, one[...]))
    second = low(nt(shape_two, two[...]))
    for b in range(8):
        wide[b, :, 0:384] = first[b * 64 : (b + 1) * 64]
        wide[b, :, 384:512] = second[b * 64 : (b + 1) * 64]
    put_tall(tall, low(nn(two[...], shape_two)))


def shape_of(grams):
    return call(shape_kernel, [(item.shape, F32) for item in grams], grams, micros=13)


def carry(base, value, ratio, factor):
    return MUON_KEEP * base + value * factor


def renew(base, value, ratio, factor):
    return base - MUON_RATE * (value * ratio + WEIGHT_DECAY * base)


def selection(count, far, depth, size, x, width, target):
    column = lax.broadcasted_iota(jnp.int32, (count * far * depth, 1), 0)
    place = lax.rem(column, depth)
    block = lax.div(column, depth)
    goal = target(lax.div(block, far), place)
    goal = jnp.where((place < size) & (lax.rem(block, far) == x), goal, -1)
    columns = lax.broadcasted_iota(jnp.int32, (count * far * depth, width), 1)
    return low((goal == columns).astype(F32))


def place_kernel(
    rule, far, main_rows, depth, place, factor, own, across, others, lateral, condense, mixing,
    restore, lateral_out, condense_out, mixing_out, restore_out, frames,
):
    for k, part in enumerate((own[...], others[0], across[...], others[1])):
        frames[jnp.bitwise_xor(place[0], k)] = part
    half_one, half_two = [
        [frames.at[2 * target + c] for target in range(far)] for c in range(2)
    ]
    halves = (half_one, half_two)
    batch_count, out_rows, lanes_all = own.shape
    edge = far * main_rows
    stop = far * depth
    scale = factor[...]

    def put(out, base, spot, values):
        lanes = slice(spot, spot + values.shape[1])
        out[:, lanes] = rule(base[:, lanes], values.astype(F32), 1.0, scale)
        return spot + values.shape[1]

    devices = 2 * far
    rest_depth = depth - main_rows
    for target, out, base, main_taps in ((0, condense_out, condense, 2), (1, mixing_out, mixing, 8)):
        share = batch_count // main_taps
        spot = 0
        for tap in range(main_taps):
            for device in range(devices):
                lanes = slice(device // 2 * main_rows, (device // 2 + 1) * main_rows)
                for k in range(tap * share, (tap + 1) * share):
                    spot = put(out, base, spot, halves[device % 2][target][k, :, lanes])
        size = (out.shape[1] - spot) // (batch_count * devices)
        rests = [
            jnp.concatenate([half[target][k, :, edge:stop] for k in range(batch_count)], axis=1)
            for half in halves
        ]
        for x in range(far):
            chosen = selection(
                batch_count, far, rest_depth, size, x, batch_count * size,
                lambda k, r: k * size + r,
            )
            for rest in rests:
                spot = put(out, base, spot, nn(rest, chosen))
    side_depth = (lanes_all - stop) // far
    side_size = lateral.shape[1] // (batch_count * devices)
    channels = CF // devices
    sides = [
        jnp.concatenate([half[1][k, :, stop:] for k in range(batch_count)], axis=1)
        for half in halves
    ]
    for x in range(far):
        total = None
        for c, side in enumerate(sides):

            def goal(k, r):
                row = k * side_size + r
                return lax.div(row, channels) * 2 * channels + c * channels + lax.rem(row, channels)

            chosen = selection(
                batch_count, far, side_depth, side_size, x, 10 * channels, goal
            )
            term = nn(side, chosen)
            total = term if total is None else total + term
        for tap in range(5):
            put(
                lateral_out, lateral, tap * CF + 2 * x * channels,
                total[:, tap * 2 * channels : (tap + 1) * 2 * channels],
            )
    width = lanes_all - stop
    ratio = math.sqrt(max(1.0, restore.shape[0] * batch_count / restore.shape[1]))
    for c, half in enumerate(halves):
        for k in range(batch_count * out_rows // width):
            for h in range(far):
                start = (2 * h + c) * out_rows
                rows = slice(start, start + out_rows)
                lanes = slice(k * width, (k + 1) * width)
                values = half[0][k * width // out_rows + h, :, stop:].astype(F32)
                restore_out[rows, lanes] = rule(restore[rows, lanes], values, ratio, scale)


def adam(weight, moment, square, grad, rate, decay):
    moment = ADAM_ONE * moment + (1.0 - ADAM_ONE) * grad
    square = ADAM_TWO * square + (1.0 - ADAM_TWO) * grad * grad
    fixed_one = 1.0 - ADAM_ONE**STEP
    fixed_two = 1.0 - ADAM_TWO**STEP
    weight = weight - rate * (
        moment / fixed_one / (jnp.sqrt(square / fixed_two) + ADAM_EPS) + decay * weight
    )
    return (weight, moment, square)


def per_device(
    video,
    video_ids,
    crop_scales,
    labels,
    valid_clips,
    stem_weight,
    lateral_weight,
    condense,
    mixing,
    restore,
    squeeze,
    blending,
    recover,
    head_weight,
    stem_velocity,
    lateral_velocity,
    condense_velocity,
    mixing_velocity,
    restore_velocity,
    squeeze_velocity,
    blending_velocity,
    recover_velocity,
    head_moment,
    head_square,
    affine,
    affine_moment,
    affine_square,
):
    tm_count = lax.axis_size("tm")
    batch_count = lax.axis_size("batch")
    devices = tm_count * batch_count
    far = tm_count // 2
    tm_place = lax.axis_index("tm")
    batch_place = lax.axis_index("batch")
    core = tm_place % 2
    both = ("tm", "batch")

    clips, frames, height = video.shape[0:3]
    spots = height * height
    rows = spots * clips

    def quarter(block):
        part = block.shape[0] // tm_count
        return lax.dynamic_slice_in_dim(block, tm_place * part, part, axis=0)

    def gather(block):
        return lax.all_gather(quarter(block), ("batch", "tm"), axis=0, tiled=True)

    def by_place(items, place):
        whole = jnp.zeros((len(items),) + items[0].shape, items[0].dtype)
        for k, item in enumerate(items):
            whole = lax.dynamic_update_index_in_dim(whole, item, place ^ k, 0)
        return whole

    def over_tm(block):
        held = by_place(
            [block] + [swap(block, "tm", 2 * k) for k in range(1, far)], tm_place // 2
        )
        held = by_place([held, swap(held, "tm", 1)], core)
        return jnp.swapaxes(held, 0, 1).reshape((tm_count,) + block.shape)

    def gather_steps(block):
        held = spread_all(block, ("batch",))
        held = held.reshape(batch_count, -1, block.shape[1])
        held = jnp.swapaxes(over_tm(held), 0, 1)
        return held.reshape(-1, block.shape[1])

    out_rows = condense.shape[0]
    small_rows = squeeze.shape[0]
    weights_low = jnp.concatenate(
        [mixing, lateral_weight, condense]
        + [restore[k * out_rows : (k + 1) * out_rows] for k in range(4)],
        axis=1,
    )
    weights_low = quarter(weights_low).astype(BF16)
    stem_low = quarter(stem_weight).astype(BF16)
    weights_low, stem_low, video = lax.optimization_barrier((weights_low, stem_low, video))
    weights_full = lax.all_gather(weights_low, ("batch", "tm"), axis=0, tiled=True)
    stem_full = gather_steps(stem_low)
    small = jnp.concatenate(
        [squeeze, blending, recover.reshape(small_rows, -1)], axis=1
    ).astype(BF16)
    small_full = spread_all(small, ("batch",)).reshape(CFM, -1)
    squeeze_full = small_full[:, 0 : 3 * CF]
    blending_full = small_full[:, 3 * CF : 3 * CF + 9 * CFM]
    recover_full = small_full[:, 3 * CF + 9 * CFM :].reshape(CF, CFM)
    head_full = gather(head_weight.astype(BF16))

    own_video = jnp.transpose(video, (1, 2, 3, 0, 4)).reshape(frames, rows, -1)
    before = shift(
        jnp.concatenate([own_video[0:1], own_video[frames - 2 :]], axis=0), "tm", 1
    )
    after = shift(own_video[0:1], "tm", -1)
    slow_video = jnp.concatenate([before[0:1], own_video[0:1], after], axis=0)
    fast_video = jnp.concatenate([before[1:], own_video, after], axis=0)

    side = (height - crop_scales).astype(F32)
    places = jnp.arange(height).astype(F32)
    inside = (places[:, None] < side[None, :]).astype(F32)
    mask = (inside[:, None, :] * inside[None, :, :]).reshape(rows, 1)
    area = (side * side)[:, None]
    gains, shifts, class_bias = split_affine(affine)
    par = [jnp.stack([gain, shift]) for gain, shift in zip(gains, shifts)]
    valid = valid_clips.astype(F32)[:, None]
    blend_taps = jnp.transpose(blending_full.reshape(CFM, 9, CFM), (1, 2, 0))
    narrow = ((devices, 8, 256), F32)
    narrow_low = ((devices, 8, 256), BF16)
    total_narrow = ((8, 256), F32)
    wide = ((8, 640), F32)

    def exchange(copies):
        return lax.all_to_all(copies, both, 0, 0, tiled=True)

    def exchange_wide(block):
        return spread_all(block, both).reshape((devices,) + block.shape)

    slow_shape = (rows, CSM)
    fast_shape = (frames, rows, CFM)
    slow_wide = (rows, CS)
    fast_wide = (frames, rows, CF)
    first_shape = ((CSM, 5 * CF + 3 * CS), BF16)
    mixing_shape = ((CSM, 9 * CSM), BF16)
    restore_shape = ((CS, CSM), BF16)
    pad_shape = ((height + 2, height + 2, clips, CSM), F32)
    fast_pad = ((height + 2, height + 2, clips, CFM), F32)

    pieces = batch_count * far
    main_rows = 2048 // pieces
    mixing_rows = 9 * CSM // 2 // pieces
    condense_rows = 3 * CS // 2 // pieces
    far_place = tm_place // 2
    depth_one = condense_rows
    depth_two = CS // 2 // pieces

    def share_of(item, taps, place):
        width = item.shape[1] // taps
        size = width // tm_count
        return jnp.concatenate(
            [
                lax.dynamic_slice_in_dim(item, tap * width + place * size, size, axis=1)
                for tap in range(taps)
            ],
            axis=1,
        ).astype(BF16)

    def sent_columns(item, taps, parts):
        held = []
        start = 0
        shares = [share_of(item, taps, 2 * k + core) for k in range(far)]
        for size, depth in parts:
            for share in shares:
                block = share[:, start : start + size * batch_count]
                block = block.reshape(out_rows, batch_count, size)
                held.append(jnp.pad(block, ((0, 0), (0, 0), (0, depth - size))))
            start = start + size * batch_count
        return jnp.transpose(jnp.concatenate(held, axis=-1), (1, 0, 2))

    lateral_rows = 5 * CF // tm_count // batch_count
    rest_depth = depth_one - main_rows
    speed_send = jnp.concatenate(
        [
            jnp.where(
                far_place == 0,
                sent_columns(
                    condense_velocity, 3, ((main_rows, main_rows), (rest_depth, rest_depth))
                ),
                sent_columns(
                    mixing_velocity,
                    9,
                    ((main_rows, main_rows), (mixing_rows - main_rows, rest_depth)),
                ),
            ),
            sent_columns(lateral_velocity, 5, ((lateral_rows, depth_two),)),
        ],
        axis=-1,
    )
    small_speed = jnp.concatenate(
        [squeeze_velocity, blending_velocity, recover_velocity.reshape(small_rows, -1)], axis=1
    )
    small_speed = small_speed.astype(BF16).reshape(-1, speed_send.shape[-1])
    small_speed = jnp.broadcast_to(small_speed[None], (batch_count,) + small_speed.shape)
    speed_send = jnp.concatenate([speed_send, small_speed], axis=1)
    speed_send, small_full = lax.optimization_barrier((speed_send, small_full))
    speed = lax.all_to_all(speed_send, "batch", 0, 0, tiled=True)

    near = tm_count == 4 and batch_count == 8
    place_cell = tm_place.astype(jnp.int32).reshape(1)
    quarter_shape = (rows, CS // tm_count)
    slow_pre, fast_pre, slow_low, fast_low, *shares = call(
        functools.partial(stem_kernel, near),
        [
            (slow_wide, F32),
            (fast_wide, F32),
            ((3, rows, CS), BF16),
            ((frames + 3, rows, CF), BF16),
        ]
        + (
            [(quarter_shape, BF16)] * 4 + [((5, rows, 128), BF16)] * 2
            if near
            else [((tm_count,) + quarter_shape, BF16)]
        ),
        [place_cell, slow_video, fast_video, stem_full, mask],
        scalars=(0,),
    )
    def in_turn(items, margin=0):
        whole = jnp.zeros((len(items) + 2 * margin,) + items[0].shape, items[0].dtype)
        for k, item in enumerate(items):
            whole = lax.dynamic_update_index_in_dim(whole, item, (tm_place ^ k) + margin, 0)
        return whole

    def share_out(parts, margin=0):
        items = [pick(parts, 0, tm_place)]
        items += [swap(pick(parts, 0, tm_place ^ k), "tm", k) for k in range(1, tm_count)]
        return in_turn(items, margin)

    def every(block, margin=0):
        even = [block] + [swap(block, "tm", 2 * k) for k in range(1, far)]
        odd = swap(jnp.stack(even), "tm", 1)
        items = [item for k in range(far) for item in (even[k], odd[k])]
        return in_turn(items, margin)

    def by_share(block, outer):
        parts = block.reshape(block.shape[0], outer, tm_count, -1)
        return jnp.moveaxis(parts, 2, 0).reshape(tm_count, block.shape[0], -1)

    def swaps(parts):
        return [parts[0]] + [swap(parts[k], "tm", k) for k in range(1, tm_count)]

    def pairs_of(own, given):
        across = swap(given, "tm", 2)
        return [own, across, swap(jnp.stack([own, across]), "tm", 1)]

    if near:
        slow_shares = swaps(shares[0:4])
        side_shares = pairs_of(shares[4], shares[5])
    else:
        sides = jnp.transpose(fast_low[0:5], (1, 0, 2)).reshape(rows, 5 * CF)
        slow_shares = share_out(shares[0], 1)
        side_shares = share_out(by_share(sides, 5))
    slow_low, speed = lax.optimization_barrier((slow_low, speed))
    h1, h4, sent = call(
        first_kernel,
        [(slow_shape, F32), (fast_shape, F32), narrow],
        [slow_low, fast_low, weights_full, squeeze_full, mask, valid],
        [total_narrow, first_shape],
        far=(2,),
        copies=4,
    )
    act_width = CSM // tm_count
    act_shapes = [((rows, 128), BF16)] * 4 if near else [(slow_shape, BF16)]
    h2, h5, total1, sent, *acts = call(
        functools.partial(second_kernel, near),
        [(slow_shape, F32), (fast_shape, F32), total_narrow, narrow] + act_shapes,
        [place_cell, h1, h4, exchange(sent), par[0], par[3], mask, weights_full, blend_taps],
        [pad_shape, fast_pad, total_narrow, mixing_shape],
        far=(7,),
        copies=9,
        scalars=(0,),
    )
    acts = swaps(acts) if near else share_out(by_share(acts[0], 1))
    a2, a5, h3, h6, total2, sent = call(
        third_kernel,
        [
            (slow_shape, BF16),
            (fast_shape, BF16),
            (slow_wide, F32),
            (fast_wide, F32),
            total_narrow,
            wide,
        ],
        [h2, h5, total1, exchange(sent), par[1], par[4], mask, weights_full, recover_full],
        [restore_shape],
        far=(7,),
        copies=4 * batch_count,
    )
    a2_every = pairs_of(a2, a2) if near else every(a2)
    if near:
        h3, slow_shares[1], slow_shares[3] = lax.optimization_barrier(
            (h3, slow_shares[1], slow_shares[3])
        )
    else:
        h3, slow_shares, side_shares = lax.optimization_barrier((h3, slow_shares, side_shares))
    pool, total3 = call(
        pool_kernel,
        [((clips, CS + CF), F32), wide],
        [h3, h6, slow_pre, fast_pre, total1, exchange_wide(sent), par[2], par[5], mask],
    )
    if near:
        pools = jnp.stack([pool] + [swap(pool, "tm", k) for k in range(1, tm_count)])
    else:
        pools = spread_all(pool, ("tm",)).reshape(tm_count, clips, CS + CF)
    if near:
        pools, slow_shares[2] = lax.optimization_barrier((pools, slow_shares[2]))
    feature_low, logit_low, d3, d6, sent = call(
        head_kernel,
        [((clips, CS + CF), BF16), ((clips, CLS), BF16), (slow_wide, F32), (fast_wide, F32), wide],
        [
            pools,
            head_full,
            class_bias[None],
            video_ids[:, None],
            video_ids[None],
            labels[:, None],
            valid,
            area,
            h3,
            h6,
            slow_pre,
            fast_pre,
            total1,
            total3,
            par[2],
            par[5],
            mask,
        ],
    )
    d3, acts, a2_every, side_shares = lax.optimization_barrier((d3, acts, a2_every, side_shares))
    u6, e2, e5, back3, sent, *u3 = call(
        functools.partial(third_back_kernel, near),
        [
            (fast_wide, BF16),
            (slow_shape, F32),
            (fast_shape, F32),
            wide,
            narrow_low,
        ]
        + ([(quarter_shape, BF16)] * 4 if near else [(slow_wide, BF16)]),
        [
            place_cell,
            d3,
            d6,
            h3,
            h6,
            h2,
            h5,
            total1,
            total3,
            total2,
            exchange_wide(low(sent)),
            par[2],
            par[5],
            par[1],
            par[4],
            mask,
            weights_full,
            recover_full,
        ],
        [total_narrow, restore_shape],
        far=(16,),
        copies=4 * batch_count,
        scalars=(0,),
    )
    if near:
        (restore_grad,) = call(
            early_kernel,
            [((batch_count, CS // tm_count // batch_count, CSM), BF16)],
            [*swaps(u3), *a2_every],
        )
    else:
        u3_shares = share_out(by_share(u3[0], batch_count))
        restore_grad = low(dot(u3_shares, a2_every, ((0, 1), (0, 1))))
    recover_grad = over_rows(a5.reshape(frames * rows, CFM), u6.reshape(frames * rows, CF))

    u2, u5, e1, e4, blend_grad, back2, sent = call(
        second_back_kernel,
        [
            (slow_shape, BF16),
            (fast_shape, BF16),
            (slow_shape, F32),
            (fast_shape, F32),
            ((9, CFM, CFM), F32),
            total_narrow,
            narrow_low,
        ],
        [
            e2,
            e5,
            h2,
            h5,
            h1,
            h4,
            total2,
            total1,
            exchange(sent),
            par[1],
            par[4],
            par[0],
            par[3],
            mask,
            weights_full,
            blend_taps,
        ],
        [pad_shape, fast_pad, fast_pad, total_narrow, mixing_shape],
        far=(14,),
        copies=9,
    )
    blending_grad = jnp.transpose(blend_grad, (1, 0, 2)).reshape(CFM, 9 * CFM)

    def by_batch(parts):
        return jnp.concatenate(
            [part.reshape(batch_count, -1, part.shape[-1]) for part in parts], axis=1
        )

    def over_batch(view):
        got = lax.all_to_all(view, "batch", 0, 0, tiled=True)
        return jnp.sum(got.reshape(view.shape).astype(F32), axis=0)

    if near:
        (early,) = call(
            mixing_kernel,
            [((batch_count, 208, CSM), BF16)],
            [*acts, *pairs_of(u2, u2), restore_grad],
            [((tm_count, height + 2, height + 2, clips, act_width), F32)],
        )
    else:
        (mixing_grad,) = call(
            mixing_grad_kernel,
            [((9, act_width, CSM), BF16)],
            [acts, every(u2)],
            [((tm_count, height + 2, height + 2, clips, act_width), F32)],
        )
        mixing_grad = mixing_grad.reshape(9 * act_width, CSM)
        main_edge = 8 * act_width
        early = by_batch([mixing_grad[0:main_edge], mixing_grad[main_edge:], restore_grad])
    early, e1 = lax.optimization_barrier((early, e1))
    early = over_batch(early)

    u1, u4, back1 = call(
        first_back_kernel,
        [(slow_shape, BF16), (fast_shape, BF16), total_narrow],
        [e1, e4, h1, h4, total1, exchange(sent), par[0], par[3], mask],
    )
    if near:
        u1_parts = pairs_of(u1, u1)
        u1_held = u1_parts
    else:
        u1_held = every(u1, 1)
    squeeze_grad = jnp.concatenate(
        [dot(u4, fast_low[1 + k : 1 + k + frames], ((0, 1), (0, 1))) for k in range(3)], axis=1
    )
    slow_up, fast_up = call(
        functools.partial(stem_back_kernel, near),
        [(slow_wide, BF16), (fast_wide, BF16)],
        [
            place_cell,
            *(u1_held if near else [u1_held]),
            u4,
            shift(u4[frames - 1], "tm", 1),
            shift(u4[0], "tm", -1),
            weights_full,
            squeeze_full,
            d3,
            d6,
            slow_pre,
            fast_pre,
            mask,
        ],
        [first_shape, ((6,) + slow_shape, BF16)],
        far=(7 if near else 5,),
        copies=4,
        scalars=(0,),
    )
    slow_up, fast_up, u1_held = lax.optimization_barrier((slow_up, fast_up, u1_held))
    if near:
        (late,) = call(
            late_kernel,
            [((batch_count, 240, CSM), BF16)],
            [place_cell, *slow_shares, *side_shares, *u1_held],
            [((6,) + quarter_shape, BF16), ((128, CSM), F32), ((320, CSM), F32)],
            scalars=(0,),
        )
    else:
        u1_inner = u1_held[1 : tm_count + 1]
        cells = ((0, 1), (0, 1))
        condense_grad = [
            low(dot(slow_shares[k : k + tm_count], u1_inner, cells)) for k in range(3)
        ]
        lateral_grad = low(dot(side_shares, u1_inner, cells))
        late = by_batch(
            [jnp.concatenate(condense_grad[0:2]), condense_grad[2], lateral_grad]
        )
    late, early = lax.optimization_barrier((late, early))
    late = over_batch(late)
    clip_count = total1[7, 0] / tm_count
    loss_total = (back3[4, 512] + back3[5, 512] + back3[6, 512]) / tm_count
    slow_back3, fast_back3 = get_wide(back3)
    slow_back2, fast_back2 = get_narrow(back2)
    slow_back1, fast_back1 = get_narrow(back1)
    (b1, g1), (b2, g2), (b3, g3) = [
        [item[0] for item in pair] for pair in (slow_back1, slow_back2, slow_back3)
    ]
    (b4, g4), (b5, g5), (b6, g6) = [
        [item[0] for item in pair] for pair in (fast_back1, fast_back2, fast_back3)
    ]

    main_rows = 2048 // pieces
    mixing_rows = 9 * CSM // 2 // pieces
    condense_rows = 3 * CS // 2 // pieces
    tm_all = bits("tm", 0)
    columns_wide = stem_weight.shape[-1]

    def blocks(item):
        item = jnp.pad(item, ((0, 0), (0, -item.shape[1] % columns_wide)))
        item = item.reshape(batch_count, small_rows, -1, columns_wide)
        return jnp.swapaxes(item, 1, 2)

    small_view = [blocks(item) for item in (squeeze_grad, blending_grad, recover_grad)]
    small_view = jnp.concatenate(small_view, axis=1)
    small_blocks = small_view.shape[1]
    head_rows = head_weight.shape[0]
    feature_parts = jnp.transpose(feature_low.reshape(clips, batch_count, head_rows), (1, 0, 2))
    logit_parts = jnp.broadcast_to(logit_low.reshape(1, -1), (batch_count, clips * CLS))
    riders = jnp.concatenate([feature_parts.reshape(batch_count, -1), logit_parts], axis=1)
    riders = jnp.pad(riders, ((0, 0), (0, -riders.shape[1] % columns_wide)))
    riders = riders.reshape(batch_count, -1, columns_wide)
    if near:
        small_tm = small_view.reshape(batch_count, tm_count, -1, columns_wide)
        small_part = small_tm.shape[2]
        small_tm = jnp.pad(jnp.swapaxes(small_tm, 0, 1), ((0, 0), (0, 0), (0, 6), (0, 0)))
        share_shape = (batch_count, stem_weight.shape[0] // tm_count + 24, columns_wide)
        stem_shares = call(
            stem_grad_kernel,
            [(share_shape, BF16)] * 4,
            [place_cell, slow_up, fast_up, own_video, small_tm],
            [((CS + CF, columns_wide), F32)],
            scalars=(0,),
        )
        stem_shares = swaps(stem_shares)
        stem_shares = low(sum(share.astype(F32) for share in stem_shares))
        riders = jnp.concatenate([stem_shares, riders], axis=1)
        got = [pick(riders, 0, batch_place)] + [
            swap(pick(riders, 0, batch_place ^ k), "batch", k) for k in range(1, batch_count)
        ]
        shards_sum = sum(item[0 : share_shape[1]].astype(F32) for item in got)
        stem_part = share_shape[1] - 24
        stem_shard, small_shard = shards_sum[0:stem_part], shards_sum[stem_part:]
        riders = jnp.stack([item[share_shape[1] :] for item in got])
        riders = riders.reshape(batch_count, -1)
    else:
        stem_grad = jnp.concatenate(
            [over_rows(slow_up, own_video[0]), dot(fast_up, own_video, ((0, 1), (0, 1)))], axis=0
        )
        stem_view = stem_grad.reshape((batch_count,) + (2,) * len(tm_all) + (-1, stem_grad.shape[-1]))
        small_view = small_view.reshape(-1, columns_wide)
        live = list(tm_all)
        for axis, bit in tm_all[::-1]:
            dim = 1 + live.index((axis, bit))
            flag = (tm_place >> bit) & 1
            keep, give = pick(stem_view, dim, flag), pick(stem_view, dim, 1 - flag)
            flat_give = give.reshape(-1, columns_wide)
            count = flat_give.shape[0]
            sent = jnp.concatenate([flat_give, small_view]).astype(BF16)
            sent = lax.optimization_barrier(sent)
            got = swap(sent, axis, 1 << bit)
            stem_view = keep + got[0:count].astype(F32).reshape(keep.shape)
            small_view = sent[count:].astype(F32) + got[count:].astype(F32)
            live.remove((axis, bit))
        small_view = small_view.reshape(batch_count, -1, columns_wide)
        stem_part = stem_view.shape[1]
        late, riders = lax.optimization_barrier((late, riders))
        riders = jnp.concatenate([stem_view.astype(BF16), small_view.astype(BF16), riders], axis=1)
        got = lax.all_to_all(riders, "batch", 0, 0, tiled=True).reshape(batch_count, -1, columns_wide)
        both_parts = stem_part + small_view.shape[1]
        shards_sum = jnp.sum(got[:, 0:both_parts].astype(F32), axis=0)
        stem_shard, small_shard = shards_sum[0:stem_part], shards_sum[stem_part:]
        riders = got[:, both_parts:].reshape(batch_count, -1)
    feature_size = clips * head_rows
    feature_all = riders[:, 0:feature_size].reshape(batch_count * clips, head_rows)
    logit_all = riders[:, feature_size : feature_size + clips * CLS]
    logit_all = logit_all.reshape(batch_count * clips, CLS)
    mixing_shard, restore_shard = early[0:mixing_rows], early[mixing_rows:]
    condense_shard = late[0:condense_rows]
    lateral_shard = late[condense_rows : condense_rows + lateral_rows]
    head_grad = over_rows(feature_all, logit_all)
    class_grad = jnp.sum(logit_all.astype(F32), axis=0)
    affine_grad = jnp.concatenate([g1, g2, g3, g4, g5, g6, b1, b2, b3, b4, b5, b6, class_grad])

    small_speed = jnp.concatenate(
        [squeeze_velocity, blending_velocity, recover_velocity.reshape(small_rows, -1)], axis=1
    )
    small_speed = spread_all(small_speed.astype(BF16), ("batch",)).reshape(CFM, -1)

    leader = (tm_place == 0).astype(F32)
    squares = sum(jnp.sum(item * item) for item in (late, early, stem_shard))
    small_share = 1.0 if near else leader
    squares = squares + small_share * jnp.sum(small_shard * small_shard)
    squares = squares + leader * jnp.sum(head_grad * head_grad)
    first_device = leader * (batch_place == 0).astype(F32)
    squares = squares + first_device * jnp.sum(affine_grad * affine_grad)
    (total_squares,) = all_sum([squares], both)
    grad_norm = jnp.sqrt(total_squares) / clip_count
    factor = jnp.minimum(1.0, CLIP_AT / grad_norm) / clip_count

    small_speed = speed[:, out_rows:].reshape(CFM, -1)
    stem_rows = stem_weight.shape[0]
    if near:
        held = over_tm(low(shards_sum))
        stem_own = held[:, 0:stem_part].reshape(stem_rows, -1)
        small_shard = held[:, stem_part : stem_part + small_part].reshape(-1, columns_wide)
    else:
        stem_own = over_tm(low(stem_shard)).reshape(stem_rows, -1)

    def small_parts(small_whole):
        small_whole = small_whole.reshape(batch_count, small_blocks, small_rows, columns_wide)
        small_whole = jnp.swapaxes(small_whole, 1, 2).reshape(CFM, -1)
        small_grads = unpack(small_whole[:, 0 : 3 * CF + 9 * CFM + CF])
        speeds = unpack(small_speed)
        speeds = (speeds[0], speeds[1], speeds[2].reshape(CF, CFM).T)
        items = [
            low(MUON_KEEP * held.astype(F32) + grad.astype(F32) * factor)
            for held, grad in zip(speeds, small_grads)
        ]
        return small_grads, items

    def unpack(values):
        first = values[:, 0 : 3 * CF]
        second = values[:, 3 * CF : 3 * CF + 9 * CFM]
        return (first, second, values[:, 3 * CF + 9 * CFM :])

    def ratio_of(base):
        return math.sqrt(max(1.0, base.shape[0] * batch_count / base.shape[1]))

    def own(values, part):
        return lax.dynamic_slice_in_dim(values, batch_place * part, part, axis=0)

    def direct_orthos(stem_moved, shapes, items):
        tall_part = recover.shape[0]
        results = (
            rows_by_columns(stem_moved, shapes[0]),
            rows_by_columns(own(shapes[1], small_rows), items[0]),
            rows_by_columns(own(shapes[2], small_rows), items[1]),
            rows_by_columns(own(items[2].T, tall_part), shapes[3]),
        )
        return [low(result) for result in results]

    far_place = tm_place // 2
    factor_cell = factor.reshape(1, 1)
    bases = {
        carry: (lateral_velocity, condense_velocity, mixing_velocity, restore_velocity),
        renew: (lateral_weight, condense, mixing, restore),
    }

    def deep(item, depth):
        return jnp.pad(item, ((0, depth - item.shape[0]), (0, 0)))

    if near:
        pair_one = low(jnp.concatenate([condense_shard, restore_shard]))
        pair_two = low(
            jnp.concatenate([deep(mixing_shard, depth_one), deep(lateral_shard, depth_two)])
        )
        pair_own = jnp.where(far_place == 0, pair_one, pair_two)
        pair_got = swap(jnp.where(far_place == 0, pair_two, pair_one), "tm", 2)
        restore_speed = pick(restore_velocity.reshape(far, 2, depth_two, CSM), 1, core)
        restore_speed = low(restore_speed.reshape(far * depth_two, CSM))
        wide_shape = ((batch_count, out_rows, CSM), BF16)
        tall_shape = ((batch_count, out_rows, far * depth_two), BF16)
        gram_shape = ((CSM, CSM), BF16)
        moved_one, moved_two, stem_moved, keep, give, stem_gram, grad_wide, grad_tall = call(
            gram_kernel,
            [
                ((far * depth_one, CSM), BF16),
                ((far * depth_two, CSM), BF16),
                (stem_own.shape, BF16),
                gram_shape,
                gram_shape,
                ((batch_count, 16, CSM), BF16),
                wide_shape,
                tall_shape,
            ],
            [
                place_cell,
                factor_cell,
                speed,
                restore_speed,
                pair_own,
                pair_got,
                stem_velocity,
                stem_own,
            ],
            [((CSM, CSM), F32)],
            scalars=(0,),
        )
        gram = low(keep.astype(F32) + swap(give, "tm", 1).astype(F32))
        riders = low(small_shard)
        riders = jnp.concatenate(
            [
                jnp.pad(riders[0:40], ((0, 0), (0, 64))),
                jnp.pad(riders[40:], ((0, 8), (0, 64))),
            ],
            axis=1,
        )
        riders = jnp.broadcast_to(riders[None], (batch_count,) + riders.shape)
        got = lax.all_to_all(
            jnp.concatenate([gram.reshape(wide_shape[0]), stem_gram, riders], axis=1),
            "batch", 0, 0, tiled=True,
        )
        summed = low(jnp.sum(got[:, 0:80].astype(F32), axis=0))
        small_whole = jnp.concatenate([got[:, 80:120, 0:192], got[:, 80:112, 256:448]], axis=1)
        small_grads, items = small_parts(small_whole)
        whole = lax.all_to_all(
            jnp.concatenate(
                [jnp.broadcast_to(summed[None], (batch_count,) + summed.shape), grad_wide], axis=1
            ),
            "batch", 0, 0, tiled=True,
        )
        shaped, *shapes = call(
            block_shape_kernel,
            [gram_shape, ((192, 192), BF16)] + [((CFM, CFM), BF16)] * 3,
            [whole] + [rows_by_rows(item, item) for item in items],
            [((CSM, CSM), F32), ((192, 192), F32)],
            micros=10,
        )

        def put_rows(rule, held, tall):
            edge = far * depth_one
            second = jnp.where(far_place == 0, tall, held[..., edge:])
            held = jnp.concatenate([held[..., 0:edge], second], axis=-1)
            kernel = functools.partial(place_kernel, rule, far, main_rows, depth_one)
            return call(
                kernel,
                [(base.shape, F32) for base in bases[rule]],
                [place_cell, factor_cell, *pairs_of(held, held), *bases[rule]],
                [((tm_count,) + wide_shape[0], BF16)],
                scalars=(0,),
            )

        grads = put_rows(carry, whole[:, 80:144], grad_tall)
        ortho_wide, ortho_tall = call(
            ortho_kernel,
            [wide_shape, tall_shape],
            [place_cell, shaped, swap(shaped, "tm", 1), moved_one, moved_two],
            scalars=(0,),
        )
        ortho_wide = lax.all_to_all(ortho_wide, "batch", 0, 0, tiled=True)
        direct = direct_orthos(stem_moved, shapes, items)
        tied = lax.optimization_barrier((ortho_wide, *grads, *direct))
        ortho_wide, grads, direct = tied[0], tied[1:5], tied[5:]
        orthos = put_rows(renew, ortho_wide, ortho_tall)
    else:
        pair_one = jnp.concatenate([condense_shard, deep(restore_shard, depth_two)])
        pair_two = jnp.concatenate([deep(mixing_shard, depth_one), deep(lateral_shard, depth_two)])
        pairs = jnp.stack([pair_one, pair_two] + [jnp.zeros_like(pair_one)] * (far - 2)).astype(BF16)
        grads_held = by_place(
            [pick(pairs, 0, far_place)]
            + [swap(pick(pairs, 0, far_place ^ k), "tm", 2 * k) for k in range(1, far)],
            far_place,
        )

        def cut(held):
            one = jnp.concatenate(
                [
                    held[:, 0:main_rows].reshape(far * main_rows, CSM),
                    held[:, main_rows:depth_one].reshape(far * (depth_one - main_rows), CSM),
                ]
            )
            return one, held[:, depth_one:].reshape(far * depth_two, CSM)

        speed = speed[:, 0:out_rows].reshape(CSM, -1)
        speed_one = speed[:, 0 : far * depth_one].T
        restore_speed = pick(restore_velocity.reshape(far, 2, depth_two, CSM), 1, core)
        restore_speed = restore_speed.reshape(far * depth_two, CSM)
        speed_two = jnp.where(
            far_place == 0, restore_speed.astype(BF16), speed[:, far * depth_one :].T
        )
        grad_one, grad_two = cut(grads_held)
        used = far_place < 2

        def step_of(speed_part, grad_part):
            moved = MUON_KEEP * speed_part.astype(F32) + grad_part.astype(F32) * factor
            return jnp.where(used, moved, 0.0).astype(BF16)

        stem_moved = low(MUON_KEEP * stem_velocity + stem_own.astype(F32) * factor)

        moved_one = step_of(speed_one, grad_one)
        moved_two = step_of(speed_two, grad_two)
        gram_one = over_rows(moved_one, moved_one)
        gram_two = over_rows(moved_two, moved_two)
        gram = jnp.where(core == 0, gram_one, gram_two) + swap(
            jnp.where(core == 0, gram_two, gram_one), "tm", 1
        )
        stem_gram = over_rows(stem_moved, stem_moved)

        def flat_rows(item):
            return item.reshape(batch_count, -1).astype(GRAM)

        parts = [flat_rows(gram), flat_rows(stem_gram)]
        sizes = [part.shape[1] for part in parts]
        riders = jnp.broadcast_to(small_shard.reshape(1, -1).astype(GRAM), (batch_count, small_shard.size))

        def packed(items):
            whole = jnp.concatenate(items, axis=1)
            whole = jnp.pad(whole, ((0, 0), (0, -whole.shape[1] % 2048)))
            return whole.reshape(batch_count, -1, 256)

        def exchanged(items):
            whole = lax.all_to_all(packed(items), "batch", 0, 0, tiled=True)
            return whole.reshape(batch_count, -1)

        got = exchanged(parts + [riders])
        summed = jnp.sum(got[:, 0 : sum(sizes)].astype(F32), axis=0, keepdims=True).astype(GRAM)
        small_whole = got[:, sum(sizes) : sum(sizes) + small_shard.size]
        small_grads, items = small_parts(small_whole)
        grad_one, grad_two, summed = lax.optimization_barrier((grad_one, grad_two, summed))
        whole = exchanged([jnp.broadcast_to(summed, (batch_count, summed.shape[1]))]).astype(F32)
        gram = whole[:, 0 : sizes[0]].reshape(CSM, CSM)
        stem_gram = whole[:, sizes[0] : sum(sizes)].reshape(stem_gram.shape)

        shaped, *shapes = shape_of([gram, stem_gram] + [rows_by_rows(item, item) for item in items])
        shaped = low(shaped)
        shapes = [low(shape) for shape in shapes]
        shaped_other = swap(shaped, "tm", 1)
        shape_one = jnp.where(core == 0, shaped, shaped_other)
        shape_two = jnp.where(core == 0, shaped_other, shaped)

        def spread_rows(rule, bases, wide_one, wide_two, tall_two):
            lateral_base, condense_base, mixing_base, restore_base = bases
            wide_both = jnp.concatenate([wide_one, wide_two], axis=1)
            wide_both = wide_both.reshape(batch_count, out_rows, -1)
            held = lax.all_to_all(wide_both, "batch", 0, 0, tiled=True)
            width = far * depth_two
            tall = jnp.concatenate(
                [tall_two[:, k * width : (k + 1) * width] for k in range(CSM // width)], axis=0
            ).reshape(batch_count, out_rows, width)
            second = jnp.where(far_place == 0, tall, held[..., far * depth_one :])
            held = jnp.concatenate([held[..., 0 : far * depth_one], second], axis=-1)
            held = by_place(
                [held] + [swap(held, "tm", 2 * k) for k in range(1, far)], far_place
            )[0:2]
            other = swap(held, "tm", 1)
            held = (jnp.where(core == 0, held, other), jnp.where(core == 0, other, held))

            edge = far * main_rows
            stop = far * depth_one
            def taps_of(place, base, main_taps, size):
                block = jnp.stack([half[place] for half in held])
                main = block[..., 0:edge].reshape(
                    2, main_taps, batch_count // main_taps, out_rows, far, main_rows
                )
                main = jnp.transpose(main, (3, 1, 4, 0, 2, 5)).reshape(out_rows, -1)
                rest = block[..., edge:stop].reshape(
                    2, batch_count, out_rows, far, depth_one - main_rows
                )[..., 0:size]
                rest = jnp.transpose(rest, (2, 3, 0, 1, 4)).reshape(out_rows, -1)
                return jnp.concatenate([main, rest], axis=1)

            block = jnp.stack([half[1, :, :, stop:] for half in held])
            block = block.reshape(2, batch_count, out_rows, far, depth_two)[..., 0:lateral_rows]
            block = jnp.transpose(block, (2, 3, 0, 1, 4)).reshape(out_rows, tm_count, 5, -1)
            side_rows = jnp.swapaxes(block, 1, 2).reshape(out_rows, 5 * CF)
            tall_rows = []
            for half in held:
                block = half[0, :, :, stop:].reshape(CSM // width, width, width)
                block = jnp.concatenate([block[k] for k in range(CSM // width)], axis=1)
                tall_rows.append(block.reshape(far, depth_two, CSM))
            tall_rows = jnp.stack(tall_rows, axis=1).reshape(-1, CSM)
            results = (
                side_rows,
                taps_of(0, condense_base, 2, rest_depth),
                taps_of(1, mixing_base, 8, mixing_rows - main_rows),
                tall_rows,
            )
            return [rule(base, item.astype(F32), ratio_of(base), factor) for base, item in zip(bases, results)]

        grads = spread_rows(
            carry, bases[carry],
            grad_one.T, grad_two.T, grad_two,
        )
        orthos = spread_rows(
            renew, bases[renew],
            low(rows_by_rows(shape_one, moved_one)),
            low(rows_by_rows(shape_two, moved_two)),
            low(rows_by_columns(moved_two, shape_two)),
        )

    if not near:
        direct = direct_orthos(stem_moved, shapes, items)
    stem_ortho, *small_orthos = direct
    part = recover.shape[0]
    small_own = [
        own(small_grads[0], small_rows),
        own(small_grads[1], small_rows),
        own(small_grads[2].T, part),
    ]

    def both_of(weight, speed, grad, ortho):
        ortho = low(ortho).astype(F32)
        return (
            carry(speed, grad.astype(F32), 1.0, factor),
            renew(weight, ortho, ratio_of(weight), factor),
        )

    stem_pair = both_of(stem_weight, stem_velocity, stem_own, stem_ortho)
    small_pairs = [
        both_of(*items)
        for items in zip(
            (squeeze, blending, recover),
            (squeeze_velocity, blending_velocity, recover_velocity),
            small_own,
            small_orthos,
        )
    ]
    carried = [stem_pair[0], *grads] + [pair[0] for pair in small_pairs]
    updated = [stem_pair[1], *orthos] + [pair[1] for pair in small_pairs]
    head_new, head_first, head_second = adam(
        head_weight, head_moment, head_square, head_grad * factor, HEAD_RATE, WEIGHT_DECAY
    )
    affine_new, affine_first, affine_second = adam(
        affine, affine_moment, affine_square, affine_grad * factor, AFFINE_RATE, 0.0
    )
    return (
        *carried,
        *updated,
        head_new,
        head_first,
        head_second,
        affine_new,
        affine_first,
        affine_second,
        loss_total,
        clip_count,
        grad_norm,
    )


def solution(mesh):
    in_specs = (
        P("batch", "tm", None, None, None),
        P("batch"),
        P("batch"),
        P("batch"),
        P("batch"),
        P("batch", None),
        P("batch", None),
        P("batch", None),
        P("batch", None),
        P("batch", None),
        P("batch", None),
        P("batch", None),
        P("batch", None),
        P("batch", None),
        P("batch", None),
        P("batch", None),
        P("batch", None),
        P("batch", None),
        P("batch", None),
        P("batch", None),
        P("batch", None),
        P("batch", None),
        P("batch", None),
        P("batch", None),
        P(),
        P(),
        P(),
    )
    out_specs = (
        P("batch", None),
        P("batch", None),
        P("batch", None),
        P("batch", None),
        P("batch", None),
        P("batch", None),
        P("batch", None),
        P("batch", None),
        P("batch", None),
        P("batch", None),
        P("batch", None),
        P("batch", None),
        P("batch", None),
        P("batch", None),
        P("batch", None),
        P("batch", None),
        P("batch", None),
        P("batch", None),
        P("batch", None),
        P(),
        P(),
        P(),
        P(),
        P(),
        P(),
    )
    return jax.shard_map(
        per_device, mesh=mesh, in_specs=in_specs, out_specs=out_specs, check_vma=False
    )
```

```python
import functools
import math

import jax
import jax.numpy as jnp
from jax import lax
from jax.experimental import pallas as pl
from jax.experimental.pallas import tpu as pltpu
from jax.sharding import PartitionSpec as P

CS = 2048
CSM = 512
CF = 256
CFM = 64
CLS = 400
ALPHA = 4
NS_STEPS = 3
STEP = 10


HIGHEST = lax.Precision.HIGHEST
NORM_EPS = 1e-05
CLIP_AT = 0.01
MUON_RATE = 0.5
MUON_KEEP = 0.95
WEIGHT_DECAY = 0.01
ADAM_ONE = 0.9
ADAM_TWO = 0.999
ADAM_EPS = 1e-08
HEAD_RATE = 0.02
AFFINE_RATE = 0.1
NS_FIRST = 3.4445
NS_SECOND = -4.775
NS_THIRD = 2.0315


F32 = jnp.float32
BF16 = jnp.bfloat16
VMEM = 61 * 1024 * 1024
SIDE_AT = 9 * CSM
CONDENSE_AT = SIDE_AT + 5 * CF
RESTORE_AT = CONDENSE_AT + 3 * CS
GRAM = BF16
SIX = (CSM, CSM, CS, CFM, CFM, CF)


def swap(values, axis, mask):
    count = lax.axis_size(axis)
    return lax.ppermute(values, axis, [(i, i ^ mask) for i in range(count)])


def shift(values, axis, step):
    count = lax.axis_size(axis)
    route = [(i, i + step) for i in range(count) if 0 <= i + step < count]
    return lax.ppermute(values, axis, route)


def spread_all(rows, axes):
    count = math.prod(lax.axis_size(axis) for axis in axes)
    copies = jnp.broadcast_to(rows[None], (count,) + rows.shape)
    return lax.all_to_all(copies, axes, 0, 0, tiled=True)


def all_sum(pieces, axes):
    flat = jnp.concatenate([piece.reshape(-1) for piece in pieces])
    length = flat.shape[0]
    wide = -(-length // 1024) * 128
    flat = jnp.pad(flat, (0, 8 * wide - length)).reshape(8, wide)
    total = jnp.sum(spread_all(flat, axes), axis=0).reshape(-1)
    parts = []
    start = 0
    for piece in pieces:
        parts.append(total[start : start + piece.size].reshape(piece.shape))
        start = start + piece.size
    return parts


def pick(values, dim, place):
    return lax.dynamic_index_in_dim(values, place, dim, keepdims=False)


def bits(axis, low):
    count = lax.axis_size(axis).bit_length() - 1
    return [(axis, bit) for bit in range(count - 1, low - 1, -1)]


def halve(view, live, order):
    live = list(live)
    for axis, bit in order:
        dim = live.index((axis, bit))
        flag = (lax.axis_index(axis) >> bit) & 1
        got = swap(pick(view, dim, 1 - flag).astype(BF16), axis, 1 << bit)
        view = pick(view, dim, flag) + got.astype(F32)
        live.remove((axis, bit))
    return view


def dot(left, right, dims):
    return lax.dot_general(left, right, ((dims[0], dims[1]), ((), ())), preferred_element_type=F32)


def rows_by_rows(left, right):
    return dot(left, right, ((1,), (1,)))


def rows_by_columns(left, right):
    return dot(left, right, ((1,), (0,)))


def over_rows(left, right):
    return dot(left, right, ((0,), (0,)))


def split_affine(vector):
    gains = []
    shifts = []
    start = 0
    for width in SIX:
        gains.append(vector[start : start + width])
        start = start + width
    for width in SIX:
        shifts.append(vector[start : start + width])
        start = start + width
    return (gains, shifts, vector[start : start + CLS])


def silu_grad(values):
    sigma = jax.nn.sigmoid(values)
    return sigma * (1.0 + values * (1.0 - sigma))


def call(kernel, outs, args, scratch=(), far=(), copies=0, micros=6, scalars=()):
    specs = [
        pl.BlockSpec(
            memory_space=pl.ANY
            if place in far
            else pltpu.SMEM
            if place in scalars
            else pltpu.VMEM
        )
        for place in range(len(args))
    ]
    shapes = [pltpu.VMEM(shape, kind) for shape, kind in scratch]
    if copies:
        shapes.append(pltpu.SemaphoreType.DMA((copies,)))
    return pl.pallas_call(
        kernel,
        in_specs=specs,
        out_shape=[jax.ShapeDtypeStruct(shape, kind) for shape, kind in outs],
        scratch_shapes=shapes,
        compiler_params=pltpu.CompilerParams(vmem_limit_bytes=VMEM),
        cost_estimate=pl.CostEstimate(
            flops=micros * 1150000000, bytes_accessed=micros * 3000000, transcendentals=0
        ),
    )(*args)


def fetch(source, target, flags, spans):
    started = []
    for place, (there, here, width) in enumerate(spans):
        copy = pltpu.make_async_copy(
            source.at[:, pl.ds(there, width)], target.at[:, pl.ds(here, width)], flags.at[place]
        )
        copy.start()
        started.append(copy)
    return started


def fetch_tall(source, target, flags, start):
    started = []
    count = flags.shape[0] // 4
    block = source.shape[0] // count
    for place in range(4 * count):
        b, k = (place // 4, place % 4)
        copy = pltpu.make_async_copy(
            source.at[pl.ds(b * block, block), pl.ds(start + k * CSM, CSM)],
            target.at[pl.ds(place * block, block), :],
            flags.at[place],
        )
        copy.start()
        started.append(copy)
    return started


def nt(left, right):
    return dot(left, right, ((1,), (1,)))


def nn(left, right):
    return dot(left, right, ((1,), (0,)))


def silu(values):
    return values * jax.nn.sigmoid(values)


def low(values):
    return values.astype(BF16)


def sums(held, other):
    return (
        jnp.sum(held, axis=0, keepdims=True),
        jnp.sum(held * other, axis=0, keepdims=True),
    )


def flat(values):
    return values.reshape(values.shape[0] * values.shape[1], values.shape[2])


def put_narrow(out, block, slow, fast, extra=()):
    block[...] = jnp.zeros_like(block)
    for place, vector in enumerate(slow):
        block[2 * place : 2 * place + 1, :] = vector[:, 0:256]
        block[2 * place + 1 : 2 * place + 2, :] = vector[:, 256:512]
    for place, vector in enumerate(fast):
        block[4 + place : 5 + place, 0:CFM] = vector
    for place, value in enumerate(extra):
        block[6 + place : 7 + place, 0:128] = jnp.broadcast_to(value, (1, 128))
    out[...] = jnp.broadcast_to(block[...][None], out.shape).astype(out.dtype)


def get_narrow(total):
    slow = [
        jnp.concatenate([total[2 * k : 2 * k + 1], total[2 * k + 1 : 2 * k + 2]], axis=1)
        for k in range(2)
    ]
    fast = [total[4 + k : 5 + k, 0:CFM] for k in range(2)]
    return slow, fast


def put_wide(out, slow, fast, extra=None):
    out[...] = jnp.zeros_like(out)
    for place, vector in enumerate(slow):
        for row in range(4):
            out[4 * place + row : 4 * place + row + 1, 0:512] = vector[:, 512 * row : 512 * row + 512]
    for place, vector in enumerate(fast):
        for row in range(2):
            spot = 2 * place + row
            out[spot : spot + 1, 512:640] = vector[:, 128 * row : 128 * row + 128]
    if extra is not None:
        for row in range(4, 7):
            part = low(jnp.broadcast_to(extra, (1, 128))).astype(F32)
            out[row : row + 1, 512:640] = part
            extra = extra - part


def get_wide(total):
    slow = [
        jnp.concatenate([total[4 * k + row : 4 * k + row + 1, 0:512] for row in range(4)], axis=1)
        for k in range(2)
    ]
    fast = [
        jnp.concatenate(
            [total[2 * k + row : 2 * k + row + 1, 512:640] for row in range(2)], axis=1
        )
        for k in range(2)
    ]
    return slow, fast


def moments(pair, count):
    mean = pair[0] / count
    spread = pair[1] / count - mean * mean
    return mean, lax.rsqrt(spread + NORM_EPS)


def counts(total, frames):
    count = total[6:7, 0:1]
    return count, count * frames


def in_relation(place, outs, values):
    for k, out in enumerate(outs):
        for p, value in enumerate(values):

            @pl.when(jnp.bitwise_xor(place, k) == p)
            def store(out=out, value=value):
                out[...] = value


def stem_kernel(near, place, slow_video, fast_video, weight, mask, *refs):
    videos = refs[0:4] if near else ()
    slow_pre, fast_pre, slow_low, fast_low, *shares = refs[len(videos) :]
    held = mask[...]
    for k in range(3):
        pre = nt(slow_video[k], weight[0:CS, :])
        if k == 1:
            slow_pre[...] = pre
        act = low(silu(pre) * held)
        slow_low[k] = act
        if k == 1 and not near:
            count, _, width = shares[0].shape
            for p in range(count):
                shares[0][p] = act[:, p * width : (p + 1) * width]
    if near:
        width = CS // 4
        own_rows = weight[pl.ds(pl.multiple_of(place[0] * width, width), width), :]
        for video, share in zip(videos, shares[0:4]):
            share[...] = low(silu(nt(video[...], own_rows)) * held)
    count = fast_video.shape[0]
    for k in range(count):
        pre = nt(fast_video[k], weight[CS:, :])
        if 2 <= k < count - 1:
            fast_pre[k - 2] = pre
        act = low(silu(pre) * held)
        fast_low[k] = act
        if near and k < 5:
            parts = [act[:, 0:128], act[:, 128:256]]
            in_relation(place[0] // 2, [side.at[k] for side in shares[4:6]], parts)


def first_kernel(
    slow_low, fast_low, weights, squeeze, mask, valid, h1, h4, out, block, first, flags
):
    spans = [(SIDE_AT, 0, 5 * CF)]
    spans += [(CONDENSE_AT + k * CS, 5 * CF + k * CS, CS) for k in range(3)]
    copies = fetch(weights, first, flags, spans)
    held = mask[...]
    copies[0].wait()
    total = None
    for k in range(5):
        term = nt(fast_low[k], first[:, k * CF : (k + 1) * CF])
        total = term if total is None else total + term
    for k in range(3):
        start = 5 * CF + k * CS
        copies[1 + k].wait()
        total = total + nt(slow_low[k], first[:, start : start + CS])
    h1[...] = total
    slow = sums(total * held, total)
    frames = h4.shape[0]
    fast = None
    for frame in range(frames):
        piece = None
        for k in range(3):
            term = nt(fast_low[1 + k + frame], squeeze[:, k * CF : (k + 1) * CF])
            piece = term if piece is None else piece + term
        h4[frame] = piece
        pair = sums(piece * held, piece)
        fast = pair if fast is None else tuple(a + b for a, b in zip(fast, pair))
    put_narrow(out, block, slow, fast, (jnp.sum(held), jnp.sum(valid[...])))


def fill(pad, values):
    side = pad.shape[0] - 2
    pad[1 : side + 1, 1 : side + 1] = values.reshape(side, side, pad.shape[2], pad.shape[3])


def tap_of(pad, down, right):
    side = pad.shape[0] - 2
    values = pad[down : down + side, right : right + side]
    return values.reshape(side * side * pad.shape[2], pad.shape[3])


def second_kernel(near, *refs):
    place, h1, h4, got, slow_par, fast_par, mask, weights, blending = refs[0:9]
    h2, h5, total_out, out = refs[9:13]
    shares = refs[13:17] if near else refs[13:14]
    pad, fast_pad, block, mixing, flags = refs[-5:]
    copies = fetch(weights, mixing, flags, [(tap * CSM, tap * CSM, CSM) for tap in range(9)])
    held = mask[...]
    frames = h4.shape[0]
    total = jnp.sum(got[...].astype(F32), axis=0)
    total_out[...] = total
    slow, fast = get_narrow(total)
    slow_count, fast_count = counts(total, frames)
    mean, inverse = moments(slow, slow_count)
    level = slow_par[0:1] * ((h1[...] - mean) * inverse) + slow_par[1:2]
    pad[...] = jnp.zeros_like(pad)
    act = low(silu(level) * held)
    if near:
        in_relation(place[0], shares, [act[:, p * 128 : (p + 1) * 128] for p in range(4)])
    else:
        shares[0][...] = act
    fill(pad, act.astype(F32))
    acc = None
    for tap in range(9):
        piece = low(tap_of(pad, tap // 3, tap % 3))
        copies[tap].wait()
        term = nt(piece, mixing[:, tap * CSM : (tap + 1) * CSM])
        acc = term if acc is None else acc + term
    h2[...] = acc
    slow_pair = sums(acc * held, acc)
    mean, inverse = moments(fast, fast_count)
    fast_pad[...] = jnp.zeros_like(fast_pad)
    fast_pair = None
    for frame in range(frames):
        level = fast_par[0:1] * ((h4[frame] - mean) * inverse) + fast_par[1:2]
        fill(fast_pad, low(silu(level) * held).astype(F32))
        acc = None
        for tap in range(9):
            piece = low(tap_of(fast_pad, tap // 3, tap % 3))
            term = nn(piece, blending[tap])
            acc = term if acc is None else acc + term
        h5[frame] = acc
        pair = sums(acc * held, acc)
        fast_pair = pair if fast_pair is None else tuple(a + b for a, b in zip(fast_pair, pair))
    put_narrow(out, block, slow_pair, fast_pair)


def third_kernel(
    h2, h5, before, got, slow_par, fast_par, mask, weights, recover, a2, a5, h3, h6, total_out, out,
    restore, flags,
):
    copies = fetch_tall(weights, restore, flags, RESTORE_AT)
    held = mask[...]
    frames = h5.shape[0]
    total = jnp.sum(got[...].astype(F32), axis=0)
    total_out[...] = total
    slow, fast = get_narrow(total)
    slow_count, fast_count = counts(before[...], frames)
    mean, inverse = moments(slow, slow_count)
    level = slow_par[0:1] * ((h2[...] - mean) * inverse) + slow_par[1:2]
    act = low(silu(level) * held)
    a2[...] = act
    for copy in copies:
        copy.wait()
    acc = nt(act, restore[...])
    h3[...] = acc
    slow_pair = sums(acc * held, acc)
    mean, inverse = moments(fast, fast_count)
    fast_pair = None
    for frame in range(frames):
        level = fast_par[0:1] * ((h5[frame] - mean) * inverse) + fast_par[1:2]
        act = low(silu(level) * held)
        a5[frame] = act
        acc = nt(act, recover[...])
        h6[frame] = acc
        pair = sums(acc * held, acc)
        fast_pair = pair if fast_pair is None else tuple(a + b for a, b in zip(fast_pair, pair))
    put_wide(out, slow_pair, fast_pair)


def by_clip(values, clips):
    return jnp.sum(values.reshape(-1, clips, values.shape[1]), axis=0)


def pool_kernel(
    h3, h6, slow_pre, fast_pre, before, got, slow_par, fast_par, mask, out, total_out
):
    held = mask[...]
    frames = h6.shape[0]
    clips = out.shape[0]
    total = jnp.sum(got[...].astype(F32), axis=0)
    total_out[...] = total
    slow, fast = get_wide(total)
    slow_count, fast_count = counts(before[...], frames)
    mean, inverse = moments(slow, slow_count)
    scaled = (h3[...] - mean) * inverse
    residual = silu(slow_pre[...]) * held + slow_par[0:1] * scaled + slow_par[1:2]
    out[:, 0:CS] = by_clip(silu(residual) * held, clips)
    mean, inverse = moments(fast, fast_count)
    pooled = None
    for frame in range(frames):
        scaled = (h6[frame] - mean) * inverse
        residual = silu(fast_pre[frame]) * held + fast_par[0:1] * scaled + fast_par[1:2]
        part = by_clip(silu(residual) * held, clips)
        pooled = part if pooled is None else pooled + part
    out[:, CS:] = pooled


def mixed(average, values):
    total = None
    for k in range(values.shape[0]):
        term = average[:, k : k + 1] * values[k : k + 1, :]
        total = term if total is None else total + term
    return total


def head_kernel(
    pools, head, bias, ids_down, ids_across, labels, valid, area, h3, h6, slow_pre, fast_pre,
    before, total_in, slow_par, fast_par, mask, features, logit_low, d3, d6, out,
):
    held = mask[...]
    frames = h6.shape[0]
    clips = features.shape[0]
    tm_count = pools.shape[0]
    parts = [pools[k] for k in range(tm_count)]
    while len(parts) > 1:
        parts = [parts[k] + parts[k + 1] for k in range(0, len(parts), 2)]
    (pool,) = parts
    slow_divide = area[...] * tm_count
    fast_divide = slow_divide * frames
    slow_feature = low(pool[:, 0:CS] / slow_divide)
    fast_feature = low(pool[:, CS:] / fast_divide)
    features[:, 0:CS] = slow_feature
    features[:, CS:] = fast_feature
    logits = nn(slow_feature, head[0:CS, :]) + nn(fast_feature, head[CS:, :]) + bias[...]
    same = (ids_down[...] == ids_across[...]).astype(F32)
    average = same / jnp.sum(same, axis=1, keepdims=True)
    mean_logits = mixed(average, logits)
    top = jnp.max(mean_logits, axis=1, keepdims=True)
    powers = jnp.exp(mean_logits - top)
    whole = jnp.sum(powers, axis=1, keepdims=True)
    classes = lax.broadcasted_iota(jnp.int32, mean_logits.shape, 1)
    onehot = (labels[...] == classes).astype(F32)
    picked = jnp.sum(onehot * mean_logits, axis=1, keepdims=True)
    loss = jnp.sum(valid[...] * (jnp.log(whole) + top - picked))
    mean_grad = valid[...] * (powers / whole - onehot)
    logit = low(mixed(average, mean_grad))
    logit_low[...] = logit
    slow_count, fast_count = counts(before[...], frames)
    slow, fast = get_wide(total_in[...])

    grad = nt(logit, head[0:CS, :]) / slow_divide
    mean, inverse = moments(slow, slow_count)
    scaled = (h3[...] - mean) * inverse
    residual = silu(slow_pre[...]) * held + slow_par[0:1] * scaled + slow_par[1:2]
    down = held * silu_grad(residual)
    down = (down.reshape(-1, clips, CS) * grad[None]).reshape(down.shape)
    d3[...] = down
    slow_pair = sums(down, scaled)

    grad = nt(logit, head[CS:, :]) / fast_divide
    mean, inverse = moments(fast, fast_count)
    fast_pair = None
    for frame in range(frames):
        scaled = (h6[frame] - mean) * inverse
        residual = silu(fast_pre[frame]) * held + fast_par[0:1] * scaled + fast_par[1:2]
        down = held * silu_grad(residual)
        down = (down.reshape(-1, clips, CF) * grad[None]).reshape(down.shape)
        d6[frame] = down
        pair = sums(down, scaled)
        fast_pair = pair if fast_pair is None else tuple(a + b for a, b in zip(fast_pair, pair))
    put_wide(out, slow_pair, fast_pair, loss)


def under(upstream, values, mean, inverse, gain, pair, count, held):
    scaled = (values - mean) * inverse
    return low(held * gain * inverse * (upstream - (pair[0] + scaled * pair[1]) / count))


def third_back_kernel(
    near, place, d3, d6, h3, h6, h2, h5, before, total3, total2, got, slow3, fast3, slow2, fast2, mask,
    weights, recover, u6, e2, e5, total_out, out, *rest
):
    u3 = rest[0:4] if near else rest[0:1]
    block, restore, flags = rest[-3:]
    copies = fetch_tall(weights, restore, flags, RESTORE_AT)
    held = mask[...]
    frames = h6.shape[0]
    total = jnp.sum(got[...].astype(F32), axis=0)
    total_out[...] = total
    slow_count, fast_count = counts(before[...], frames)
    slow_pair, fast_pair = get_wide(total)
    slow, fast = get_wide(total3[...])
    slow_two, fast_two = get_narrow(total2[...])
    mean, inverse = moments(slow, slow_count)
    upper = under(d3[...], h3[...], mean, inverse, slow3[0:1], slow_pair, slow_count, held)
    if near:
        wide = upper.astype(F32)
        tiles = [wide[:, k * 128 : (k + 1) * 128] for k in range(CS // 128)]
        turned = [pltpu.roll(tile, 64, 1) for tile in tiles]
        first_half = lax.broadcasted_iota(jnp.int32, tiles[0].shape, 1) < 64
        parts = []
        for p in range(4):
            held_tiles = []
            for k in range(4):
                one = 4 * k + p // 2
                two = one + 2
                if p % 2 == 0:
                    tile = jnp.where(first_half, tiles[one], turned[two])
                else:
                    tile = jnp.where(first_half, turned[one], tiles[two])
                held_tiles.append(low(tile))
            parts.append(jnp.concatenate(held_tiles, axis=1))
        in_relation(place[0], u3, parts)
    else:
        u3[0][...] = upper
    mean, inverse = moments(slow_two, slow_count)
    scaled = (h2[...] - mean) * inverse
    for copy in copies:
        copy.wait()
    down = nn(upper, restore[...]) * held * silu_grad(slow2[0:1] * scaled + slow2[1:2])
    e2[...] = down
    slow_out = sums(down, scaled)
    mean, inverse = moments(fast, fast_count)
    mean_two, inverse_two = moments(fast_two, fast_count)
    fast_out = None
    for frame in range(frames):
        upper = under(d6[frame], h6[frame], mean, inverse, fast3[0:1], fast_pair, fast_count, held)
        u6[frame] = upper
        scaled = (h5[frame] - mean_two) * inverse_two
        down = nn(upper, recover[...]) * held * silu_grad(fast2[0:1] * scaled + fast2[1:2])
        e5[frame] = down
        pair = sums(down, scaled)
        fast_out = pair if fast_out is None else tuple(a + b for a, b in zip(fast_out, pair))
    put_narrow(out, block, slow_out, fast_out)


def second_back_kernel(
    e2, e5, h2, h5, h1, h4, total2, total1, got, slow2, fast2, slow1, fast1, mask,
    weights, blending, u2, u5, e1, e4, blend_grad, total_out, out, pad, fast_pad, act_pad, block,
    mixing, flags,
):
    copies = fetch(weights, mixing, flags, [(tap * CSM, tap * CSM, CSM) for tap in range(9)])
    held = mask[...]
    frames = h5.shape[0]
    total = jnp.sum(got[...].astype(F32), axis=0)
    total_out[...] = total
    slow_count, fast_count = counts(total1[...], frames)
    slow_pair, fast_pair = get_narrow(total)
    slow_two, fast_two = get_narrow(total2[...])
    slow_one, fast_one = get_narrow(total1[...])
    mean, inverse = moments(slow_two, slow_count)
    upper = under(e2[...], h2[...], mean, inverse, slow2[0:1], slow_pair, slow_count, held)
    u2[...] = upper
    pad[...] = jnp.zeros_like(pad)
    fill(pad, upper.astype(F32))
    acc = None
    for tap in range(9):
        piece = low(tap_of(pad, 2 - tap // 3, 2 - tap % 3))
        copies[tap].wait()
        term = nn(piece, mixing[:, tap * CSM : (tap + 1) * CSM])
        acc = term if acc is None else acc + term
    mean, inverse = moments(slow_one, slow_count)
    scaled = (h1[...] - mean) * inverse
    down = acc * held * silu_grad(slow1[0:1] * scaled + slow1[1:2])
    e1[...] = down
    slow_out = sums(down, scaled)
    mean, inverse = moments(fast_two, fast_count)
    mean_one, inverse_one = moments(fast_one, fast_count)
    fast_pad[...] = jnp.zeros_like(fast_pad)
    act_pad[...] = jnp.zeros_like(act_pad)
    fast_out = None
    for frame in range(frames):
        upper = under(e5[frame], h5[frame], mean, inverse, fast2[0:1], fast_pair, fast_count, held)
        u5[frame] = upper
        scaled = (h4[frame] - mean_one) * inverse_one
        level = fast1[0:1] * scaled + fast1[1:2]
        fill(fast_pad, upper.astype(F32))
        fill(act_pad, low(silu(level) * held).astype(F32))
        turned = low(upper.astype(F32).T)
        acc = None
        for tap in range(9):
            down_by, right_by = (tap // 3, tap % 3)
            piece = low(tap_of(fast_pad, 2 - down_by, 2 - right_by))
            term = nt(piece, blending[tap])
            acc = term if acc is None else acc + term
            part = nn(turned, low(tap_of(act_pad, down_by, right_by)))
            blend_grad[tap] = part if frame == 0 else blend_grad[tap] + part
        down = acc * held * silu_grad(level)
        e4[frame] = down
        pair = sums(down, scaled)
        fast_out = pair if fast_out is None else tuple(a + b for a, b in zip(fast_out, pair))
    put_narrow(out, block, slow_out, fast_out)


def mixing_grad_kernel(acts, uppers, out, pad):
    count = acts.shape[0]
    pad[...] = jnp.zeros_like(pad)
    for place in range(count):
        fill(pad.at[place], acts[place].astype(F32))
    for tap in range(9):
        total = None
        for place in range(count):
            piece = low(tap_of(pad.at[place], tap // 3, tap % 3))
            term = dot(piece, uppers[place], ((0,), (0,)))
            total = term if total is None else total + term
        out[tap] = low(total)


def first_back_kernel(
    e1, e4, h1, h4, total1, got, slow1, fast1, mask, u1, u4, total_out
):
    held = mask[...]
    frames = h4.shape[0]
    total = jnp.sum(got[...].astype(F32), axis=0)
    total_out[...] = total
    slow_count, fast_count = counts(total1[...], frames)
    slow_pair, fast_pair = get_narrow(total)
    slow, fast = get_narrow(total1[...])
    mean, inverse = moments(slow, slow_count)
    u1[...] = under(e1[...], h1[...], mean, inverse, slow1[0:1], slow_pair, slow_count, held)
    mean, inverse = moments(fast, fast_count)
    for frame in range(frames):
        u4[frame] = under(
            e4[frame], h4[frame], mean, inverse, fast1[0:1], fast_pair, fast_count, held
        )


def by_frame(place, target, parts):
    target[0] = jnp.zeros_like(target[0])
    target[len(parts) + 1] = jnp.zeros_like(target[0])
    for k, part in enumerate(parts):
        target[jnp.bitwise_xor(place, k) + 1] = part


def turn(parts):
    own, across, others = parts
    return [own[...], others[0], across[...], others[1]]


def stem_grad_kernel(
    place, slow_up, fast_up, video, small, out_0, out_1, out_2, out_3, total
):
    total[0:CS, :] = dot(slow_up[...], video[0], ((0,), (0,)))
    fast = None
    for frame in range(fast_up.shape[0]):
        term = dot(fast_up[frame], video[frame], ((0,), (0,)))
        fast = term if fast is None else fast + term
    total[CS:, :] = fast
    size = total.shape[0] // 8
    for k, out in enumerate((out_0, out_1, out_2, out_3)):
        target = jnp.bitwise_xor(place[0], k)
        for b in range(8):
            start = pl.multiple_of(b * size + target * (size // 4), 8)
            rows = total[pl.ds(start, size // 4), :]
            out[b] = low(jnp.concatenate([rows, small[target, b]]))


def early_kernel(*refs):
    uppers, acts, out = refs[0:4], refs[4:7], refs[7]
    total = None
    for upper, act in zip(uppers, turn(acts)):
        term = dot(upper[...], act, ((0,), (0,)))
        total = term if total is None else total + term
    size = total.shape[0] // out.shape[0]
    for b in range(out.shape[0]):
        out[b] = low(total[b * size : (b + 1) * size])


def mixing_kernel(*refs):
    acts, uppers, restore, out, pad = refs[0:4], refs[4:7], refs[7], refs[8], refs[9]
    pad[...] = jnp.zeros_like(pad)
    for k, act in enumerate(acts):
        fill(pad.at[k], act[...].astype(F32))
    parts = turn(uppers)
    for tap in range(9):
        total = None
        for k, upper in enumerate(parts):
            term = dot(low(tap_of(pad.at[k], tap // 3, tap % 3)), upper, ((0,), (0,)))
            total = term if total is None else total + term
        if tap < 8:
            out[tap, 0:128, :] = low(total)
        else:
            for b in range(8):
                out[b, 128:144, :] = low(total[b * 16 : (b + 1) * 16])
    for b in range(8):
        out[b, 144:208, :] = restore[b]


def late_kernel(*refs):
    place, cells, sides, uppers = refs[0], refs[1:5], refs[5:8], refs[8:11]
    out, frames, side_total, side_rows = refs[11:15]
    here = place[0]
    by_frame(here, frames, [cell[...] for cell in cells])
    parts = turn(uppers)
    for tap in range(3):
        total = None
        for k, upper in enumerate(parts):
            cell = frames[jnp.bitwise_xor(here, k) + tap]
            term = dot(cell, upper, ((0,), (0,)))
            total = term if total is None else total + term
        for b in range(4):
            if tap < 2:
                out[tap * 4 + b, 0:128, :] = low(total[b * 128 : (b + 1) * 128])
            else:
                out[2 * b, 128:192, :] = low(total[b * 128 : b * 128 + 64])
                out[2 * b + 1, 128:192, :] = low(total[b * 128 + 64 : (b + 1) * 128])
    core = here % 2
    own, across, others = sides
    for tap in range(5):
        total = None
        turned = (own[tap], others[0, tap], across[tap], others[1, tap])
        for side, upper in zip(turned, parts):
            term = dot(side, upper, ((0,), (0,)))
            total = term if total is None else total + term
        side_total[...] = total
        side_rows[tap * 64 : (tap + 1) * 64, :] = side_total[
            pl.ds(pl.multiple_of(core * 64, 64), 64), :
        ]
    blank = jnp.zeros((8, CSM), F32)
    for b in range(8):
        rows = jnp.concatenate([side_rows[b * 40 : (b + 1) * 40, :], blank])
        out[b, 192:240, :] = low(rows)


def stem_back_kernel(near, place, *refs):
    u1_held = refs[0:3] if near else refs[0]
    (
        u4, u4_before, u4_after, weights, squeeze, d3, d6, slow_pre, fast_pre,
        mask, slow_up, fast_up, first, frames_held, flags,
    ) = refs[-15:]
    spans = [(CONDENSE_AT + k * CS, 5 * CF + k * CS, CS) for k in range(3)]
    copies = fetch(weights, first, flags, spans + [(SIDE_AT, 0, 5 * CF)])
    held = mask[...]
    frames = fast_up.shape[0]
    total = d3[...]
    if near:
        by_frame(place[0], frames_held, turn(u1_held))
        source = frames_held
    else:
        source = u1_held
    u1_before, u1, u1_after = [source[place[0] + k] for k in range(3)]
    for tap, piece in enumerate((u1_after, u1, u1_before)):
        start = 5 * CF + tap * CS
        copies[tap].wait()
        total = total + nn(piece, first[:, start : start + CS])
    copies[3].wait()
    slow_up[...] = low(total * held * silu_grad(slow_pre[...]))
    for frame in range(frames):
        total = d6[frame]
        pairs = [(frame + 2, u1)] if frame < 3 else []
        pairs = pairs + ([(frame - 2, u1_after)] if frame >= 2 else [])
        for tap, piece in pairs:
            total = total + nn(piece, first[:, tap * CF : (tap + 1) * CF])
        for tap in range(3):
            place = frame + 1 - tap
            if place < 0:
                piece = u4_before[...]
            elif place >= frames:
                piece = u4_after[...]
            else:
                piece = u4[place]
            total = total + nn(piece, squeeze[:, tap * CF : (tap + 1) * CF])
        fast_up[frame] = low(total * held * silu_grad(fast_pre[frame]))


def product(left, right):
    left_high = low(left)
    right_high = low(right)
    if left.shape[0] >= CSM:
        return nn(left_high, right_high)
    left_rest = low(left - left_high.astype(F32))
    right_rest = low(right - right_high.astype(F32))
    return nn(left_high, right_high) + (nn(left_high, right_rest) + nn(left_rest, right_high))


def shape_kernel(*refs):
    half = len(refs) // 2
    grams = []
    eyes = []
    scales = []
    totals = []
    for source in refs[:half]:
        size = source.shape[0]
        gram = source[...]
        rows = lax.broadcasted_iota(jnp.int32, (size, size), 0)
        columns = lax.broadcasted_iota(jnp.int32, (size, size), 1)
        eye = (rows == columns).astype(F32)
        diagonal = jnp.sum(gram * eye, axis=1, keepdims=True)
        diagonal = jnp.sum(diagonal, axis=0, keepdims=True)
        scale = 1.0 / (jnp.sqrt(diagonal) + 1e-07)
        grams.append(gram * (scale * scale))
        eyes.append(eye)
        scales.append(scale)
    for step in range(NS_STEPS):
        extras = [NS_SECOND * gram + NS_THIRD * product(gram, gram) for gram in grams]
        if step == 0:
            totals = [NS_FIRST * eye + extra for eye, extra in zip(eyes, extras)]
        else:
            totals = [
                NS_FIRST * total + product(extra, total) for total, extra in zip(totals, extras)
            ]
        if step + 1 < NS_STEPS:
            middles = [NS_FIRST * g + product(extra, g) for g, extra in zip(grams, extras)]
            grams = [NS_FIRST * m + product(extra, m) for m, extra in zip(middles, extras)]
    for target, total, scale in zip(refs[half:], totals, scales):
        target[...] = (total * scale).astype(target.dtype)


def block_shape_kernel(whole, *refs):
    small, outs = refs[0:3], refs[3:8]
    gram, stem, packed = refs[8:11]
    for b in range(8):
        packed[b * 40 : (b + 1) * 40, :] = whole[b, 64:112, :].astype(F32)[0:40]
        rows = whole[b, 96:128, :].astype(F32)[8:24]
        stem[b * 24 : b * 24 + 16, :] = rows[:, 0:192]
        stem[b * 24 + 16 : b * 24 + 24, :] = rows[0:8, 256:448]
    gram[0:128, :] = packed[0:128, :]
    gram[128:256, 128:512] = packed[128:256, 0:384]
    gram[256:384, 256:384] = packed[128:256, 384:512]
    for k, (row, column) in enumerate(((256, 384), (384, 384))):
        for half in range(2):
            start = (2 * k + half) * 128
            gram[row + 64 * half : row + 64 * half + 64, column : column + 128] = packed[
                256:320, start : start + 128
            ]
    for k in range(3):
        edge = 128 * (k + 1)
        gram[edge:512, edge - 128 : edge] = gram[edge - 128 : edge, edge:512].T
    shape_kernel(gram, stem, *small, *outs)


def gram_kernel(
    place, factor, speed, restore_speed, own, got, stem_speed, stem_grad, one, two, stem_out,
    keep, give, stem_gram, wide, tall, held,
):
    x = place[0] // 2
    core = place[0] % 2
    scale = factor[...]
    for spot, part in ((x, own), (1 - x, got)):
        held[pl.ds(pl.multiple_of(spot * 128, 128), 128), :] = part[0:128, :].astype(F32)
        held[pl.ds(pl.multiple_of(spot * 64 + 256, 64), 64), :] = part[128:192, :].astype(F32)
        held[pl.ds(pl.multiple_of(spot * 64 + 384, 64), 64), :] = part[192:256, :].astype(F32)
    speeds = jnp.concatenate([speed[b, 0:64, :].astype(F32) for b in range(8)]).T
    grads = held[...]
    speed_two = jnp.where(x == 0, restore_speed[...].astype(F32), speeds[384:512])
    moved_one = low(MUON_KEEP * speeds[0:384] + grads[0:384] * scale)
    moved_two = low(MUON_KEEP * speed_two + grads[384:512] * scale)
    one[...] = moved_one
    two[...] = moved_two
    gram_one = low(dot(moved_one, moved_one, ((0,), (0,))))
    gram_two = low(dot(moved_two, moved_two, ((0,), (0,))))
    put_packed(keep, jnp.where(core == 0, gram_one, gram_two))
    put_packed(give, jnp.where(core == 0, gram_two, gram_one))
    moved = low(MUON_KEEP * stem_speed[...] + stem_grad[...].astype(F32) * scale)
    stem_out[...] = moved
    gram = dot(moved, moved, ((0,), (0,)))
    stem_gram[...] = jnp.zeros_like(stem_gram)
    blank = jnp.zeros((8, 192), F32)
    for b in range(8):
        stem_gram[b, :, 0:192] = low(gram[b * 24 : b * 24 + 16])
        rest = jnp.concatenate([gram[b * 24 + 16 : b * 24 + 24], blank])
        stem_gram[b, :, 256:448] = low(rest)
    turned = low(grads.T)
    for b in range(8):
        wide[b] = turned[b * 64 : (b + 1) * 64]
    put_tall(tall, low(grads[384:512]))


def put_packed(out, gram):
    out[0:128, :] = gram[0:128]
    out[128:256, 0:384] = gram[128:256, 128:512]
    out[128:256, 384:512] = gram[256:384, 256:384]
    for k, (row, column) in enumerate(((256, 384), (384, 384))):
        for half in range(2):
            start = (2 * k + half) * 128
            out[256:320, start : start + 128] = gram[
                row + 64 * half : row + 64 * half + 64, column : column + 128
            ]


def put_tall(out, values):
    for k in range(4):
        for h in range(2):
            out[2 * k + h] = values[h * 64 : (h + 1) * 64, k * 128 : (k + 1) * 128]


def ortho_kernel(place, shaped, other, one, two, wide, tall):
    core = place[0] % 2
    shape_one = jnp.where(core == 0, shaped[...], other[...])
    shape_two = jnp.where(core == 0, other[...], shaped[...])
    first = low(nt(shape_one, one[...]))
    second = low(nt(shape_two, two[...]))
    for b in range(8):
        wide[b, :, 0:384] = first[b * 64 : (b + 1) * 64]
        wide[b, :, 384:512] = second[b * 64 : (b + 1) * 64]
    put_tall(tall, low(nn(two[...], shape_two)))


def shape_of(grams):
    return call(shape_kernel, [(item.shape, F32) for item in grams], grams, micros=13)


def carry(base, value, ratio, factor):
    return MUON_KEEP * base + value * factor


def renew(base, value, ratio, factor):
    return base - MUON_RATE * (value * ratio + WEIGHT_DECAY * base)


def selection(count, far, depth, size, x, width, target):
    column = lax.broadcasted_iota(jnp.int32, (count * far * depth, 1), 0)
    place = lax.rem(column, depth)
    block = lax.div(column, depth)
    goal = target(lax.div(block, far), place)
    goal = jnp.where((place < size) & (lax.rem(block, far) == x), goal, -1)
    columns = lax.broadcasted_iota(jnp.int32, (count * far * depth, width), 1)
    return low((goal == columns).astype(F32))


def place_kernel(
    rule, far, main_rows, depth, place, factor, own, across, others, lateral, condense, mixing,
    restore, lateral_out, condense_out, mixing_out, restore_out, frames,
):
    for k, part in enumerate((own[...], others[0], across[...], others[1])):
        frames[jnp.bitwise_xor(place[0], k)] = part
    half_one, half_two = [
        [frames.at[2 * target + c] for target in range(far)] for c in range(2)
    ]
    halves = (half_one, half_two)
    batch_count, out_rows, lanes_all = own.shape
    edge = far * main_rows
    stop = far * depth
    scale = factor[...]

    def put(out, base, spot, values):
        lanes = slice(spot, spot + values.shape[1])
        out[:, lanes] = rule(base[:, lanes], values.astype(F32), 1.0, scale)
        return spot + values.shape[1]

    devices = 2 * far
    rest_depth = depth - main_rows
    for target, out, base, main_taps in ((0, condense_out, condense, 2), (1, mixing_out, mixing, 8)):
        share = batch_count // main_taps
        spot = 0
        for tap in range(main_taps):
            for device in range(devices):
                lanes = slice(device // 2 * main_rows, (device // 2 + 1) * main_rows)
                for k in range(tap * share, (tap + 1) * share):
                    spot = put(out, base, spot, halves[device % 2][target][k, :, lanes])
        size = (out.shape[1] - spot) // (batch_count * devices)
        rests = [
            jnp.concatenate([half[target][k, :, edge:stop] for k in range(batch_count)], axis=1)
            for half in halves
        ]
        for x in range(far):
            chosen = selection(
                batch_count, far, rest_depth, size, x, batch_count * size,
                lambda k, r: k * size + r,
            )
            for rest in rests:
                spot = put(out, base, spot, nn(rest, chosen))
    side_depth = (lanes_all - stop) // far
    side_size = lateral.shape[1] // (batch_count * devices)
    channels = CF // devices
    sides = [
        jnp.concatenate([half[1][k, :, stop:] for k in range(batch_count)], axis=1)
        for half in halves
    ]
    for x in range(far):
        total = None
        for c, side in enumerate(sides):

            def goal(k, r):
                row = k * side_size + r
                return lax.div(row, channels) * 2 * channels + c * channels + lax.rem(row, channels)

            chosen = selection(
                batch_count, far, side_depth, side_size, x, 10 * channels, goal
            )
            term = nn(side, chosen)
            total = term if total is None else total + term
        for tap in range(5):
            put(
                lateral_out, lateral, tap * CF + 2 * x * channels,
                total[:, tap * 2 * channels : (tap + 1) * 2 * channels],
            )
    width = lanes_all - stop
    ratio = math.sqrt(max(1.0, restore.shape[0] * batch_count / restore.shape[1]))
    for c, half in enumerate(halves):
        for k in range(batch_count * out_rows // width):
            for h in range(far):
                start = (2 * h + c) * out_rows
                rows = slice(start, start + out_rows)
                lanes = slice(k * width, (k + 1) * width)
                values = half[0][k * width // out_rows + h, :, stop:].astype(F32)
                restore_out[rows, lanes] = rule(restore[rows, lanes], values, ratio, scale)


def adam(weight, moment, square, grad, rate, decay):
    moment = ADAM_ONE * moment + (1.0 - ADAM_ONE) * grad
    square = ADAM_TWO * square + (1.0 - ADAM_TWO) * grad * grad
    fixed_one = 1.0 - ADAM_ONE**STEP
    fixed_two = 1.0 - ADAM_TWO**STEP
    weight = weight - rate * (
        moment / fixed_one / (jnp.sqrt(square / fixed_two) + ADAM_EPS) + decay * weight
    )
    return (weight, moment, square)


def per_device(
    video,
    video_ids,
    crop_scales,
    labels,
    valid_clips,
    stem_weight,
    lateral_weight,
    condense,
    mixing,
    restore,
    squeeze,
    blending,
    recover,
    head_weight,
    stem_velocity,
    lateral_velocity,
    condense_velocity,
    mixing_velocity,
    restore_velocity,
    squeeze_velocity,
    blending_velocity,
    recover_velocity,
    head_moment,
    head_square,
    affine,
    affine_moment,
    affine_square,
):
    tm_count = lax.axis_size("tm")
    batch_count = lax.axis_size("batch")
    devices = tm_count * batch_count
    far = tm_count // 2
    tm_place = lax.axis_index("tm")
    batch_place = lax.axis_index("batch")
    core = tm_place % 2
    both = ("tm", "batch")

    clips, frames, height = video.shape[0:3]
    spots = height * height
    rows = spots * clips

    def quarter(block):
        part = block.shape[0] // tm_count
        return lax.dynamic_slice_in_dim(block, tm_place * part, part, axis=0)

    def gather(block):
        return lax.all_gather(quarter(block), ("batch", "tm"), axis=0, tiled=True)

    def by_place(items, place):
        whole = jnp.zeros((len(items),) + items[0].shape, items[0].dtype)
        for k, item in enumerate(items):
            whole = lax.dynamic_update_index_in_dim(whole, item, place ^ k, 0)
        return whole

    def over_tm(block):
        held = by_place(
            [block] + [swap(block, "tm", 2 * k) for k in range(1, far)], tm_place // 2
        )
        held = by_place([held, swap(held, "tm", 1)], core)
        return jnp.swapaxes(held, 0, 1).reshape((tm_count,) + block.shape)

    def gather_steps(block):
        held = spread_all(block, ("batch",))
        held = held.reshape(batch_count, -1, block.shape[1])
        held = jnp.swapaxes(over_tm(held), 0, 1)
        return held.reshape(-1, block.shape[1])

    out_rows = condense.shape[0]
    small_rows = squeeze.shape[0]
    weights_low = jnp.concatenate(
        [mixing, lateral_weight, condense]
        + [restore[k * out_rows : (k + 1) * out_rows] for k in range(4)],
        axis=1,
    )
    weights_low = quarter(weights_low).astype(BF16)
    stem_low = quarter(stem_weight).astype(BF16)
    weights_low, stem_low, video = lax.optimization_barrier((weights_low, stem_low, video))
    weights_full = lax.all_gather(weights_low, ("batch", "tm"), axis=0, tiled=True)
    stem_full = gather_steps(stem_low)
    small = jnp.concatenate(
        [squeeze, blending, recover.reshape(small_rows, -1)], axis=1
    ).astype(BF16)
    small_full = spread_all(small, ("batch",)).reshape(CFM, -1)
    squeeze_full = small_full[:, 0 : 3 * CF]
    blending_full = small_full[:, 3 * CF : 3 * CF + 9 * CFM]
    recover_full = small_full[:, 3 * CF + 9 * CFM :].reshape(CF, CFM)
    head_full = gather(head_weight.astype(BF16))

    own_video = jnp.transpose(video, (1, 2, 3, 0, 4)).reshape(frames, rows, -1)
    before = shift(
        jnp.concatenate([own_video[0:1], own_video[frames - 2 :]], axis=0), "tm", 1
    )
    after = shift(own_video[0:1], "tm", -1)
    slow_video = jnp.concatenate([before[0:1], own_video[0:1], after], axis=0)
    fast_video = jnp.concatenate([before[1:], own_video, after], axis=0)

    side = (height - crop_scales).astype(F32)
    places = jnp.arange(height).astype(F32)
    inside = (places[:, None] < side[None, :]).astype(F32)
    mask = (inside[:, None, :] * inside[None, :, :]).reshape(rows, 1)
    area = (side * side)[:, None]
    gains, shifts, class_bias = split_affine(affine)
    par = [jnp.stack([gain, shift]) for gain, shift in zip(gains, shifts)]
    valid = valid_clips.astype(F32)[:, None]
    blend_taps = jnp.transpose(blending_full.reshape(CFM, 9, CFM), (1, 2, 0))
    narrow = ((devices, 8, 256), F32)
    narrow_low = ((devices, 8, 256), BF16)
    total_narrow = ((8, 256), F32)
    wide = ((8, 640), F32)

    def exchange(copies):
        return lax.all_to_all(copies, both, 0, 0, tiled=True)

    def exchange_wide(block):
        return spread_all(block, both).reshape((devices,) + block.shape)

    slow_shape = (rows, CSM)
    fast_shape = (frames, rows, CFM)
    slow_wide = (rows, CS)
    fast_wide = (frames, rows, CF)
    first_shape = ((CSM, 5 * CF + 3 * CS), BF16)
    mixing_shape = ((CSM, 9 * CSM), BF16)
    restore_shape = ((CS, CSM), BF16)
    pad_shape = ((height + 2, height + 2, clips, CSM), F32)
    fast_pad = ((height + 2, height + 2, clips, CFM), F32)

    pieces = batch_count * far
    main_rows = 2048 // pieces
    mixing_rows = 9 * CSM // 2 // pieces
    condense_rows = 3 * CS // 2 // pieces
    far_place = tm_place // 2
    depth_one = condense_rows
    depth_two = CS // 2 // pieces

    def share_of(item, taps, place):
        width = item.shape[1] // taps
        size = width // tm_count
        return jnp.concatenate(
            [
                lax.dynamic_slice_in_dim(item, tap * width + place * size, size, axis=1)
                for tap in range(taps)
            ],
            axis=1,
        ).astype(BF16)

    def sent_columns(item, taps, parts):
        held = []
        start = 0
        shares = [share_of(item, taps, 2 * k + core) for k in range(far)]
        for size, depth in parts:
            for share in shares:
                block = share[:, start : start + size * batch_count]
                block = block.reshape(out_rows, batch_count, size)
                held.append(jnp.pad(block, ((0, 0), (0, 0), (0, depth - size))))
            start = start + size * batch_count
        return jnp.transpose(jnp.concatenate(held, axis=-1), (1, 0, 2))

    lateral_rows = 5 * CF // tm_count // batch_count
    rest_depth = depth_one - main_rows
    speed_send = jnp.concatenate(
        [
            jnp.where(
                far_place == 0,
                sent_columns(
                    condense_velocity, 3, ((main_rows, main_rows), (rest_depth, rest_depth))
                ),
                sent_columns(
                    mixing_velocity,
                    9,
                    ((main_rows, main_rows), (mixing_rows - main_rows, rest_depth)),
                ),
            ),
            sent_columns(lateral_velocity, 5, ((lateral_rows, depth_two),)),
        ],
        axis=-1,
    )
    small_speed = jnp.concatenate(
        [squeeze_velocity, blending_velocity, recover_velocity.reshape(small_rows, -1)], axis=1
    )
    small_speed = small_speed.astype(BF16).reshape(-1, speed_send.shape[-1])
    small_speed = jnp.broadcast_to(small_speed[None], (batch_count,) + small_speed.shape)
    speed_send = jnp.concatenate([speed_send, small_speed], axis=1)
    speed_send, small_full = lax.optimization_barrier((speed_send, small_full))
    speed = lax.all_to_all(speed_send, "batch", 0, 0, tiled=True)

    near = tm_count == 4 and batch_count == 8
    place_cell = tm_place.astype(jnp.int32).reshape(1)
    quarter_shape = (rows, CS // tm_count)
    slow_pre, fast_pre, slow_low, fast_low, *shares = call(
        functools.partial(stem_kernel, near),
        [
            (slow_wide, F32),
            (fast_wide, F32),
            ((3, rows, CS), BF16),
            ((frames + 3, rows, CF), BF16),
        ]
        + (
            [(quarter_shape, BF16)] * 4 + [((5, rows, 128), BF16)] * 2
            if near
            else [((tm_count,) + quarter_shape, BF16)]
        ),
        [place_cell, slow_video, fast_video, stem_full, mask]
        + ([own_video[0]] + [swap(own_video[0], "tm", k) for k in range(1, 4)] if near else []),
        scalars=(0,),
    )
    def in_turn(items, margin=0):
        whole = jnp.zeros((len(items) + 2 * margin,) + items[0].shape, items[0].dtype)
        for k, item in enumerate(items):
            whole = lax.dynamic_update_index_in_dim(whole, item, (tm_place ^ k) + margin, 0)
        return whole

    def share_out(parts, margin=0):
        items = [pick(parts, 0, tm_place)]
        items += [swap(pick(parts, 0, tm_place ^ k), "tm", k) for k in range(1, tm_count)]
        return in_turn(items, margin)

    def every(block, margin=0):
        even = [block] + [swap(block, "tm", 2 * k) for k in range(1, far)]
        odd = swap(jnp.stack(even), "tm", 1)
        items = [item for k in range(far) for item in (even[k], odd[k])]
        return in_turn(items, margin)

    def by_share(block, outer):
        parts = block.reshape(block.shape[0], outer, tm_count, -1)
        return jnp.moveaxis(parts, 2, 0).reshape(tm_count, block.shape[0], -1)

    def swaps(parts):
        return [parts[0]] + [swap(parts[k], "tm", k) for k in range(1, tm_count)]

    def pairs_of(own, given):
        across = swap(given, "tm", 2)
        return [own, across, swap(jnp.stack([own, across]), "tm", 1)]

    if near:
        slow_shares = shares[0:4]
        side_shares = pairs_of(shares[4], shares[5])
    else:
        sides = jnp.transpose(fast_low[0:5], (1, 0, 2)).reshape(rows, 5 * CF)
        slow_shares = share_out(shares[0], 1)
        side_shares = share_out(by_share(sides, 5))
    slow_low, speed = lax.optimization_barrier((slow_low, speed))
    h1, h4, sent = call(
        first_kernel,
        [(slow_shape, F32), (fast_shape, F32), narrow],
        [slow_low, fast_low, weights_full, squeeze_full, mask, valid],
        [total_narrow, first_shape],
        far=(2,),
        copies=4,
    )
    act_width = CSM // tm_count
    act_shapes = [((rows, 128), BF16)] * 4 if near else [(slow_shape, BF16)]
    h2, h5, total1, sent, *acts = call(
        functools.partial(second_kernel, near),
        [(slow_shape, F32), (fast_shape, F32), total_narrow, narrow] + act_shapes,
        [place_cell, h1, h4, exchange(sent), par[0], par[3], mask, weights_full, blend_taps],
        [pad_shape, fast_pad, total_narrow, mixing_shape],
        far=(7,),
        copies=9,
        scalars=(0,),
    )
    acts = swaps(acts) if near else share_out(by_share(acts[0], 1))
    a2, a5, h3, h6, total2, sent = call(
        third_kernel,
        [
            (slow_shape, BF16),
            (fast_shape, BF16),
            (slow_wide, F32),
            (fast_wide, F32),
            total_narrow,
            wide,
        ],
        [h2, h5, total1, exchange(sent), par[1], par[4], mask, weights_full, recover_full],
        [restore_shape],
        far=(7,),
        copies=4 * batch_count,
    )
    a2_every = pairs_of(a2, a2) if near else every(a2)
    if near:
        h3, side_shares[1] = lax.optimization_barrier((h3, side_shares[1]))
    else:
        h3, slow_shares, side_shares = lax.optimization_barrier((h3, slow_shares, side_shares))
    pool, total3 = call(
        pool_kernel,
        [((clips, CS + CF), F32), wide],
        [h3, h6, slow_pre, fast_pre, total1, exchange_wide(sent), par[2], par[5], mask],
    )
    if near:
        pools = jnp.stack([pool] + [swap(pool, "tm", k) for k in range(1, tm_count)])
    else:
        pools = spread_all(pool, ("tm",)).reshape(tm_count, clips, CS + CF)
    feature_low, logit_low, d3, d6, sent = call(
        head_kernel,
        [((clips, CS + CF), BF16), ((clips, CLS), BF16), (slow_wide, F32), (fast_wide, F32), wide],
        [
            pools,
            head_full,
            class_bias[None],
            video_ids[:, None],
            video_ids[None],
            labels[:, None],
            valid,
            area,
            h3,
            h6,
            slow_pre,
            fast_pre,
            total1,
            total3,
            par[2],
            par[5],
            mask,
        ],
    )
    d3, acts, a2_every, side_shares = lax.optimization_barrier((d3, acts, a2_every, side_shares))
    u6, e2, e5, back3, sent, *u3 = call(
        functools.partial(third_back_kernel, near),
        [
            (fast_wide, BF16),
            (slow_shape, F32),
            (fast_shape, F32),
            wide,
            narrow_low,
        ]
        + ([(quarter_shape, BF16)] * 4 if near else [(slow_wide, BF16)]),
        [
            place_cell,
            d3,
            d6,
            h3,
            h6,
            h2,
            h5,
            total1,
            total3,
            total2,
            exchange_wide(low(sent)),
            par[2],
            par[5],
            par[1],
            par[4],
            mask,
            weights_full,
            recover_full,
        ],
        [total_narrow, restore_shape],
        far=(16,),
        copies=4 * batch_count,
        scalars=(0,),
    )
    if near:
        (restore_grad,) = call(
            early_kernel,
            [((batch_count, CS // tm_count // batch_count, CSM), BF16)],
            [*swaps(u3), *a2_every],
        )
    else:
        u3_shares = share_out(by_share(u3[0], batch_count))
        restore_grad = low(dot(u3_shares, a2_every, ((0, 1), (0, 1))))
    recover_grad = over_rows(a5.reshape(frames * rows, CFM), u6.reshape(frames * rows, CF))

    u2, u5, e1, e4, blend_grad, back2, sent = call(
        second_back_kernel,
        [
            (slow_shape, BF16),
            (fast_shape, BF16),
            (slow_shape, F32),
            (fast_shape, F32),
            ((9, CFM, CFM), F32),
            total_narrow,
            narrow_low,
        ],
        [
            e2,
            e5,
            h2,
            h5,
            h1,
            h4,
            total2,
            total1,
            exchange(sent),
            par[1],
            par[4],
            par[0],
            par[3],
            mask,
            weights_full,
            blend_taps,
        ],
        [pad_shape, fast_pad, fast_pad, total_narrow, mixing_shape],
        far=(14,),
        copies=9,
    )
    blending_grad = jnp.transpose(blend_grad, (1, 0, 2)).reshape(CFM, 9 * CFM)

    def by_batch(parts):
        return jnp.concatenate(
            [part.reshape(batch_count, -1, part.shape[-1]) for part in parts], axis=1
        )

    def over_batch(view):
        got = lax.all_to_all(view, "batch", 0, 0, tiled=True)
        return jnp.sum(got.reshape(view.shape).astype(F32), axis=0)

    if near:
        (early,) = call(
            mixing_kernel,
            [((batch_count, 208, CSM), BF16)],
            [*acts, *pairs_of(u2, u2), restore_grad],
            [((tm_count, height + 2, height + 2, clips, act_width), F32)],
        )
    else:
        (mixing_grad,) = call(
            mixing_grad_kernel,
            [((9, act_width, CSM), BF16)],
            [acts, every(u2)],
            [((tm_count, height + 2, height + 2, clips, act_width), F32)],
        )
        mixing_grad = mixing_grad.reshape(9 * act_width, CSM)
        main_edge = 8 * act_width
        early = by_batch([mixing_grad[0:main_edge], mixing_grad[main_edge:], restore_grad])
    early, e1 = lax.optimization_barrier((early, e1))
    early = over_batch(early)

    u1, u4, back1 = call(
        first_back_kernel,
        [(slow_shape, BF16), (fast_shape, BF16), total_narrow],
        [e1, e4, h1, h4, total1, exchange(sent), par[0], par[3], mask],
    )
    if near:
        u1_parts = pairs_of(u1, u1)
        u1_held = u1_parts
    else:
        u1_held = every(u1, 1)
    squeeze_grad = jnp.concatenate(
        [dot(u4, fast_low[1 + k : 1 + k + frames], ((0, 1), (0, 1))) for k in range(3)], axis=1
    )
    slow_up, fast_up = call(
        functools.partial(stem_back_kernel, near),
        [(slow_wide, BF16), (fast_wide, BF16)],
        [
            place_cell,
            *(u1_held if near else [u1_held]),
            u4,
            shift(u4[frames - 1], "tm", 1),
            shift(u4[0], "tm", -1),
            weights_full,
            squeeze_full,
            d3,
            d6,
            slow_pre,
            fast_pre,
            mask,
        ],
        [first_shape, ((6,) + slow_shape, BF16)],
        far=(7 if near else 5,),
        copies=4,
        scalars=(0,),
    )
    slow_up, fast_up, u1_held = lax.optimization_barrier((slow_up, fast_up, u1_held))
    if near:
        (late,) = call(
            late_kernel,
            [((batch_count, 240, CSM), BF16)],
            [place_cell, *slow_shares, *side_shares, *u1_held],
            [((6,) + quarter_shape, BF16), ((128, CSM), F32), ((320, CSM), F32)],
            scalars=(0,),
        )
    else:
        u1_inner = u1_held[1 : tm_count + 1]
        cells = ((0, 1), (0, 1))
        condense_grad = [
            low(dot(slow_shares[k : k + tm_count], u1_inner, cells)) for k in range(3)
        ]
        lateral_grad = low(dot(side_shares, u1_inner, cells))
        late = by_batch(
            [jnp.concatenate(condense_grad[0:2]), condense_grad[2], lateral_grad]
        )
    late, early = lax.optimization_barrier((late, early))
    late = over_batch(late)
    clip_count = total1[7, 0] / tm_count
    loss_total = (back3[4, 512] + back3[5, 512] + back3[6, 512]) / tm_count
    slow_back3, fast_back3 = get_wide(back3)
    slow_back2, fast_back2 = get_narrow(back2)
    slow_back1, fast_back1 = get_narrow(back1)
    (b1, g1), (b2, g2), (b3, g3) = [
        [item[0] for item in pair] for pair in (slow_back1, slow_back2, slow_back3)
    ]
    (b4, g4), (b5, g5), (b6, g6) = [
        [item[0] for item in pair] for pair in (fast_back1, fast_back2, fast_back3)
    ]

    main_rows = 2048 // pieces
    mixing_rows = 9 * CSM // 2 // pieces
    condense_rows = 3 * CS // 2 // pieces
    tm_all = bits("tm", 0)
    columns_wide = stem_weight.shape[-1]

    def blocks(item):
        item = jnp.pad(item, ((0, 0), (0, -item.shape[1] % columns_wide)))
        item = item.reshape(batch_count, small_rows, -1, columns_wide)
        return jnp.swapaxes(item, 1, 2)

    small_view = [blocks(item) for item in (squeeze_grad, blending_grad, recover_grad)]
    small_view = jnp.concatenate(small_view, axis=1)
    small_blocks = small_view.shape[1]
    head_rows = head_weight.shape[0]
    feature_parts = jnp.transpose(feature_low.reshape(clips, batch_count, head_rows), (1, 0, 2))
    logit_parts = jnp.broadcast_to(logit_low.reshape(1, -1), (batch_count, clips * CLS))
    riders = jnp.concatenate([feature_parts.reshape(batch_count, -1), logit_parts], axis=1)
    riders = jnp.pad(riders, ((0, 0), (0, -riders.shape[1] % columns_wide)))
    riders = riders.reshape(batch_count, -1, columns_wide)
    if near:
        small_tm = small_view.reshape(batch_count, tm_count, -1, columns_wide)
        small_part = small_tm.shape[2]
        small_tm = jnp.pad(jnp.swapaxes(small_tm, 0, 1), ((0, 0), (0, 0), (0, 6), (0, 0)))
        share_shape = (batch_count, stem_weight.shape[0] // tm_count + 24, columns_wide)
        stem_shares = call(
            stem_grad_kernel,
            [(share_shape, BF16)] * 4,
            [place_cell, slow_up, fast_up, own_video, small_tm],
            [((CS + CF, columns_wide), F32)],
            scalars=(0,),
        )
        stem_shares = swaps(stem_shares)
        stem_shares = low(sum(share.astype(F32) for share in stem_shares))
        riders = jnp.concatenate([stem_shares, riders], axis=1)
        got = [pick(riders, 0, batch_place)] + [
            swap(pick(riders, 0, batch_place ^ k), "batch", k) for k in range(1, batch_count)
        ]
        shards_sum = sum(item[0 : share_shape[1]].astype(F32) for item in got)
        stem_part = share_shape[1] - 24
        stem_shard, small_shard = shards_sum[0:stem_part], shards_sum[stem_part:]
        riders = jnp.stack([item[share_shape[1] :] for item in got])
        riders = riders.reshape(batch_count, -1)
    else:
        stem_grad = jnp.concatenate(
            [over_rows(slow_up, own_video[0]), dot(fast_up, own_video, ((0, 1), (0, 1)))], axis=0
        )
        stem_view = stem_grad.reshape((batch_count,) + (2,) * len(tm_all) + (-1, stem_grad.shape[-1]))
        small_view = small_view.reshape(-1, columns_wide)
        live = list(tm_all)
        for axis, bit in tm_all[::-1]:
            dim = 1 + live.index((axis, bit))
            flag = (tm_place >> bit) & 1
            keep, give = pick(stem_view, dim, flag), pick(stem_view, dim, 1 - flag)
            flat_give = give.reshape(-1, columns_wide)
            count = flat_give.shape[0]
            sent = jnp.concatenate([flat_give, small_view]).astype(BF16)
            sent = lax.optimization_barrier(sent)
            got = swap(sent, axis, 1 << bit)
            stem_view = keep + got[0:count].astype(F32).reshape(keep.shape)
            small_view = sent[count:].astype(F32) + got[count:].astype(F32)
            live.remove((axis, bit))
        small_view = small_view.reshape(batch_count, -1, columns_wide)
        stem_part = stem_view.shape[1]
        late, riders = lax.optimization_barrier((late, riders))
        riders = jnp.concatenate([stem_view.astype(BF16), small_view.astype(BF16), riders], axis=1)
        got = lax.all_to_all(riders, "batch", 0, 0, tiled=True).reshape(batch_count, -1, columns_wide)
        both_parts = stem_part + small_view.shape[1]
        shards_sum = jnp.sum(got[:, 0:both_parts].astype(F32), axis=0)
        stem_shard, small_shard = shards_sum[0:stem_part], shards_sum[stem_part:]
        riders = got[:, both_parts:].reshape(batch_count, -1)
    feature_size = clips * head_rows
    feature_all = riders[:, 0:feature_size].reshape(batch_count * clips, head_rows)
    logit_all = riders[:, feature_size : feature_size + clips * CLS]
    logit_all = logit_all.reshape(batch_count * clips, CLS)
    mixing_shard, restore_shard = early[0:mixing_rows], early[mixing_rows:]
    condense_shard = late[0:condense_rows]
    lateral_shard = late[condense_rows : condense_rows + lateral_rows]
    head_grad = over_rows(feature_all, logit_all)
    class_grad = jnp.sum(logit_all.astype(F32), axis=0)
    affine_grad = jnp.concatenate([g1, g2, g3, g4, g5, g6, b1, b2, b3, b4, b5, b6, class_grad])

    small_speed = jnp.concatenate(
        [squeeze_velocity, blending_velocity, recover_velocity.reshape(small_rows, -1)], axis=1
    )
    small_speed = spread_all(small_speed.astype(BF16), ("batch",)).reshape(CFM, -1)

    leader = (tm_place == 0).astype(F32)
    squares = sum(jnp.sum(item * item) for item in (late, early, stem_shard))
    small_share = 1.0 if near else leader
    squares = squares + small_share * jnp.sum(small_shard * small_shard)
    squares = squares + leader * jnp.sum(head_grad * head_grad)
    first_device = leader * (batch_place == 0).astype(F32)
    squares = squares + first_device * jnp.sum(affine_grad * affine_grad)
    (total_squares,) = all_sum([squares], both)
    grad_norm = jnp.sqrt(total_squares) / clip_count
    factor = jnp.minimum(1.0, CLIP_AT / grad_norm) / clip_count

    small_speed = speed[:, out_rows:].reshape(CFM, -1)
    stem_rows = stem_weight.shape[0]
    if near:
        stem_own = over_tm(low(stem_shard)).reshape(stem_rows, -1)
    else:
        stem_own = over_tm(low(stem_shard)).reshape(stem_rows, -1)

    def small_parts(small_whole):
        small_whole = small_whole.reshape(batch_count, small_blocks, small_rows, columns_wide)
        small_whole = jnp.swapaxes(small_whole, 1, 2).reshape(CFM, -1)
        small_grads = unpack(small_whole[:, 0 : 3 * CF + 9 * CFM + CF])
        speeds = unpack(small_speed)
        speeds = (speeds[0], speeds[1], speeds[2].reshape(CF, CFM).T)
        items = [
            low(MUON_KEEP * held.astype(F32) + grad.astype(F32) * factor)
            for held, grad in zip(speeds, small_grads)
        ]
        return small_grads, items

    def unpack(values):
        first = values[:, 0 : 3 * CF]
        second = values[:, 3 * CF : 3 * CF + 9 * CFM]
        return (first, second, values[:, 3 * CF + 9 * CFM :])

    def ratio_of(base):
        return math.sqrt(max(1.0, base.shape[0] * batch_count / base.shape[1]))

    def own(values, part):
        return lax.dynamic_slice_in_dim(values, batch_place * part, part, axis=0)

    def direct_orthos(stem_moved, shapes, items):
        tall_part = recover.shape[0]
        results = (
            rows_by_columns(stem_moved, shapes[0]),
            rows_by_columns(own(shapes[1], small_rows), items[0]),
            rows_by_columns(own(shapes[2], small_rows), items[1]),
            rows_by_columns(own(items[2].T, tall_part), shapes[3]),
        )
        return [low(result) for result in results]

    far_place = tm_place // 2
    factor_cell = factor.reshape(1, 1)
    bases = {
        carry: (lateral_velocity, condense_velocity, mixing_velocity, restore_velocity),
        renew: (lateral_weight, condense, mixing, restore),
    }

    def deep(item, depth):
        return jnp.pad(item, ((0, depth - item.shape[0]), (0, 0)))

    if near:
        pair_one = low(jnp.concatenate([condense_shard, restore_shard]))
        pair_two = low(
            jnp.concatenate([deep(mixing_shard, depth_one), deep(lateral_shard, depth_two)])
        )
        pair_own = jnp.where(far_place == 0, pair_one, pair_two)
        pair_got = swap(jnp.where(far_place == 0, pair_two, pair_one), "tm", 2)
        restore_speed = pick(restore_velocity.reshape(far, 2, depth_two, CSM), 1, core)
        restore_speed = low(restore_speed.reshape(far * depth_two, CSM))
        wide_shape = ((batch_count, out_rows, CSM), BF16)
        tall_shape = ((batch_count, out_rows, far * depth_two), BF16)
        gram_shape = ((CSM, CSM), BF16)
        moved_one, moved_two, stem_moved, keep, give, stem_gram, grad_wide, grad_tall = call(
            gram_kernel,
            [
                ((far * depth_one, CSM), BF16),
                ((far * depth_two, CSM), BF16),
                (stem_own.shape, BF16),
                ((320, CSM), BF16),
                ((320, CSM), BF16),
                ((batch_count, 16, CSM), BF16),
                wide_shape,
                tall_shape,
            ],
            [
                place_cell,
                factor_cell,
                speed,
                restore_speed,
                pair_own,
                pair_got,
                stem_velocity,
                stem_own,
            ],
            [((CSM, CSM), F32)],
            scalars=(0,),
        )
        gram = low(keep.astype(F32) + swap(give, "tm", 1).astype(F32))
        riders = low(small_shard)
        riders = jnp.concatenate(
            [
                jnp.pad(riders[0:16], ((0, 0), (0, 64))),
                jnp.pad(riders[16:24], ((0, 8), (0, 64))),
            ],
            axis=1,
        )
        riders = jnp.broadcast_to(riders[None], (batch_count,) + riders.shape)
        got = lax.all_to_all(
            jnp.concatenate([gram.reshape(batch_count, 40, CSM), stem_gram, riders], axis=1),
            "batch", 0, 0, tiled=True,
        )
        summed = low(jnp.sum(got[:, 0:56].astype(F32), axis=0))
        summed = jnp.pad(summed, ((0, 8), (0, 0)))
        small_whole = jnp.concatenate([got[:, 56:72, 0:192], got[:, 56:64, 256:448]], axis=1)
        small_whole = over_tm(small_whole)[:, :, 0:small_part]
        small_grads, items = small_parts(jnp.swapaxes(small_whole, 0, 1))
        whole = lax.all_to_all(
            jnp.concatenate(
                [grad_wide, jnp.broadcast_to(summed[None], (batch_count,) + summed.shape)], axis=1
            ),
            "batch", 0, 0, tiled=True,
        )
        shaped, *shapes = call(
            block_shape_kernel,
            [gram_shape, ((192, 192), BF16)] + [((CFM, CFM), BF16)] * 3,
            [whole] + [rows_by_rows(item, item) for item in items],
            [((CSM, CSM), F32), ((192, 192), F32), ((320, CSM), F32)],
            micros=10,
        )

        def put_rows(rule, held, tall):
            edge = far * depth_one
            second = jnp.where(far_place == 0, tall, held[..., edge:])
            held = jnp.concatenate([held[..., 0:edge], second], axis=-1)
            kernel = functools.partial(place_kernel, rule, far, main_rows, depth_one)
            return call(
                kernel,
                [(base.shape, F32) for base in bases[rule]],
                [place_cell, factor_cell, *pairs_of(held, held), *bases[rule]],
                [((tm_count,) + wide_shape[0], BF16)],
                scalars=(0,),
            )

        grads = put_rows(carry, whole[:, 0:64], grad_tall)
        ortho_wide, ortho_tall = call(
            ortho_kernel,
            [wide_shape, tall_shape],
            [place_cell, shaped, swap(shaped, "tm", 1), moved_one, moved_two],
            scalars=(0,),
        )
        ortho_wide = lax.all_to_all(ortho_wide, "batch", 0, 0, tiled=True)
        direct = direct_orthos(stem_moved, shapes, items)
        tied = lax.optimization_barrier((ortho_wide, *grads, *direct))
        ortho_wide, grads, direct = tied[0], tied[1:5], tied[5:]
        orthos = put_rows(renew, ortho_wide, ortho_tall)
    else:
        pair_one = jnp.concatenate([condense_shard, deep(restore_shard, depth_two)])
        pair_two = jnp.concatenate([deep(mixing_shard, depth_one), deep(lateral_shard, depth_two)])
        pairs = jnp.stack([pair_one, pair_two] + [jnp.zeros_like(pair_one)] * (far - 2)).astype(BF16)
        grads_held = by_place(
            [pick(pairs, 0, far_place)]
            + [swap(pick(pairs, 0, far_place ^ k), "tm", 2 * k) for k in range(1, far)],
            far_place,
        )

        def cut(held):
            one = jnp.concatenate(
                [
                    held[:, 0:main_rows].reshape(far * main_rows, CSM),
                    held[:, main_rows:depth_one].reshape(far * (depth_one - main_rows), CSM),
                ]
            )
            return one, held[:, depth_one:].reshape(far * depth_two, CSM)

        speed = speed[:, 0:out_rows].reshape(CSM, -1)
        speed_one = speed[:, 0 : far * depth_one].T
        restore_speed = pick(restore_velocity.reshape(far, 2, depth_two, CSM), 1, core)
        restore_speed = restore_speed.reshape(far * depth_two, CSM)
        speed_two = jnp.where(
            far_place == 0, restore_speed.astype(BF16), speed[:, far * depth_one :].T
        )
        grad_one, grad_two = cut(grads_held)
        used = far_place < 2

        def step_of(speed_part, grad_part):
            moved = MUON_KEEP * speed_part.astype(F32) + grad_part.astype(F32) * factor
            return jnp.where(used, moved, 0.0).astype(BF16)

        stem_moved = low(MUON_KEEP * stem_velocity + stem_own.astype(F32) * factor)

        moved_one = step_of(speed_one, grad_one)
        moved_two = step_of(speed_two, grad_two)
        gram_one = over_rows(moved_one, moved_one)
        gram_two = over_rows(moved_two, moved_two)
        gram = jnp.where(core == 0, gram_one, gram_two) + swap(
            jnp.where(core == 0, gram_two, gram_one), "tm", 1
        )
        stem_gram = over_rows(stem_moved, stem_moved)

        def flat_rows(item):
            return item.reshape(batch_count, -1).astype(GRAM)

        parts = [flat_rows(gram), flat_rows(stem_gram)]
        sizes = [part.shape[1] for part in parts]
        riders = jnp.broadcast_to(small_shard.reshape(1, -1).astype(GRAM), (batch_count, small_shard.size))

        def packed(items):
            whole = jnp.concatenate(items, axis=1)
            whole = jnp.pad(whole, ((0, 0), (0, -whole.shape[1] % 2048)))
            return whole.reshape(batch_count, -1, 256)

        def exchanged(items):
            whole = lax.all_to_all(packed(items), "batch", 0, 0, tiled=True)
            return whole.reshape(batch_count, -1)

        got = exchanged(parts + [riders])
        summed = jnp.sum(got[:, 0 : sum(sizes)].astype(F32), axis=0, keepdims=True).astype(GRAM)
        small_whole = got[:, sum(sizes) : sum(sizes) + small_shard.size]
        small_grads, items = small_parts(small_whole)
        grad_one, grad_two, summed = lax.optimization_barrier((grad_one, grad_two, summed))
        whole = exchanged([jnp.broadcast_to(summed, (batch_count, summed.shape[1]))]).astype(F32)
        gram = whole[:, 0 : sizes[0]].reshape(CSM, CSM)
        stem_gram = whole[:, sizes[0] : sum(sizes)].reshape(stem_gram.shape)

        shaped, *shapes = shape_of([gram, stem_gram] + [rows_by_rows(item, item) for item in items])
        shaped = low(shaped)
        shapes = [low(shape) for shape in shapes]
        shaped_other = swap(shaped, "tm", 1)
        shape_one = jnp.where(core == 0, shaped, shaped_other)
        shape_two = jnp.where(core == 0, shaped_other, shaped)

        def spread_rows(rule, bases, wide_one, wide_two, tall_two):
            lateral_base, condense_base, mixing_base, restore_base = bases
            wide_both = jnp.concatenate([wide_one, wide_two], axis=1)
            wide_both = wide_both.reshape(batch_count, out_rows, -1)
            held = lax.all_to_all(wide_both, "batch", 0, 0, tiled=True)
            width = far * depth_two
            tall = jnp.concatenate(
                [tall_two[:, k * width : (k + 1) * width] for k in range(CSM // width)], axis=0
            ).reshape(batch_count, out_rows, width)
            second = jnp.where(far_place == 0, tall, held[..., far * depth_one :])
            held = jnp.concatenate([held[..., 0 : far * depth_one], second], axis=-1)
            held = by_place(
                [held] + [swap(held, "tm", 2 * k) for k in range(1, far)], far_place
            )[0:2]
            other = swap(held, "tm", 1)
            held = (jnp.where(core == 0, held, other), jnp.where(core == 0, other, held))

            edge = far * main_rows
            stop = far * depth_one
            def taps_of(place, base, main_taps, size):
                block = jnp.stack([half[place] for half in held])
                main = block[..., 0:edge].reshape(
                    2, main_taps, batch_count // main_taps, out_rows, far, main_rows
                )
                main = jnp.transpose(main, (3, 1, 4, 0, 2, 5)).reshape(out_rows, -1)
                rest = block[..., edge:stop].reshape(
                    2, batch_count, out_rows, far, depth_one - main_rows
                )[..., 0:size]
                rest = jnp.transpose(rest, (2, 3, 0, 1, 4)).reshape(out_rows, -1)
                return jnp.concatenate([main, rest], axis=1)

            block = jnp.stack([half[1, :, :, stop:] for half in held])
            block = block.reshape(2, batch_count, out_rows, far, depth_two)[..., 0:lateral_rows]
            block = jnp.transpose(block, (2, 3, 0, 1, 4)).reshape(out_rows, tm_count, 5, -1)
            side_rows = jnp.swapaxes(block, 1, 2).reshape(out_rows, 5 * CF)
            tall_rows = []
            for half in held:
                block = half[0, :, :, stop:].reshape(CSM // width, width, width)
                block = jnp.concatenate([block[k] for k in range(CSM // width)], axis=1)
                tall_rows.append(block.reshape(far, depth_two, CSM))
            tall_rows = jnp.stack(tall_rows, axis=1).reshape(-1, CSM)
            results = (
                side_rows,
                taps_of(0, condense_base, 2, rest_depth),
                taps_of(1, mixing_base, 8, mixing_rows - main_rows),
                tall_rows,
            )
            return [rule(base, item.astype(F32), ratio_of(base), factor) for base, item in zip(bases, results)]

        grads = spread_rows(
            carry, bases[carry],
            grad_one.T, grad_two.T, grad_two,
        )
        orthos = spread_rows(
            renew, bases[renew],
            low(rows_by_rows(shape_one, moved_one)),
            low(rows_by_rows(shape_two, moved_two)),
            low(rows_by_columns(moved_two, shape_two)),
        )

    if not near:
        direct = direct_orthos(stem_moved, shapes, items)
    stem_ortho, *small_orthos = direct
    part = recover.shape[0]
    small_own = [
        own(small_grads[0], small_rows),
        own(small_grads[1], small_rows),
        own(small_grads[2].T, part),
    ]

    def both_of(weight, speed, grad, ortho):
        ortho = low(ortho).astype(F32)
        return (
            carry(speed, grad.astype(F32), 1.0, factor),
            renew(weight, ortho, ratio_of(weight), factor),
        )

    stem_pair = both_of(stem_weight, stem_velocity, stem_own, stem_ortho)
    small_pairs = [
        both_of(*items)
        for items in zip(
            (squeeze, blending, recover),
            (squeeze_velocity, blending_velocity, recover_velocity),
            small_own,
            small_orthos,
        )
    ]
    carried = [stem_pair[0], *grads] + [pair[0] for pair in small_pairs]
    updated = [stem_pair[1], *orthos] + [pair[1] for pair in small_pairs]
    head_new, head_first, head_second = adam(
        head_weight, head_moment, head_square, head_grad * factor, HEAD_RATE, WEIGHT_DECAY
    )
    affine_new, affine_first, affine_second = adam(
        affine, affine_moment, affine_square, affine_grad * factor, AFFINE_RATE, 0.0
    )
    return (
        *carried,
        *updated,
        head_new,
        head_first,
        head_second,
        affine_new,
        affine_first,
        affine_second,
        loss_total,
        clip_count,
        grad_norm,
    )


def solution(mesh):
    in_specs = (
        P("batch", "tm", None, None, None),
        P("batch"),
        P("batch"),
        P("batch"),
        P("batch"),
        P("batch", None),
        P("batch", None),
        P("batch", None),
        P("batch", None),
        P("batch", None),
        P("batch", None),
        P("batch", None),
        P("batch", None),
        P("batch", None),
        P("batch", None),
        P("batch", None),
        P("batch", None),
        P("batch", None),
        P("batch", None),
        P("batch", None),
        P("batch", None),
        P("batch", None),
        P("batch", None),
        P("batch", None),
        P(),
        P(),
        P(),
    )
    out_specs = (
        P("batch", None),
        P("batch", None),
        P("batch", None),
        P("batch", None),
        P("batch", None),
        P("batch", None),
        P("batch", None),
        P("batch", None),
        P("batch", None),
        P("batch", None),
        P("batch", None),
        P("batch", None),
        P("batch", None),
        P("batch", None),
        P("batch", None),
        P("batch", None),
        P("batch", None),
        P("batch", None),
        P("batch", None),
        P(),
        P(),
        P(),
        P(),
        P(),
        P(),
    )
    return jax.shard_map(
        per_device, mesh=mesh, in_specs=in_specs, out_specs=out_specs, check_vma=False
    )
```

```python
import functools
import math

import jax
import jax.numpy as jnp
from jax import lax
from jax.experimental import pallas as pl
from jax.experimental.pallas import tpu as pltpu
from jax.sharding import PartitionSpec as P

CS = 2048
CSM = 512
CF = 256
CFM = 64
CLS = 400
ALPHA = 4
NS_STEPS = 3
STEP = 10


HIGHEST = lax.Precision.HIGHEST
NORM_EPS = 1e-05
CLIP_AT = 0.01
MUON_RATE = 0.5
MUON_KEEP = 0.95
WEIGHT_DECAY = 0.01
ADAM_ONE = 0.9
ADAM_TWO = 0.999
ADAM_EPS = 1e-08
HEAD_RATE = 0.02
AFFINE_RATE = 0.1
NS_FIRST = 3.4445
NS_SECOND = -4.775
NS_THIRD = 2.0315


F32 = jnp.float32
BF16 = jnp.bfloat16
VMEM = 61 * 1024 * 1024
SIDE_AT = 9 * CSM
CONDENSE_AT = SIDE_AT + 5 * CF
RESTORE_AT = CONDENSE_AT + 3 * CS
GRAM = BF16
SIX = (CSM, CSM, CS, CFM, CFM, CF)


def swap(values, axis, mask):
    count = lax.axis_size(axis)
    return lax.ppermute(values, axis, [(i, i ^ mask) for i in range(count)])


def shift(values, axis, step):
    count = lax.axis_size(axis)
    route = [(i, i + step) for i in range(count) if 0 <= i + step < count]
    return lax.ppermute(values, axis, route)


def spread_all(rows, axes):
    count = math.prod(lax.axis_size(axis) for axis in axes)
    copies = jnp.broadcast_to(rows[None], (count,) + rows.shape)
    return lax.all_to_all(copies, axes, 0, 0, tiled=True)


def all_sum(pieces, axes):
    flat = jnp.concatenate([piece.reshape(-1) for piece in pieces])
    length = flat.shape[0]
    wide = -(-length // 1024) * 128
    flat = jnp.pad(flat, (0, 8 * wide - length)).reshape(8, wide)
    total = jnp.sum(spread_all(flat, axes), axis=0).reshape(-1)
    parts = []
    start = 0
    for piece in pieces:
        parts.append(total[start : start + piece.size].reshape(piece.shape))
        start = start + piece.size
    return parts


def pick(values, dim, place):
    return lax.dynamic_index_in_dim(values, place, dim, keepdims=False)


def bits(axis, low):
    count = lax.axis_size(axis).bit_length() - 1
    return [(axis, bit) for bit in range(count - 1, low - 1, -1)]


def halve(view, live, order):
    live = list(live)
    for axis, bit in order:
        dim = live.index((axis, bit))
        flag = (lax.axis_index(axis) >> bit) & 1
        got = swap(pick(view, dim, 1 - flag).astype(BF16), axis, 1 << bit)
        view = pick(view, dim, flag) + got.astype(F32)
        live.remove((axis, bit))
    return view


def dot(left, right, dims):
    return lax.dot_general(left, right, ((dims[0], dims[1]), ((), ())), preferred_element_type=F32)


def rows_by_rows(left, right):
    return dot(left, right, ((1,), (1,)))


def rows_by_columns(left, right):
    return dot(left, right, ((1,), (0,)))


def over_rows(left, right):
    return dot(left, right, ((0,), (0,)))


def split_affine(vector):
    gains = []
    shifts = []
    start = 0
    for width in SIX:
        gains.append(vector[start : start + width])
        start = start + width
    for width in SIX:
        shifts.append(vector[start : start + width])
        start = start + width
    return (gains, shifts, vector[start : start + CLS])


def silu_grad(values):
    sigma = jax.nn.sigmoid(values)
    return sigma * (1.0 + values * (1.0 - sigma))


def call(kernel, outs, args, scratch=(), far=(), copies=0, micros=6, scalars=()):
    specs = [
        pl.BlockSpec(
            memory_space=pl.ANY
            if place in far
            else pltpu.SMEM
            if place in scalars
            else pltpu.VMEM
        )
        for place in range(len(args))
    ]
    shapes = [pltpu.VMEM(shape, kind) for shape, kind in scratch]
    if copies:
        shapes.append(pltpu.SemaphoreType.DMA((copies,)))
    return pl.pallas_call(
        kernel,
        in_specs=specs,
        out_shape=[jax.ShapeDtypeStruct(shape, kind) for shape, kind in outs],
        scratch_shapes=shapes,
        compiler_params=pltpu.CompilerParams(vmem_limit_bytes=VMEM),
        cost_estimate=pl.CostEstimate(
            flops=micros * 1150000000, bytes_accessed=micros * 3000000, transcendentals=0
        ),
    )(*args)


def fetch(source, target, flags, spans):
    started = []
    for place, (there, here, width) in enumerate(spans):
        copy = pltpu.make_async_copy(
            source.at[:, pl.ds(there, width)], target.at[:, pl.ds(here, width)], flags.at[place]
        )
        copy.start()
        started.append(copy)
    return started


def fetch_tall(source, target, flags, start):
    started = []
    count = flags.shape[0] // 4
    block = source.shape[0] // count
    for place in range(4 * count):
        b, k = (place // 4, place % 4)
        copy = pltpu.make_async_copy(
            source.at[pl.ds(b * block, block), pl.ds(start + k * CSM, CSM)],
            target.at[pl.ds(place * block, block), :],
            flags.at[place],
        )
        copy.start()
        started.append(copy)
    return started


def nt(left, right):
    return dot(left, right, ((1,), (1,)))


def nn(left, right):
    return dot(left, right, ((1,), (0,)))


def silu(values):
    return values * jax.nn.sigmoid(values)


def low(values):
    return values.astype(BF16)


def sums(held, other):
    return (
        jnp.sum(held, axis=0, keepdims=True),
        jnp.sum(held * other, axis=0, keepdims=True),
    )


def flat(values):
    return values.reshape(values.shape[0] * values.shape[1], values.shape[2])


def put_narrow(out, block, slow, fast, extra=()):
    block[...] = jnp.zeros_like(block)
    for place, vector in enumerate(slow):
        block[2 * place : 2 * place + 1, :] = vector[:, 0:256]
        block[2 * place + 1 : 2 * place + 2, :] = vector[:, 256:512]
    for place, vector in enumerate(fast):
        block[4 + place : 5 + place, 0:CFM] = vector
    for place, value in enumerate(extra):
        block[6 + place : 7 + place, 0:128] = jnp.broadcast_to(value, (1, 128))
    out[...] = jnp.broadcast_to(block[...][None], out.shape).astype(out.dtype)


def get_narrow(total):
    slow = [
        jnp.concatenate([total[2 * k : 2 * k + 1], total[2 * k + 1 : 2 * k + 2]], axis=1)
        for k in range(2)
    ]
    fast = [total[4 + k : 5 + k, 0:CFM] for k in range(2)]
    return slow, fast


def put_wide(out, slow, fast, extra=None):
    out[...] = jnp.zeros_like(out)
    for place, vector in enumerate(slow):
        for row in range(4):
            out[4 * place + row : 4 * place + row + 1, 0:512] = vector[:, 512 * row : 512 * row + 512]
    for place, vector in enumerate(fast):
        for row in range(2):
            spot = 2 * place + row
            out[spot : spot + 1, 512:640] = vector[:, 128 * row : 128 * row + 128]
    if extra is not None:
        for row in range(4, 7):
            part = low(jnp.broadcast_to(extra, (1, 128))).astype(F32)
            out[row : row + 1, 512:640] = part
            extra = extra - part


def get_wide(total):
    slow = [
        jnp.concatenate([total[4 * k + row : 4 * k + row + 1, 0:512] for row in range(4)], axis=1)
        for k in range(2)
    ]
    fast = [
        jnp.concatenate(
            [total[2 * k + row : 2 * k + row + 1, 512:640] for row in range(2)], axis=1
        )
        for k in range(2)
    ]
    return slow, fast


def moments(pair, count):
    mean = pair[0] / count
    spread = pair[1] / count - mean * mean
    return mean, lax.rsqrt(spread + NORM_EPS)


def counts(total, frames):
    count = total[6:7, 0:1]
    return count, count * frames


def in_relation(place, outs, values):
    for k, out in enumerate(outs):
        for p, value in enumerate(values):

            @pl.when(jnp.bitwise_xor(place, k) == p)
            def store(out=out, value=value):
                out[...] = value


def stem_kernel(near, place, slow_video, fast_video, weight, mask, *refs):
    videos = refs[0:4] if near else ()
    slow_pre, fast_pre, slow_low, fast_low, *shares = refs[len(videos) :]
    held = mask[...]
    for k in range(3):
        pre = nt(slow_video[k], weight[0:CS, :])
        if k == 1:
            slow_pre[...] = pre
        act = low(silu(pre) * held)
        slow_low[k] = act
        if k == 1 and not near:
            count, _, width = shares[0].shape
            for p in range(count):
                shares[0][p] = act[:, p * width : (p + 1) * width]
    if near:
        width = CS // 4
        own_rows = weight[pl.ds(pl.multiple_of(place[0] * width, width), width), :]
        for video, share in zip(videos, shares[0:4]):
            share[...] = low(silu(nt(video[...], own_rows)) * held)
    count = fast_video.shape[0]
    for k in range(count):
        pre = nt(fast_video[k], weight[CS:, :])
        if 2 <= k < count - 1:
            fast_pre[k - 2] = pre
        act = low(silu(pre) * held)
        fast_low[k] = act
        if near and k < 5:
            parts = [act[:, 0:128], act[:, 128:256]]
            in_relation(place[0] // 2, [side.at[k] for side in shares[4:6]], parts)


def first_kernel(
    slow_low, fast_low, weights, squeeze, mask, valid, h1, h4, out, block, first, flags
):
    spans = [(SIDE_AT, 0, 5 * CF)]
    spans += [(CONDENSE_AT + k * CS, 5 * CF + k * CS, CS) for k in range(3)]
    copies = fetch(weights, first, flags, spans)
    held = mask[...]
    copies[0].wait()
    total = None
    for k in range(5):
        term = nt(fast_low[k], first[:, k * CF : (k + 1) * CF])
        total = term if total is None else total + term
    for k in range(3):
        start = 5 * CF + k * CS
        copies[1 + k].wait()
        total = total + nt(slow_low[k], first[:, start : start + CS])
    h1[...] = total
    slow = sums(total * held, total)
    frames = h4.shape[0]
    fast = None
    for frame in range(frames):
        piece = None
        for k in range(3):
            term = nt(fast_low[1 + k + frame], squeeze[:, k * CF : (k + 1) * CF])
            piece = term if piece is None else piece + term
        h4[frame] = piece
        pair = sums(piece * held, piece)
        fast = pair if fast is None else tuple(a + b for a, b in zip(fast, pair))
    put_narrow(out, block, slow, fast, (jnp.sum(held), jnp.sum(valid[...])))


def fill(pad, values):
    side = pad.shape[0] - 2
    pad[1 : side + 1, 1 : side + 1] = values.reshape(side, side, pad.shape[2], pad.shape[3])


def tap_of(pad, down, right):
    side = pad.shape[0] - 2
    values = pad[down : down + side, right : right + side]
    return values.reshape(side * side * pad.shape[2], pad.shape[3])


def second_kernel(near, *refs):
    place, h1, h4, got, slow_par, fast_par, mask, weights, blending = refs[0:9]
    h2, h5, total_out, out = refs[9:13]
    shares = refs[13:17] if near else refs[13:14]
    pad, fast_pad, block, mixing, flags = refs[-5:]
    copies = fetch(weights, mixing, flags, [(tap * CSM, tap * CSM, CSM) for tap in range(9)])
    held = mask[...]
    frames = h4.shape[0]
    total = jnp.sum(got[...].astype(F32), axis=0)
    total_out[...] = total
    slow, fast = get_narrow(total)
    slow_count, fast_count = counts(total, frames)
    mean, inverse = moments(slow, slow_count)
    level = slow_par[0:1] * ((h1[...] - mean) * inverse) + slow_par[1:2]
    pad[...] = jnp.zeros_like(pad)
    act = low(silu(level) * held)
    if near:
        in_relation(place[0], shares, [act[:, p * 128 : (p + 1) * 128] for p in range(4)])
    else:
        shares[0][...] = act
    fill(pad, act.astype(F32))
    acc = None
    for tap in range(9):
        piece = low(tap_of(pad, tap // 3, tap % 3))
        copies[tap].wait()
        term = nt(piece, mixing[:, tap * CSM : (tap + 1) * CSM])
        acc = term if acc is None else acc + term
    h2[...] = acc
    slow_pair = sums(acc * held, acc)
    mean, inverse = moments(fast, fast_count)
    fast_pad[...] = jnp.zeros_like(fast_pad)
    fast_pair = None
    for frame in range(frames):
        level = fast_par[0:1] * ((h4[frame] - mean) * inverse) + fast_par[1:2]
        fill(fast_pad, low(silu(level) * held).astype(F32))
        acc = None
        for tap in range(9):
            piece = low(tap_of(fast_pad, tap // 3, tap % 3))
            term = nn(piece, blending[tap])
            acc = term if acc is None else acc + term
        h5[frame] = acc
        pair = sums(acc * held, acc)
        fast_pair = pair if fast_pair is None else tuple(a + b for a, b in zip(fast_pair, pair))
    put_narrow(out, block, slow_pair, fast_pair)


def third_kernel(
    h2, h5, before, got, slow_par, fast_par, mask, weights, recover, a2, a5, h3, h6, total_out, out,
    restore, flags,
):
    copies = fetch_tall(weights, restore, flags, RESTORE_AT)
    held = mask[...]
    frames = h5.shape[0]
    total = jnp.sum(got[...].astype(F32), axis=0)
    total_out[...] = total
    slow, fast = get_narrow(total)
    slow_count, fast_count = counts(before[...], frames)
    mean, inverse = moments(slow, slow_count)
    level = slow_par[0:1] * ((h2[...] - mean) * inverse) + slow_par[1:2]
    act = low(silu(level) * held)
    a2[...] = act
    for copy in copies:
        copy.wait()
    acc = nt(act, restore[...])
    h3[...] = acc
    slow_pair = sums(acc * held, acc)
    mean, inverse = moments(fast, fast_count)
    fast_pair = None
    for frame in range(frames):
        level = fast_par[0:1] * ((h5[frame] - mean) * inverse) + fast_par[1:2]
        act = low(silu(level) * held)
        a5[frame] = act
        acc = nt(act, recover[...])
        h6[frame] = acc
        pair = sums(acc * held, acc)
        fast_pair = pair if fast_pair is None else tuple(a + b for a, b in zip(fast_pair, pair))
    put_wide(out, slow_pair, fast_pair)


def by_clip(values, clips):
    return jnp.sum(values.reshape(-1, clips, values.shape[1]), axis=0)


def pool_kernel(
    h3, h6, slow_pre, fast_pre, before, got, slow_par, fast_par, mask, out, total_out
):
    held = mask[...]
    frames = h6.shape[0]
    clips = out.shape[0]
    total = jnp.sum(got[...].astype(F32), axis=0)
    total_out[...] = total
    slow, fast = get_wide(total)
    slow_count, fast_count = counts(before[...], frames)
    mean, inverse = moments(slow, slow_count)
    scaled = (h3[...] - mean) * inverse
    residual = silu(slow_pre[...]) * held + slow_par[0:1] * scaled + slow_par[1:2]
    out[:, 0:CS] = by_clip(silu(residual) * held, clips)
    mean, inverse = moments(fast, fast_count)
    pooled = None
    for frame in range(frames):
        scaled = (h6[frame] - mean) * inverse
        residual = silu(fast_pre[frame]) * held + fast_par[0:1] * scaled + fast_par[1:2]
        part = by_clip(silu(residual) * held, clips)
        pooled = part if pooled is None else pooled + part
    out[:, CS:] = pooled


def mixed(average, values):
    total = None
    for k in range(values.shape[0]):
        term = average[:, k : k + 1] * values[k : k + 1, :]
        total = term if total is None else total + term
    return total


def head_kernel(
    pools, head, bias, ids_down, ids_across, labels, valid, area, h3, h6, slow_pre, fast_pre,
    before, total_in, slow_par, fast_par, mask, features, logit_low, d3, d6, out,
):
    held = mask[...]
    frames = h6.shape[0]
    clips = features.shape[0]
    tm_count = pools.shape[0]
    parts = [pools[k] for k in range(tm_count)]
    while len(parts) > 1:
        parts = [parts[k] + parts[k + 1] for k in range(0, len(parts), 2)]
    (pool,) = parts
    slow_divide = area[...] * tm_count
    fast_divide = slow_divide * frames
    slow_feature = low(pool[:, 0:CS] / slow_divide)
    fast_feature = low(pool[:, CS:] / fast_divide)
    features[:, 0:CS] = slow_feature
    features[:, CS:] = fast_feature
    logits = nn(slow_feature, head[0:CS, :]) + nn(fast_feature, head[CS:, :]) + bias[...]
    same = (ids_down[...] == ids_across[...]).astype(F32)
    average = same / jnp.sum(same, axis=1, keepdims=True)
    mean_logits = mixed(average, logits)
    top = jnp.max(mean_logits, axis=1, keepdims=True)
    powers = jnp.exp(mean_logits - top)
    whole = jnp.sum(powers, axis=1, keepdims=True)
    classes = lax.broadcasted_iota(jnp.int32, mean_logits.shape, 1)
    onehot = (labels[...] == classes).astype(F32)
    picked = jnp.sum(onehot * mean_logits, axis=1, keepdims=True)
    loss = jnp.sum(valid[...] * (jnp.log(whole) + top - picked))
    mean_grad = valid[...] * (powers / whole - onehot)
    logit = low(mixed(average, mean_grad))
    logit_low[...] = logit
    slow_count, fast_count = counts(before[...], frames)
    slow, fast = get_wide(total_in[...])

    grad = nt(logit, head[0:CS, :]) / slow_divide
    mean, inverse = moments(slow, slow_count)
    scaled = (h3[...] - mean) * inverse
    residual = silu(slow_pre[...]) * held + slow_par[0:1] * scaled + slow_par[1:2]
    down = held * silu_grad(residual)
    down = (down.reshape(-1, clips, CS) * grad[None]).reshape(down.shape)
    d3[...] = down
    slow_pair = sums(down, scaled)

    grad = nt(logit, head[CS:, :]) / fast_divide
    mean, inverse = moments(fast, fast_count)
    fast_pair = None
    for frame in range(frames):
        scaled = (h6[frame] - mean) * inverse
        residual = silu(fast_pre[frame]) * held + fast_par[0:1] * scaled + fast_par[1:2]
        down = held * silu_grad(residual)
        down = (down.reshape(-1, clips, CF) * grad[None]).reshape(down.shape)
        d6[frame] = down
        pair = sums(down, scaled)
        fast_pair = pair if fast_pair is None else tuple(a + b for a, b in zip(fast_pair, pair))
    put_wide(out, slow_pair, fast_pair, loss)


def under(upstream, values, mean, inverse, gain, pair, count, held):
    scaled = (values - mean) * inverse
    return low(held * gain * inverse * (upstream - (pair[0] + scaled * pair[1]) / count))


def third_back_kernel(
    near, place, d3, d6, h3, h6, h2, h5, before, total3, total2, got, slow3, fast3, slow2, fast2, mask,
    weights, recover, u6, e2, e5, total_out, out, *rest
):
    u3 = rest[0:4] if near else rest[0:1]
    block, restore, flags = rest[-3:]
    copies = fetch_tall(weights, restore, flags, RESTORE_AT)
    held = mask[...]
    frames = h6.shape[0]
    total = jnp.sum(got[...].astype(F32), axis=0)
    total_out[...] = total
    slow_count, fast_count = counts(before[...], frames)
    slow_pair, fast_pair = get_wide(total)
    slow, fast = get_wide(total3[...])
    slow_two, fast_two = get_narrow(total2[...])
    mean, inverse = moments(slow, slow_count)
    upper = under(d3[...], h3[...], mean, inverse, slow3[0:1], slow_pair, slow_count, held)
    if near:
        wide = upper.astype(F32)
        tiles = [wide[:, k * 128 : (k + 1) * 128] for k in range(CS // 128)]
        turned = [pltpu.roll(tile, 64, 1) for tile in tiles]
        first_half = lax.broadcasted_iota(jnp.int32, tiles[0].shape, 1) < 64
        parts = []
        for p in range(4):
            held_tiles = []
            for k in range(4):
                one = 4 * k + p // 2
                two = one + 2
                if p % 2 == 0:
                    tile = jnp.where(first_half, tiles[one], turned[two])
                else:
                    tile = jnp.where(first_half, turned[one], tiles[two])
                held_tiles.append(low(tile))
            parts.append(jnp.concatenate(held_tiles, axis=1))
        in_relation(place[0], u3, parts)
    else:
        u3[0][...] = upper
    mean, inverse = moments(slow_two, slow_count)
    scaled = (h2[...] - mean) * inverse
    for copy in copies:
        copy.wait()
    down = nn(upper, restore[...]) * held * silu_grad(slow2[0:1] * scaled + slow2[1:2])
    e2[...] = down
    slow_out = sums(down, scaled)
    mean, inverse = moments(fast, fast_count)
    mean_two, inverse_two = moments(fast_two, fast_count)
    fast_out = None
    for frame in range(frames):
        upper = under(d6[frame], h6[frame], mean, inverse, fast3[0:1], fast_pair, fast_count, held)
        u6[frame] = upper
        scaled = (h5[frame] - mean_two) * inverse_two
        down = nn(upper, recover[...]) * held * silu_grad(fast2[0:1] * scaled + fast2[1:2])
        e5[frame] = down
        pair = sums(down, scaled)
        fast_out = pair if fast_out is None else tuple(a + b for a, b in zip(fast_out, pair))
    put_narrow(out, block, slow_out, fast_out)


def second_back_kernel(
    e2, e5, h2, h5, h1, h4, total2, total1, got, slow2, fast2, slow1, fast1, mask,
    weights, blending, u2, u5, e1, e4, blend_grad, total_out, out, pad, fast_pad, act_pad, block,
    mixing, flags,
):
    copies = fetch(weights, mixing, flags, [(tap * CSM, tap * CSM, CSM) for tap in range(9)])
    held = mask[...]
    frames = h5.shape[0]
    total = jnp.sum(got[...].astype(F32), axis=0)
    total_out[...] = total
    slow_count, fast_count = counts(total1[...], frames)
    slow_pair, fast_pair = get_narrow(total)
    slow_two, fast_two = get_narrow(total2[...])
    slow_one, fast_one = get_narrow(total1[...])
    mean, inverse = moments(slow_two, slow_count)
    upper = under(e2[...], h2[...], mean, inverse, slow2[0:1], slow_pair, slow_count, held)
    u2[...] = upper
    pad[...] = jnp.zeros_like(pad)
    fill(pad, upper.astype(F32))
    acc = None
    for tap in range(9):
        piece = low(tap_of(pad, 2 - tap // 3, 2 - tap % 3))
        copies[tap].wait()
        term = nn(piece, mixing[:, tap * CSM : (tap + 1) * CSM])
        acc = term if acc is None else acc + term
    mean, inverse = moments(slow_one, slow_count)
    scaled = (h1[...] - mean) * inverse
    down = acc * held * silu_grad(slow1[0:1] * scaled + slow1[1:2])
    e1[...] = down
    slow_out = sums(down, scaled)
    mean, inverse = moments(fast_two, fast_count)
    mean_one, inverse_one = moments(fast_one, fast_count)
    fast_pad[...] = jnp.zeros_like(fast_pad)
    act_pad[...] = jnp.zeros_like(act_pad)
    fast_out = None
    for frame in range(frames):
        upper = under(e5[frame], h5[frame], mean, inverse, fast2[0:1], fast_pair, fast_count, held)
        u5[frame] = upper
        scaled = (h4[frame] - mean_one) * inverse_one
        level = fast1[0:1] * scaled + fast1[1:2]
        fill(fast_pad, upper.astype(F32))
        fill(act_pad, low(silu(level) * held).astype(F32))
        turned = low(upper.astype(F32).T)
        acc = None
        for tap in range(9):
            down_by, right_by = (tap // 3, tap % 3)
            piece = low(tap_of(fast_pad, 2 - down_by, 2 - right_by))
            term = nt(piece, blending[tap])
            acc = term if acc is None else acc + term
            part = nn(turned, low(tap_of(act_pad, down_by, right_by)))
            blend_grad[tap] = part if frame == 0 else blend_grad[tap] + part
        down = acc * held * silu_grad(level)
        e4[frame] = down
        pair = sums(down, scaled)
        fast_out = pair if fast_out is None else tuple(a + b for a, b in zip(fast_out, pair))
    put_narrow(out, block, slow_out, fast_out)


def mixing_grad_kernel(acts, uppers, out, pad):
    count = acts.shape[0]
    pad[...] = jnp.zeros_like(pad)
    for place in range(count):
        fill(pad.at[place], acts[place].astype(F32))
    for tap in range(9):
        total = None
        for place in range(count):
            piece = low(tap_of(pad.at[place], tap // 3, tap % 3))
            term = dot(piece, uppers[place], ((0,), (0,)))
            total = term if total is None else total + term
        out[tap] = low(total)


def first_back_kernel(
    e1, e4, h1, h4, total1, got, slow1, fast1, mask, u1, u4, total_out
):
    held = mask[...]
    frames = h4.shape[0]
    total = jnp.sum(got[...].astype(F32), axis=0)
    total_out[...] = total
    slow_count, fast_count = counts(total1[...], frames)
    slow_pair, fast_pair = get_narrow(total)
    slow, fast = get_narrow(total1[...])
    mean, inverse = moments(slow, slow_count)
    u1[...] = under(e1[...], h1[...], mean, inverse, slow1[0:1], slow_pair, slow_count, held)
    mean, inverse = moments(fast, fast_count)
    for frame in range(frames):
        u4[frame] = under(
            e4[frame], h4[frame], mean, inverse, fast1[0:1], fast_pair, fast_count, held
        )


def by_frame(place, target, parts):
    target[0] = jnp.zeros_like(target[0])
    target[len(parts) + 1] = jnp.zeros_like(target[0])
    for k, part in enumerate(parts):
        target[jnp.bitwise_xor(place, k) + 1] = part


def turn(parts):
    own, across, beside, beyond = parts
    return [own[...], beside[...], across[...], beyond[...]]


def stem_grad_kernel(
    place, slow_up, fast_up, video, small, out_0, out_1, out_2, out_3, total
):
    total[0:CS, :] = dot(slow_up[...], video[0], ((0,), (0,)))
    fast = None
    for frame in range(fast_up.shape[0]):
        term = dot(fast_up[frame], video[frame], ((0,), (0,)))
        fast = term if fast is None else fast + term
    total[CS:, :] = fast
    size = total.shape[0] // 8
    for k, out in enumerate((out_0, out_1, out_2, out_3)):
        target = jnp.bitwise_xor(place[0], k)
        for b in range(8):
            start = pl.multiple_of(b * size + target * (size // 4), 8)
            rows = total[pl.ds(start, size // 4), :]
            out[b] = low(jnp.concatenate([rows, small[target, b]]))


def early_kernel(*refs):
    uppers, acts, out = refs[0:4], refs[4:8], refs[8]
    total = None
    for upper, act in zip(uppers, turn(acts)):
        term = dot(upper[...], act, ((0,), (0,)))
        total = term if total is None else total + term
    size = total.shape[0] // out.shape[0]
    for b in range(out.shape[0]):
        out[b] = low(total[b * size : (b + 1) * size])


def mixing_kernel(*refs):
    acts, uppers, restore, out, pad = refs[0:4], refs[4:8], refs[8], refs[9], refs[10]
    pad[...] = jnp.zeros_like(pad)
    for k, act in enumerate(acts):
        fill(pad.at[k], act[...].astype(F32))
    parts = turn(uppers)
    for tap in range(9):
        total = None
        for k, upper in enumerate(parts):
            term = dot(low(tap_of(pad.at[k], tap // 3, tap % 3)), upper, ((0,), (0,)))
            total = term if total is None else total + term
        if tap < 8:
            out[tap, 0:128, :] = low(total)
        else:
            for b in range(8):
                out[b, 128:144, :] = low(total[b * 16 : (b + 1) * 16])
    for b in range(8):
        out[b, 144:208, :] = restore[b]


def late_kernel(*refs):
    place, cells, sides, uppers = refs[0], refs[1:5], refs[5:9], refs[9:13]
    out, frames, side_total, side_rows = refs[13:17]
    here = place[0]
    by_frame(here, frames, [cell[...] for cell in cells])
    parts = turn(uppers)
    for tap in range(3):
        total = None
        for k, upper in enumerate(parts):
            cell = frames[jnp.bitwise_xor(here, k) + tap]
            term = dot(cell, upper, ((0,), (0,)))
            total = term if total is None else total + term
        for b in range(4):
            if tap < 2:
                out[tap * 4 + b, 0:128, :] = low(total[b * 128 : (b + 1) * 128])
            else:
                out[2 * b, 128:192, :] = low(total[b * 128 : b * 128 + 64])
                out[2 * b + 1, 128:192, :] = low(total[b * 128 + 64 : (b + 1) * 128])
    core = here % 2
    own, across, beside, beyond = sides
    for tap in range(5):
        total = None
        turned = (own[tap], beside[tap], across[tap], beyond[tap])
        for side, upper in zip(turned, parts):
            term = dot(side, upper, ((0,), (0,)))
            total = term if total is None else total + term
        side_total[...] = total
        side_rows[tap * 64 : (tap + 1) * 64, :] = side_total[
            pl.ds(pl.multiple_of(core * 64, 64), 64), :
        ]
    blank = jnp.zeros((8, CSM), F32)
    for b in range(8):
        rows = jnp.concatenate([side_rows[b * 40 : (b + 1) * 40, :], blank])
        out[b, 192:240, :] = low(rows)


def stem_back_kernel(near, place, *refs):
    u1_held = refs[0:4] if near else refs[0]
    (
        u4, u4_before, u4_after, weights, squeeze, d3, d6, slow_pre, fast_pre,
        mask, slow_up, fast_up, first, frames_held, flags,
    ) = refs[-15:]
    spans = [(CONDENSE_AT + k * CS, 5 * CF + k * CS, CS) for k in range(3)]
    copies = fetch(weights, first, flags, spans + [(SIDE_AT, 0, 5 * CF)])
    held = mask[...]
    frames = fast_up.shape[0]
    total = d3[...]
    if near:
        by_frame(place[0], frames_held, turn(u1_held))
        source = frames_held
    else:
        source = u1_held
    u1_before, u1, u1_after = [source[place[0] + k] for k in range(3)]
    for tap, piece in enumerate((u1_after, u1, u1_before)):
        start = 5 * CF + tap * CS
        copies[tap].wait()
        total = total + nn(piece, first[:, start : start + CS])
    copies[3].wait()
    slow_up[...] = low(total * held * silu_grad(slow_pre[...]))
    for frame in range(frames):
        total = d6[frame]
        pairs = [(frame + 2, u1)] if frame < 3 else []
        pairs = pairs + ([(frame - 2, u1_after)] if frame >= 2 else [])
        for tap, piece in pairs:
            total = total + nn(piece, first[:, tap * CF : (tap + 1) * CF])
        for tap in range(3):
            place = frame + 1 - tap
            if place < 0:
                piece = u4_before[...]
            elif place >= frames:
                piece = u4_after[...]
            else:
                piece = u4[place]
            total = total + nn(piece, squeeze[:, tap * CF : (tap + 1) * CF])
        fast_up[frame] = low(total * held * silu_grad(fast_pre[frame]))


def product(left, right):
    left_high = low(left)
    right_high = low(right)
    if left.shape[0] >= CSM:
        return nn(left_high, right_high)
    left_rest = low(left - left_high.astype(F32))
    right_rest = low(right - right_high.astype(F32))
    return nn(left_high, right_high) + (nn(left_high, right_rest) + nn(left_rest, right_high))


def shape_kernel(*refs):
    half = len(refs) // 2
    grams = []
    eyes = []
    scales = []
    totals = []
    for source in refs[:half]:
        size = source.shape[0]
        gram = source[...]
        rows = lax.broadcasted_iota(jnp.int32, (size, size), 0)
        columns = lax.broadcasted_iota(jnp.int32, (size, size), 1)
        eye = (rows == columns).astype(F32)
        diagonal = jnp.sum(gram * eye, axis=1, keepdims=True)
        diagonal = jnp.sum(diagonal, axis=0, keepdims=True)
        scale = 1.0 / (jnp.sqrt(diagonal) + 1e-07)
        grams.append(gram * (scale * scale))
        eyes.append(eye)
        scales.append(scale)
    for step in range(NS_STEPS):
        extras = [NS_SECOND * gram + NS_THIRD * product(gram, gram) for gram in grams]
        if step == 0:
            totals = [NS_FIRST * eye + extra for eye, extra in zip(eyes, extras)]
        else:
            totals = [
                NS_FIRST * total + product(extra, total) for total, extra in zip(totals, extras)
            ]
        if step + 1 < NS_STEPS:
            middles = [NS_FIRST * g + product(extra, g) for g, extra in zip(grams, extras)]
            grams = [NS_FIRST * m + product(extra, m) for m, extra in zip(middles, extras)]
    for target, total, scale in zip(refs[half:], totals, scales):
        target[...] = (total * scale).astype(target.dtype)


def block_shape_kernel(whole, *refs):
    small, outs = refs[0:3], refs[3:8]
    gram, stem, packed = refs[8:11]
    for b in range(8):
        packed[b * 40 : (b + 1) * 40, :] = whole[b, 64:112, :].astype(F32)[0:40]
        rows = whole[b, 96:128, :].astype(F32)[8:24]
        stem[b * 24 : b * 24 + 16, :] = rows[:, 0:192]
        stem[b * 24 + 16 : b * 24 + 24, :] = rows[0:8, 256:448]
    gram[0:128, :] = packed[0:128, :]
    gram[128:256, 128:512] = packed[128:256, 0:384]
    gram[256:384, 256:384] = packed[128:256, 384:512]
    for k, (row, column) in enumerate(((256, 384), (384, 384))):
        for half in range(2):
            start = (2 * k + half) * 128
            gram[row + 64 * half : row + 64 * half + 64, column : column + 128] = packed[
                256:320, start : start + 128
            ]
    for k in range(3):
        edge = 128 * (k + 1)
        gram[edge:512, edge - 128 : edge] = gram[edge - 128 : edge, edge:512].T
    shape_kernel(gram, stem, *small, *outs)


def gram_kernel(
    place, factor, speed, restore_speed, own, got, stem_speed, stem_grad, one, two, stem_out,
    keep, give, stem_gram, wide, tall, held,
):
    x = place[0] // 2
    core = place[0] % 2
    scale = factor[...]
    for spot, part in ((x, own), (1 - x, got)):
        held[pl.ds(pl.multiple_of(spot * 128, 128), 128), :] = part[0:128, :].astype(F32)
        held[pl.ds(pl.multiple_of(spot * 64 + 256, 64), 64), :] = part[128:192, :].astype(F32)
        held[pl.ds(pl.multiple_of(spot * 64 + 384, 64), 64), :] = part[192:256, :].astype(F32)
    speeds = jnp.concatenate([speed[b, 0:64, :].astype(F32) for b in range(8)]).T
    grads = held[...]
    speed_two = jnp.where(x == 0, restore_speed[...].astype(F32), speeds[384:512])
    moved_one = low(MUON_KEEP * speeds[0:384] + grads[0:384] * scale)
    moved_two = low(MUON_KEEP * speed_two + grads[384:512] * scale)
    one[...] = moved_one
    two[...] = moved_two
    gram_one = low(dot(moved_one, moved_one, ((0,), (0,))))
    gram_two = low(dot(moved_two, moved_two, ((0,), (0,))))
    put_packed(keep, jnp.where(core == 0, gram_one, gram_two))
    put_packed(give, jnp.where(core == 0, gram_two, gram_one))
    moved = low(MUON_KEEP * stem_speed[...] + stem_grad[...].astype(F32) * scale)
    stem_out[...] = moved
    gram = dot(moved, moved, ((0,), (0,)))
    stem_gram[...] = jnp.zeros_like(stem_gram)
    blank = jnp.zeros((8, 192), F32)
    for b in range(8):
        stem_gram[b, :, 0:192] = low(gram[b * 24 : b * 24 + 16])
        rest = jnp.concatenate([gram[b * 24 + 16 : b * 24 + 24], blank])
        stem_gram[b, :, 256:448] = low(rest)
    turned = low(grads.T)
    for b in range(8):
        wide[b] = turned[b * 64 : (b + 1) * 64]
    put_tall(tall, low(grads[384:512]))


def put_packed(out, gram):
    out[0:128, :] = gram[0:128]
    out[128:256, 0:384] = gram[128:256, 128:512]
    out[128:256, 384:512] = gram[256:384, 256:384]
    for k, (row, column) in enumerate(((256, 384), (384, 384))):
        for half in range(2):
            start = (2 * k + half) * 128
            out[256:320, start : start + 128] = gram[
                row + 64 * half : row + 64 * half + 64, column : column + 128
            ]


def put_tall(out, values):
    for k in range(4):
        for h in range(2):
            out[2 * k + h] = values[h * 64 : (h + 1) * 64, k * 128 : (k + 1) * 128]


def ortho_kernel(place, shaped, other, one, two, wide, tall):
    core = place[0] % 2
    shape_one = jnp.where(core == 0, shaped[...], other[...])
    shape_two = jnp.where(core == 0, other[...], shaped[...])
    first = low(nt(shape_one, one[...]))
    second = low(nt(shape_two, two[...]))
    for b in range(8):
        wide[b, :, 0:384] = first[b * 64 : (b + 1) * 64]
        wide[b, :, 384:512] = second[b * 64 : (b + 1) * 64]
    put_tall(tall, low(nn(two[...], shape_two)))


def shape_of(grams):
    return call(shape_kernel, [(item.shape, F32) for item in grams], grams, micros=13)


def carry(base, value, ratio, factor):
    return MUON_KEEP * base + value * factor


def renew(base, value, ratio, factor):
    return base - MUON_RATE * (value * ratio + WEIGHT_DECAY * base)


def selection(count, far, depth, size, x, width, target):
    column = lax.broadcasted_iota(jnp.int32, (count * far * depth, 1), 0)
    place = lax.rem(column, depth)
    block = lax.div(column, depth)
    goal = target(lax.div(block, far), place)
    goal = jnp.where((place < size) & (lax.rem(block, far) == x), goal, -1)
    columns = lax.broadcasted_iota(jnp.int32, (count * far * depth, width), 1)
    return low((goal == columns).astype(F32))


def place_kernel(
    rule, far, main_rows, depth, place, factor, own, across, beside, beyond, lateral, condense, mixing,
    restore, lateral_out, condense_out, mixing_out, restore_out, frames,
):
    for k, part in enumerate((own[...], beside[...], across[...], beyond[...])):
        frames[jnp.bitwise_xor(place[0], k)] = part
    half_one, half_two = [
        [frames.at[2 * target + c] for target in range(far)] for c in range(2)
    ]
    halves = (half_one, half_two)
    batch_count, out_rows, lanes_all = own.shape
    edge = far * main_rows
    stop = far * depth
    scale = factor[...]

    def put(out, base, spot, values):
        lanes = slice(spot, spot + values.shape[1])
        out[:, lanes] = rule(base[:, lanes], values.astype(F32), 1.0, scale)
        return spot + values.shape[1]

    devices = 2 * far
    rest_depth = depth - main_rows
    for target, out, base, main_taps in ((0, condense_out, condense, 2), (1, mixing_out, mixing, 8)):
        share = batch_count // main_taps
        spot = 0
        for tap in range(main_taps):
            for device in range(devices):
                lanes = slice(device // 2 * main_rows, (device // 2 + 1) * main_rows)
                for k in range(tap * share, (tap + 1) * share):
                    spot = put(out, base, spot, halves[device % 2][target][k, :, lanes])
        size = (out.shape[1] - spot) // (batch_count * devices)
        rests = [
            jnp.concatenate([half[target][k, :, edge:stop] for k in range(batch_count)], axis=1)
            for half in halves
        ]
        for x in range(far):
            chosen = selection(
                batch_count, far, rest_depth, size, x, batch_count * size,
                lambda k, r: k * size + r,
            )
            for rest in rests:
                spot = put(out, base, spot, nn(rest, chosen))
    side_depth = (lanes_all - stop) // far
    side_size = lateral.shape[1] // (batch_count * devices)
    channels = CF // devices
    sides = [
        jnp.concatenate([half[1][k, :, stop:] for k in range(batch_count)], axis=1)
        for half in halves
    ]
    for x in range(far):
        total = None
        for c, side in enumerate(sides):

            def goal(k, r):
                row = k * side_size + r
                return lax.div(row, channels) * 2 * channels + c * channels + lax.rem(row, channels)

            chosen = selection(
                batch_count, far, side_depth, side_size, x, 10 * channels, goal
            )
            term = nn(side, chosen)
            total = term if total is None else total + term
        for tap in range(5):
            put(
                lateral_out, lateral, tap * CF + 2 * x * channels,
                total[:, tap * 2 * channels : (tap + 1) * 2 * channels],
            )
    width = lanes_all - stop
    ratio = math.sqrt(max(1.0, restore.shape[0] * batch_count / restore.shape[1]))
    for c, half in enumerate(halves):
        for k in range(batch_count * out_rows // width):
            for h in range(far):
                start = (2 * h + c) * out_rows
                rows = slice(start, start + out_rows)
                lanes = slice(k * width, (k + 1) * width)
                values = half[0][k * width // out_rows + h, :, stop:].astype(F32)
                restore_out[rows, lanes] = rule(restore[rows, lanes], values, ratio, scale)


def adam(weight, moment, square, grad, rate, decay):
    moment = ADAM_ONE * moment + (1.0 - ADAM_ONE) * grad
    square = ADAM_TWO * square + (1.0 - ADAM_TWO) * grad * grad
    fixed_one = 1.0 - ADAM_ONE**STEP
    fixed_two = 1.0 - ADAM_TWO**STEP
    weight = weight - rate * (
        moment / fixed_one / (jnp.sqrt(square / fixed_two) + ADAM_EPS) + decay * weight
    )
    return (weight, moment, square)


def per_device(
    video,
    video_ids,
    crop_scales,
    labels,
    valid_clips,
    stem_weight,
    lateral_weight,
    condense,
    mixing,
    restore,
    squeeze,
    blending,
    recover,
    head_weight,
    stem_velocity,
    lateral_velocity,
    condense_velocity,
    mixing_velocity,
    restore_velocity,
    squeeze_velocity,
    blending_velocity,
    recover_velocity,
    head_moment,
    head_square,
    affine,
    affine_moment,
    affine_square,
):
    tm_count = lax.axis_size("tm")
    batch_count = lax.axis_size("batch")
    devices = tm_count * batch_count
    far = tm_count // 2
    tm_place = lax.axis_index("tm")
    batch_place = lax.axis_index("batch")
    core = tm_place % 2
    both = ("tm", "batch")

    clips, frames, height = video.shape[0:3]
    spots = height * height
    rows = spots * clips

    def quarter(block):
        part = block.shape[0] // tm_count
        return lax.dynamic_slice_in_dim(block, tm_place * part, part, axis=0)

    def gather(block):
        return lax.all_gather(quarter(block), ("batch", "tm"), axis=0, tiled=True)

    def by_place(items, place):
        whole = jnp.zeros((len(items),) + items[0].shape, items[0].dtype)
        for k, item in enumerate(items):
            whole = lax.dynamic_update_index_in_dim(whole, item, place ^ k, 0)
        return whole

    def over_tm(block):
        held = by_place(
            [block] + [swap(block, "tm", 2 * k) for k in range(1, far)], tm_place // 2
        )
        held = by_place([held, swap(held, "tm", 1)], core)
        return jnp.swapaxes(held, 0, 1).reshape((tm_count,) + block.shape)

    def gather_steps(block):
        held = spread_all(block, ("batch",))
        held = held.reshape(batch_count, -1, block.shape[1])
        held = jnp.swapaxes(over_tm(held), 0, 1)
        return held.reshape(-1, block.shape[1])

    out_rows = condense.shape[0]
    small_rows = squeeze.shape[0]
    weights_low = jnp.concatenate(
        [mixing, lateral_weight, condense]
        + [restore[k * out_rows : (k + 1) * out_rows] for k in range(4)],
        axis=1,
    )
    weights_low = quarter(weights_low).astype(BF16)
    stem_low = quarter(stem_weight).astype(BF16)
    weights_low, stem_low, video = lax.optimization_barrier((weights_low, stem_low, video))
    weights_full = lax.all_gather(weights_low, ("batch", "tm"), axis=0, tiled=True)
    stem_full = gather_steps(stem_low)
    small = jnp.concatenate(
        [squeeze, blending, recover.reshape(small_rows, -1)], axis=1
    ).astype(BF16)
    small_full = spread_all(small, ("batch",)).reshape(CFM, -1)
    squeeze_full = small_full[:, 0 : 3 * CF]
    blending_full = small_full[:, 3 * CF : 3 * CF + 9 * CFM]
    recover_full = small_full[:, 3 * CF + 9 * CFM :].reshape(CF, CFM)
    head_full = gather(head_weight.astype(BF16))

    own_video = jnp.transpose(video, (1, 2, 3, 0, 4)).reshape(frames, rows, -1)
    before = shift(
        jnp.concatenate([own_video[0:1], own_video[frames - 2 :]], axis=0), "tm", 1
    )
    after = shift(own_video[0:1], "tm", -1)
    slow_video = jnp.concatenate([before[0:1], own_video[0:1], after], axis=0)
    fast_video = jnp.concatenate([before[1:], own_video, after], axis=0)

    side = (height - crop_scales).astype(F32)
    places = jnp.arange(height).astype(F32)
    inside = (places[:, None] < side[None, :]).astype(F32)
    mask = (inside[:, None, :] * inside[None, :, :]).reshape(rows, 1)
    area = (side * side)[:, None]
    gains, shifts, class_bias = split_affine(affine)
    par = [jnp.stack([gain, shift]) for gain, shift in zip(gains, shifts)]
    valid = valid_clips.astype(F32)[:, None]
    blend_taps = jnp.transpose(blending_full.reshape(CFM, 9, CFM), (1, 2, 0))
    narrow = ((devices, 8, 256), F32)
    narrow_low = ((devices, 8, 256), BF16)
    total_narrow = ((8, 256), F32)
    wide = ((8, 640), F32)

    def exchange(copies):
        return lax.all_to_all(copies, both, 0, 0, tiled=True)

    def exchange_wide(block):
        return spread_all(block, both).reshape((devices,) + block.shape)

    slow_shape = (rows, CSM)
    fast_shape = (frames, rows, CFM)
    slow_wide = (rows, CS)
    fast_wide = (frames, rows, CF)
    first_shape = ((CSM, 5 * CF + 3 * CS), BF16)
    mixing_shape = ((CSM, 9 * CSM), BF16)
    restore_shape = ((CS, CSM), BF16)
    pad_shape = ((height + 2, height + 2, clips, CSM), F32)
    fast_pad = ((height + 2, height + 2, clips, CFM), F32)

    pieces = batch_count * far
    main_rows = 2048 // pieces
    mixing_rows = 9 * CSM // 2 // pieces
    condense_rows = 3 * CS // 2 // pieces
    far_place = tm_place // 2
    depth_one = condense_rows
    depth_two = CS // 2 // pieces

    def share_of(item, taps, place):
        width = item.shape[1] // taps
        size = width // tm_count
        return jnp.concatenate(
            [
                lax.dynamic_slice_in_dim(item, tap * width + place * size, size, axis=1)
                for tap in range(taps)
            ],
            axis=1,
        ).astype(BF16)

    def sent_columns(item, taps, parts):
        held = []
        start = 0
        shares = [share_of(item, taps, 2 * k + core) for k in range(far)]
        for size, depth in parts:
            for share in shares:
                block = share[:, start : start + size * batch_count]
                block = block.reshape(out_rows, batch_count, size)
                held.append(jnp.pad(block, ((0, 0), (0, 0), (0, depth - size))))
            start = start + size * batch_count
        return jnp.transpose(jnp.concatenate(held, axis=-1), (1, 0, 2))

    lateral_rows = 5 * CF // tm_count // batch_count
    rest_depth = depth_one - main_rows
    speed_send = jnp.concatenate(
        [
            jnp.where(
                far_place == 0,
                sent_columns(
                    condense_velocity, 3, ((main_rows, main_rows), (rest_depth, rest_depth))
                ),
                sent_columns(
                    mixing_velocity,
                    9,
                    ((main_rows, main_rows), (mixing_rows - main_rows, rest_depth)),
                ),
            ),
            sent_columns(lateral_velocity, 5, ((lateral_rows, depth_two),)),
        ],
        axis=-1,
    )
    small_speed = jnp.concatenate(
        [squeeze_velocity, blending_velocity, recover_velocity.reshape(small_rows, -1)], axis=1
    )
    small_speed = small_speed.astype(BF16).reshape(-1, speed_send.shape[-1])
    small_speed = jnp.broadcast_to(small_speed[None], (batch_count,) + small_speed.shape)
    speed_send = jnp.concatenate([speed_send, small_speed], axis=1)
    speed_send, small_full = lax.optimization_barrier((speed_send, small_full))
    speed = lax.all_to_all(speed_send, "batch", 0, 0, tiled=True)

    near = tm_count == 4 and batch_count == 8
    place_cell = tm_place.astype(jnp.int32).reshape(1)
    quarter_shape = (rows, CS // tm_count)
    slow_pre, fast_pre, slow_low, fast_low, *shares = call(
        functools.partial(stem_kernel, near),
        [
            (slow_wide, F32),
            (fast_wide, F32),
            ((3, rows, CS), BF16),
            ((frames + 3, rows, CF), BF16),
        ]
        + (
            [(quarter_shape, BF16)] * 4 + [((5, rows, 128), BF16)] * 2
            if near
            else [((tm_count,) + quarter_shape, BF16)]
        ),
        [place_cell, slow_video, fast_video, stem_full, mask]
        + ([own_video[0]] + [swap(own_video[0], "tm", k) for k in range(1, 4)] if near else []),
        scalars=(0,),
    )
    def in_turn(items, margin=0):
        whole = jnp.zeros((len(items) + 2 * margin,) + items[0].shape, items[0].dtype)
        for k, item in enumerate(items):
            whole = lax.dynamic_update_index_in_dim(whole, item, (tm_place ^ k) + margin, 0)
        return whole

    def share_out(parts, margin=0):
        items = [pick(parts, 0, tm_place)]
        items += [swap(pick(parts, 0, tm_place ^ k), "tm", k) for k in range(1, tm_count)]
        return in_turn(items, margin)

    def every(block, margin=0):
        even = [block] + [swap(block, "tm", 2 * k) for k in range(1, far)]
        odd = swap(jnp.stack(even), "tm", 1)
        items = [item for k in range(far) for item in (even[k], odd[k])]
        return in_turn(items, margin)

    def by_share(block, outer):
        parts = block.reshape(block.shape[0], outer, tm_count, -1)
        return jnp.moveaxis(parts, 2, 0).reshape(tm_count, block.shape[0], -1)

    def swaps(parts):
        return [parts[0]] + [swap(parts[k], "tm", k) for k in range(1, tm_count)]

    def pairs_of(own, given):
        across = swap(given, "tm", 2)
        return [own, across, swap(own, "tm", 1), swap(across, "tm", 1)]

    if near:
        slow_shares = shares[0:4]
        side_shares = pairs_of(shares[4], shares[5])
    else:
        sides = jnp.transpose(fast_low[0:5], (1, 0, 2)).reshape(rows, 5 * CF)
        slow_shares = share_out(shares[0], 1)
        side_shares = share_out(by_share(sides, 5))
    slow_low, speed = lax.optimization_barrier((slow_low, speed))
    h1, h4, sent = call(
        first_kernel,
        [(slow_shape, F32), (fast_shape, F32), narrow],
        [slow_low, fast_low, weights_full, squeeze_full, mask, valid],
        [total_narrow, first_shape],
        far=(2,),
        copies=4,
    )
    act_width = CSM // tm_count
    act_shapes = [((rows, 128), BF16)] * 4 if near else [(slow_shape, BF16)]
    h2, h5, total1, sent, *acts = call(
        functools.partial(second_kernel, near),
        [(slow_shape, F32), (fast_shape, F32), total_narrow, narrow] + act_shapes,
        [place_cell, h1, h4, exchange(sent), par[0], par[3], mask, weights_full, blend_taps],
        [pad_shape, fast_pad, total_narrow, mixing_shape],
        far=(7,),
        copies=9,
        scalars=(0,),
    )
    acts = swaps(acts) if near else share_out(by_share(acts[0], 1))
    a2, a5, h3, h6, total2, sent = call(
        third_kernel,
        [
            (slow_shape, BF16),
            (fast_shape, BF16),
            (slow_wide, F32),
            (fast_wide, F32),
            total_narrow,
            wide,
        ],
        [h2, h5, total1, exchange(sent), par[1], par[4], mask, weights_full, recover_full],
        [restore_shape],
        far=(7,),
        copies=4 * batch_count,
    )
    a2_every = pairs_of(a2, a2) if near else every(a2)
    if near:
        h3, side_shares[1] = lax.optimization_barrier((h3, side_shares[1]))
    else:
        h3, slow_shares, side_shares = lax.optimization_barrier((h3, slow_shares, side_shares))
    pool, total3 = call(
        pool_kernel,
        [((clips, CS + CF), F32), wide],
        [h3, h6, slow_pre, fast_pre, total1, exchange_wide(sent), par[2], par[5], mask],
    )
    if near:
        pools = jnp.stack([pool] + [swap(pool, "tm", k) for k in range(1, tm_count)])
    else:
        pools = spread_all(pool, ("tm",)).reshape(tm_count, clips, CS + CF)
    feature_low, logit_low, d3, d6, sent = call(
        head_kernel,
        [((clips, CS + CF), BF16), ((clips, CLS), BF16), (slow_wide, F32), (fast_wide, F32), wide],
        [
            pools,
            head_full,
            class_bias[None],
            video_ids[:, None],
            video_ids[None],
            labels[:, None],
            valid,
            area,
            h3,
            h6,
            slow_pre,
            fast_pre,
            total1,
            total3,
            par[2],
            par[5],
            mask,
        ],
    )
    d3, acts, a2_every, side_shares = lax.optimization_barrier((d3, acts, a2_every, side_shares))
    u6, e2, e5, back3, sent, *u3 = call(
        functools.partial(third_back_kernel, near),
        [
            (fast_wide, BF16),
            (slow_shape, F32),
            (fast_shape, F32),
            wide,
            narrow_low,
        ]
        + ([(quarter_shape, BF16)] * 4 if near else [(slow_wide, BF16)]),
        [
            place_cell,
            d3,
            d6,
            h3,
            h6,
            h2,
            h5,
            total1,
            total3,
            total2,
            exchange_wide(low(sent)),
            par[2],
            par[5],
            par[1],
            par[4],
            mask,
            weights_full,
            recover_full,
        ],
        [total_narrow, restore_shape],
        far=(16,),
        copies=4 * batch_count,
        scalars=(0,),
    )
    if near:
        (restore_grad,) = call(
            early_kernel,
            [((batch_count, CS // tm_count // batch_count, CSM), BF16)],
            [*swaps(u3), *a2_every],
        )
    else:
        u3_shares = share_out(by_share(u3[0], batch_count))
        restore_grad = low(dot(u3_shares, a2_every, ((0, 1), (0, 1))))
    recover_grad = over_rows(a5.reshape(frames * rows, CFM), u6.reshape(frames * rows, CF))

    u2, u5, e1, e4, blend_grad, back2, sent = call(
        second_back_kernel,
        [
            (slow_shape, BF16),
            (fast_shape, BF16),
            (slow_shape, F32),
            (fast_shape, F32),
            ((9, CFM, CFM), F32),
            total_narrow,
            narrow_low,
        ],
        [
            e2,
            e5,
            h2,
            h5,
            h1,
            h4,
            total2,
            total1,
            exchange(sent),
            par[1],
            par[4],
            par[0],
            par[3],
            mask,
            weights_full,
            blend_taps,
        ],
        [pad_shape, fast_pad, fast_pad, total_narrow, mixing_shape],
        far=(14,),
        copies=9,
    )
    blending_grad = jnp.transpose(blend_grad, (1, 0, 2)).reshape(CFM, 9 * CFM)

    def by_batch(parts):
        return jnp.concatenate(
            [part.reshape(batch_count, -1, part.shape[-1]) for part in parts], axis=1
        )

    def over_batch(view):
        got = lax.all_to_all(view, "batch", 0, 0, tiled=True)
        return jnp.sum(got.reshape(view.shape).astype(F32), axis=0)

    if near:
        (early,) = call(
            mixing_kernel,
            [((batch_count, 208, CSM), BF16)],
            [*acts, *pairs_of(u2, u2), restore_grad],
            [((tm_count, height + 2, height + 2, clips, act_width), F32)],
        )
    else:
        (mixing_grad,) = call(
            mixing_grad_kernel,
            [((9, act_width, CSM), BF16)],
            [acts, every(u2)],
            [((tm_count, height + 2, height + 2, clips, act_width), F32)],
        )
        mixing_grad = mixing_grad.reshape(9 * act_width, CSM)
        main_edge = 8 * act_width
        early = by_batch([mixing_grad[0:main_edge], mixing_grad[main_edge:], restore_grad])
    early, e1 = lax.optimization_barrier((early, e1))
    early = over_batch(early)

    u1, u4, back1 = call(
        first_back_kernel,
        [(slow_shape, BF16), (fast_shape, BF16), total_narrow],
        [e1, e4, h1, h4, total1, exchange(sent), par[0], par[3], mask],
    )
    if near:
        u1_parts = pairs_of(u1, u1)
        u1_held = u1_parts
    else:
        u1_held = every(u1, 1)
    squeeze_grad = jnp.concatenate(
        [dot(u4, fast_low[1 + k : 1 + k + frames], ((0, 1), (0, 1))) for k in range(3)], axis=1
    )
    slow_up, fast_up = call(
        functools.partial(stem_back_kernel, near),
        [(slow_wide, BF16), (fast_wide, BF16)],
        [
            place_cell,
            *(u1_held if near else [u1_held]),
            u4,
            shift(u4[frames - 1], "tm", 1),
            shift(u4[0], "tm", -1),
            weights_full,
            squeeze_full,
            d3,
            d6,
            slow_pre,
            fast_pre,
            mask,
        ],
        [first_shape, ((6,) + slow_shape, BF16)],
        far=(8 if near else 5,),
        copies=4,
        scalars=(0,),
    )
    slow_up, fast_up, u1_held = lax.optimization_barrier((slow_up, fast_up, u1_held))
    if near:
        (late,) = call(
            late_kernel,
            [((batch_count, 240, CSM), BF16)],
            [place_cell, *slow_shares, *side_shares, *u1_held],
            [((6,) + quarter_shape, BF16), ((128, CSM), F32), ((320, CSM), F32)],
            scalars=(0,),
        )
    else:
        u1_inner = u1_held[1 : tm_count + 1]
        cells = ((0, 1), (0, 1))
        condense_grad = [
            low(dot(slow_shares[k : k + tm_count], u1_inner, cells)) for k in range(3)
        ]
        lateral_grad = low(dot(side_shares, u1_inner, cells))
        late = by_batch(
            [jnp.concatenate(condense_grad[0:2]), condense_grad[2], lateral_grad]
        )
    late, early = lax.optimization_barrier((late, early))
    late = over_batch(late)
    clip_count = total1[7, 0] / tm_count
    loss_total = (back3[4, 512] + back3[5, 512] + back3[6, 512]) / tm_count
    slow_back3, fast_back3 = get_wide(back3)
    slow_back2, fast_back2 = get_narrow(back2)
    slow_back1, fast_back1 = get_narrow(back1)
    (b1, g1), (b2, g2), (b3, g3) = [
        [item[0] for item in pair] for pair in (slow_back1, slow_back2, slow_back3)
    ]
    (b4, g4), (b5, g5), (b6, g6) = [
        [item[0] for item in pair] for pair in (fast_back1, fast_back2, fast_back3)
    ]

    main_rows = 2048 // pieces
    mixing_rows = 9 * CSM // 2 // pieces
    condense_rows = 3 * CS // 2 // pieces
    tm_all = bits("tm", 0)
    columns_wide = stem_weight.shape[-1]

    def blocks(item):
        item = jnp.pad(item, ((0, 0), (0, -item.shape[1] % columns_wide)))
        item = item.reshape(batch_count, small_rows, -1, columns_wide)
        return jnp.swapaxes(item, 1, 2)

    small_view = [blocks(item) for item in (squeeze_grad, blending_grad, recover_grad)]
    small_view = jnp.concatenate(small_view, axis=1)
    small_blocks = small_view.shape[1]
    head_rows = head_weight.shape[0]
    feature_parts = jnp.transpose(feature_low.reshape(clips, batch_count, head_rows), (1, 0, 2))
    logit_parts = jnp.broadcast_to(logit_low.reshape(1, -1), (batch_count, clips * CLS))
    riders = jnp.concatenate([feature_parts.reshape(batch_count, -1), logit_parts], axis=1)
    riders = jnp.pad(riders, ((0, 0), (0, -riders.shape[1] % columns_wide)))
    riders = riders.reshape(batch_count, -1, columns_wide)
    if near:
        small_tm = small_view.reshape(batch_count, tm_count, -1, columns_wide)
        small_part = small_tm.shape[2]
        small_tm = jnp.pad(jnp.swapaxes(small_tm, 0, 1), ((0, 0), (0, 0), (0, 6), (0, 0)))
        share_shape = (batch_count, stem_weight.shape[0] // tm_count + 24, columns_wide)
        stem_shares = call(
            stem_grad_kernel,
            [(share_shape, BF16)] * 4,
            [place_cell, slow_up, fast_up, own_video, small_tm],
            [((CS + CF, columns_wide), F32)],
            scalars=(0,),
        )
        stem_shares = swaps(stem_shares)
        stem_shares = low(sum(share.astype(F32) for share in stem_shares))
        riders = jnp.concatenate([stem_shares, riders], axis=1)
        got = [pick(riders, 0, batch_place)] + [
            swap(pick(riders, 0, batch_place ^ k), "batch", k) for k in range(1, batch_count)
        ]
        shards_sum = sum(item[0 : share_shape[1]].astype(F32) for item in got)
        stem_part = share_shape[1] - 24
        stem_shard, small_shard = shards_sum[0:stem_part], shards_sum[stem_part:]
        riders = jnp.stack([item[share_shape[1] :] for item in got])
        riders = riders.reshape(batch_count, -1)
    else:
        stem_grad = jnp.concatenate(
            [over_rows(slow_up, own_video[0]), dot(fast_up, own_video, ((0, 1), (0, 1)))], axis=0
        )
        stem_view = stem_grad.reshape((batch_count,) + (2,) * len(tm_all) + (-1, stem_grad.shape[-1]))
        small_view = small_view.reshape(-1, columns_wide)
        live = list(tm_all)
        for axis, bit in tm_all[::-1]:
            dim = 1 + live.index((axis, bit))
            flag = (tm_place >> bit) & 1
            keep, give = pick(stem_view, dim, flag), pick(stem_view, dim, 1 - flag)
            flat_give = give.reshape(-1, columns_wide)
            count = flat_give.shape[0]
            sent = jnp.concatenate([flat_give, small_view]).astype(BF16)
            sent = lax.optimization_barrier(sent)
            got = swap(sent, axis, 1 << bit)
            stem_view = keep + got[0:count].astype(F32).reshape(keep.shape)
            small_view = sent[count:].astype(F32) + got[count:].astype(F32)
            live.remove((axis, bit))
        small_view = small_view.reshape(batch_count, -1, columns_wide)
        stem_part = stem_view.shape[1]
        late, riders = lax.optimization_barrier((late, riders))
        riders = jnp.concatenate([stem_view.astype(BF16), small_view.astype(BF16), riders], axis=1)
        got = lax.all_to_all(riders, "batch", 0, 0, tiled=True).reshape(batch_count, -1, columns_wide)
        both_parts = stem_part + small_view.shape[1]
        shards_sum = jnp.sum(got[:, 0:both_parts].astype(F32), axis=0)
        stem_shard, small_shard = shards_sum[0:stem_part], shards_sum[stem_part:]
        riders = got[:, both_parts:].reshape(batch_count, -1)
    feature_size = clips * head_rows
    feature_all = riders[:, 0:feature_size].reshape(batch_count * clips, head_rows)
    logit_all = riders[:, feature_size : feature_size + clips * CLS]
    logit_all = logit_all.reshape(batch_count * clips, CLS)
    mixing_shard, restore_shard = early[0:mixing_rows], early[mixing_rows:]
    condense_shard = late[0:condense_rows]
    lateral_shard = late[condense_rows : condense_rows + lateral_rows]
    head_grad = over_rows(feature_all, logit_all)
    class_grad = jnp.sum(logit_all.astype(F32), axis=0)
    affine_grad = jnp.concatenate([g1, g2, g3, g4, g5, g6, b1, b2, b3, b4, b5, b6, class_grad])

    small_speed = jnp.concatenate(
        [squeeze_velocity, blending_velocity, recover_velocity.reshape(small_rows, -1)], axis=1
    )
    small_speed = spread_all(small_speed.astype(BF16), ("batch",)).reshape(CFM, -1)

    leader = (tm_place == 0).astype(F32)
    squares = sum(jnp.sum(item * item) for item in (late, early, stem_shard))
    small_share = 1.0 if near else leader
    squares = squares + small_share * jnp.sum(small_shard * small_shard)
    squares = squares + leader * jnp.sum(head_grad * head_grad)
    first_device = leader * (batch_place == 0).astype(F32)
    squares = squares + first_device * jnp.sum(affine_grad * affine_grad)
    (total_squares,) = all_sum([squares], both)
    grad_norm = jnp.sqrt(total_squares) / clip_count
    factor = jnp.minimum(1.0, CLIP_AT / grad_norm) / clip_count

    small_speed = speed[:, out_rows:].reshape(CFM, -1)
    stem_rows = stem_weight.shape[0]
    if near:
        stem_own = over_tm(low(stem_shard)).reshape(stem_rows, -1)
    else:
        stem_own = over_tm(low(stem_shard)).reshape(stem_rows, -1)

    def small_parts(small_whole):
        small_whole = small_whole.reshape(batch_count, small_blocks, small_rows, columns_wide)
        small_whole = jnp.swapaxes(small_whole, 1, 2).reshape(CFM, -1)
        small_grads = unpack(small_whole[:, 0 : 3 * CF + 9 * CFM + CF])
        speeds = unpack(small_speed)
        speeds = (speeds[0], speeds[1], speeds[2].reshape(CF, CFM).T)
        items = [
            low(MUON_KEEP * held.astype(F32) + grad.astype(F32) * factor)
            for held, grad in zip(speeds, small_grads)
        ]
        return small_grads, items

    def unpack(values):
        first = values[:, 0 : 3 * CF]
        second = values[:, 3 * CF : 3 * CF + 9 * CFM]
        return (first, second, values[:, 3 * CF + 9 * CFM :])

    def ratio_of(base):
        return math.sqrt(max(1.0, base.shape[0] * batch_count / base.shape[1]))

    def own(values, part):
        return lax.dynamic_slice_in_dim(values, batch_place * part, part, axis=0)

    def direct_orthos(stem_moved, shapes, items):
        tall_part = recover.shape[0]
        results = (
            rows_by_columns(stem_moved, shapes[0]),
            rows_by_columns(own(shapes[1], small_rows), items[0]),
            rows_by_columns(own(shapes[2], small_rows), items[1]),
            rows_by_columns(own(items[2].T, tall_part), shapes[3]),
        )
        return [low(result) for result in results]

    far_place = tm_place // 2
    factor_cell = factor.reshape(1, 1)
    bases = {
        carry: (lateral_velocity, condense_velocity, mixing_velocity, restore_velocity),
        renew: (lateral_weight, condense, mixing, restore),
    }

    def deep(item, depth):
        return jnp.pad(item, ((0, depth - item.shape[0]), (0, 0)))

    if near:
        pair_one = low(jnp.concatenate([condense_shard, restore_shard]))
        pair_two = low(
            jnp.concatenate([deep(mixing_shard, depth_one), deep(lateral_shard, depth_two)])
        )
        pair_own = jnp.where(far_place == 0, pair_one, pair_two)
        pair_got = swap(jnp.where(far_place == 0, pair_two, pair_one), "tm", 2)
        restore_speed = pick(restore_velocity.reshape(far, 2, depth_two, CSM), 1, core)
        restore_speed = low(restore_speed.reshape(far * depth_two, CSM))
        wide_shape = ((batch_count, out_rows, CSM), BF16)
        tall_shape = ((batch_count, out_rows, far * depth_two), BF16)
        gram_shape = ((CSM, CSM), BF16)
        moved_one, moved_two, stem_moved, keep, give, stem_gram, grad_wide, grad_tall = call(
            gram_kernel,
            [
                ((far * depth_one, CSM), BF16),
                ((far * depth_two, CSM), BF16),
                (stem_own.shape, BF16),
                ((320, CSM), BF16),
                ((320, CSM), BF16),
                ((batch_count, 16, CSM), BF16),
                wide_shape,
                tall_shape,
            ],
            [
                place_cell,
                factor_cell,
                speed,
                restore_speed,
                pair_own,
                pair_got,
                stem_velocity,
                stem_own,
            ],
            [((CSM, CSM), F32)],
            scalars=(0,),
        )
        gram = low(keep.astype(F32) + swap(give, "tm", 1).astype(F32))
        riders = low(small_shard)
        riders = jnp.concatenate(
            [
                jnp.pad(riders[0:16], ((0, 0), (0, 64))),
                jnp.pad(riders[16:24], ((0, 8), (0, 64))),
            ],
            axis=1,
        )
        riders = jnp.broadcast_to(riders[None], (batch_count,) + riders.shape)
        got = lax.all_to_all(
            jnp.concatenate([gram.reshape(batch_count, 40, CSM), stem_gram, riders], axis=1),
            "batch", 0, 0, tiled=True,
        )
        summed = low(jnp.sum(got[:, 0:56].astype(F32), axis=0))
        summed = jnp.pad(summed, ((0, 8), (0, 0)))
        small_whole = jnp.concatenate([got[:, 56:72, 0:192], got[:, 56:64, 256:448]], axis=1)
        small_whole = over_tm(small_whole)[:, :, 0:small_part]
        small_grads, items = small_parts(jnp.swapaxes(small_whole, 0, 1))
        whole = lax.all_to_all(
            jnp.concatenate(
                [grad_wide, jnp.broadcast_to(summed[None], (batch_count,) + summed.shape)], axis=1
            ),
            "batch", 0, 0, tiled=True,
        )
        shaped, *shapes = call(
            block_shape_kernel,
            [gram_shape, ((192, 192), BF16)] + [((CFM, CFM), BF16)] * 3,
            [whole] + [rows_by_rows(item, item) for item in items],
            [((CSM, CSM), F32), ((192, 192), F32), ((320, CSM), F32)],
            micros=10,
        )

        def put_rows(rule, held, tall):
            edge = far * depth_one
            second = jnp.where(far_place == 0, tall, held[..., edge:])
            held = jnp.concatenate([held[..., 0:edge], second], axis=-1)
            kernel = functools.partial(place_kernel, rule, far, main_rows, depth_one)
            return call(
                kernel,
                [(base.shape, F32) for base in bases[rule]],
                [place_cell, factor_cell, *pairs_of(held, held), *bases[rule]],
                [((tm_count,) + wide_shape[0], BF16)],
                scalars=(0,),
            )

        grads = put_rows(carry, whole[:, 0:64], grad_tall)
        ortho_wide, ortho_tall = call(
            ortho_kernel,
            [wide_shape, tall_shape],
            [place_cell, shaped, swap(shaped, "tm", 1), moved_one, moved_two],
            scalars=(0,),
        )
        ortho_wide = lax.all_to_all(ortho_wide, "batch", 0, 0, tiled=True)
        direct = direct_orthos(stem_moved, shapes, items)
        tied = lax.optimization_barrier((ortho_wide, *grads, *direct))
        ortho_wide, grads, direct = tied[0], tied[1:5], tied[5:]
        orthos = put_rows(renew, ortho_wide, ortho_tall)
    else:
        pair_one = jnp.concatenate([condense_shard, deep(restore_shard, depth_two)])
        pair_two = jnp.concatenate([deep(mixing_shard, depth_one), deep(lateral_shard, depth_two)])
        pairs = jnp.stack([pair_one, pair_two] + [jnp.zeros_like(pair_one)] * (far - 2)).astype(BF16)
        grads_held = by_place(
            [pick(pairs, 0, far_place)]
            + [swap(pick(pairs, 0, far_place ^ k), "tm", 2 * k) for k in range(1, far)],
            far_place,
        )

        def cut(held):
            one = jnp.concatenate(
                [
                    held[:, 0:main_rows].reshape(far * main_rows, CSM),
                    held[:, main_rows:depth_one].reshape(far * (depth_one - main_rows), CSM),
                ]
            )
            return one, held[:, depth_one:].reshape(far * depth_two, CSM)

        speed = speed[:, 0:out_rows].reshape(CSM, -1)
        speed_one = speed[:, 0 : far * depth_one].T
        restore_speed = pick(restore_velocity.reshape(far, 2, depth_two, CSM), 1, core)
        restore_speed = restore_speed.reshape(far * depth_two, CSM)
        speed_two = jnp.where(
            far_place == 0, restore_speed.astype(BF16), speed[:, far * depth_one :].T
        )
        grad_one, grad_two = cut(grads_held)
        used = far_place < 2

        def step_of(speed_part, grad_part):
            moved = MUON_KEEP * speed_part.astype(F32) + grad_part.astype(F32) * factor
            return jnp.where(used, moved, 0.0).astype(BF16)

        stem_moved = low(MUON_KEEP * stem_velocity + stem_own.astype(F32) * factor)

        moved_one = step_of(speed_one, grad_one)
        moved_two = step_of(speed_two, grad_two)
        gram_one = over_rows(moved_one, moved_one)
        gram_two = over_rows(moved_two, moved_two)
        gram = jnp.where(core == 0, gram_one, gram_two) + swap(
            jnp.where(core == 0, gram_two, gram_one), "tm", 1
        )
        stem_gram = over_rows(stem_moved, stem_moved)

        def flat_rows(item):
            return item.reshape(batch_count, -1).astype(GRAM)

        parts = [flat_rows(gram), flat_rows(stem_gram)]
        sizes = [part.shape[1] for part in parts]
        riders = jnp.broadcast_to(small_shard.reshape(1, -1).astype(GRAM), (batch_count, small_shard.size))

        def packed(items):
            whole = jnp.concatenate(items, axis=1)
            whole = jnp.pad(whole, ((0, 0), (0, -whole.shape[1] % 2048)))
            return whole.reshape(batch_count, -1, 256)

        def exchanged(items):
            whole = lax.all_to_all(packed(items), "batch", 0, 0, tiled=True)
            return whole.reshape(batch_count, -1)

        got = exchanged(parts + [riders])
        summed = jnp.sum(got[:, 0 : sum(sizes)].astype(F32), axis=0, keepdims=True).astype(GRAM)
        small_whole = got[:, sum(sizes) : sum(sizes) + small_shard.size]
        small_grads, items = small_parts(small_whole)
        grad_one, grad_two, summed = lax.optimization_barrier((grad_one, grad_two, summed))
        whole = exchanged([jnp.broadcast_to(summed, (batch_count, summed.shape[1]))]).astype(F32)
        gram = whole[:, 0 : sizes[0]].reshape(CSM, CSM)
        stem_gram = whole[:, sizes[0] : sum(sizes)].reshape(stem_gram.shape)

        shaped, *shapes = shape_of([gram, stem_gram] + [rows_by_rows(item, item) for item in items])
        shaped = low(shaped)
        shapes = [low(shape) for shape in shapes]
        shaped_other = swap(shaped, "tm", 1)
        shape_one = jnp.where(core == 0, shaped, shaped_other)
        shape_two = jnp.where(core == 0, shaped_other, shaped)

        def spread_rows(rule, bases, wide_one, wide_two, tall_two):
            lateral_base, condense_base, mixing_base, restore_base = bases
            wide_both = jnp.concatenate([wide_one, wide_two], axis=1)
            wide_both = wide_both.reshape(batch_count, out_rows, -1)
            held = lax.all_to_all(wide_both, "batch", 0, 0, tiled=True)
            width = far * depth_two
            tall = jnp.concatenate(
                [tall_two[:, k * width : (k + 1) * width] for k in range(CSM // width)], axis=0
            ).reshape(batch_count, out_rows, width)
            second = jnp.where(far_place == 0, tall, held[..., far * depth_one :])
            held = jnp.concatenate([held[..., 0 : far * depth_one], second], axis=-1)
            held = by_place(
                [held] + [swap(held, "tm", 2 * k) for k in range(1, far)], far_place
            )[0:2]
            other = swap(held, "tm", 1)
            held = (jnp.where(core == 0, held, other), jnp.where(core == 0, other, held))

            edge = far * main_rows
            stop = far * depth_one
            def taps_of(place, base, main_taps, size):
                block = jnp.stack([half[place] for half in held])
                main = block[..., 0:edge].reshape(
                    2, main_taps, batch_count // main_taps, out_rows, far, main_rows
                )
                main = jnp.transpose(main, (3, 1, 4, 0, 2, 5)).reshape(out_rows, -1)
                rest = block[..., edge:stop].reshape(
                    2, batch_count, out_rows, far, depth_one - main_rows
                )[..., 0:size]
                rest = jnp.transpose(rest, (2, 3, 0, 1, 4)).reshape(out_rows, -1)
                return jnp.concatenate([main, rest], axis=1)

            block = jnp.stack([half[1, :, :, stop:] for half in held])
            block = block.reshape(2, batch_count, out_rows, far, depth_two)[..., 0:lateral_rows]
            block = jnp.transpose(block, (2, 3, 0, 1, 4)).reshape(out_rows, tm_count, 5, -1)
            side_rows = jnp.swapaxes(block, 1, 2).reshape(out_rows, 5 * CF)
            tall_rows = []
            for half in held:
                block = half[0, :, :, stop:].reshape(CSM // width, width, width)
                block = jnp.concatenate([block[k] for k in range(CSM // width)], axis=1)
                tall_rows.append(block.reshape(far, depth_two, CSM))
            tall_rows = jnp.stack(tall_rows, axis=1).reshape(-1, CSM)
            results = (
                side_rows,
                taps_of(0, condense_base, 2, rest_depth),
                taps_of(1, mixing_base, 8, mixing_rows - main_rows),
                tall_rows,
            )
            return [rule(base, item.astype(F32), ratio_of(base), factor) for base, item in zip(bases, results)]

        grads = spread_rows(
            carry, bases[carry],
            grad_one.T, grad_two.T, grad_two,
        )
        orthos = spread_rows(
            renew, bases[renew],
            low(rows_by_rows(shape_one, moved_one)),
            low(rows_by_rows(shape_two, moved_two)),
            low(rows_by_columns(moved_two, shape_two)),
        )

    if not near:
        direct = direct_orthos(stem_moved, shapes, items)
    stem_ortho, *small_orthos = direct
    part = recover.shape[0]
    small_own = [
        own(small_grads[0], small_rows),
        own(small_grads[1], small_rows),
        own(small_grads[2].T, part),
    ]

    def both_of(weight, speed, grad, ortho):
        ortho = low(ortho).astype(F32)
        return (
            carry(speed, grad.astype(F32), 1.0, factor),
            renew(weight, ortho, ratio_of(weight), factor),
        )

    stem_pair = both_of(stem_weight, stem_velocity, stem_own, stem_ortho)
    small_pairs = [
        both_of(*items)
        for items in zip(
            (squeeze, blending, recover),
            (squeeze_velocity, blending_velocity, recover_velocity),
            small_own,
            small_orthos,
        )
    ]
    carried = [stem_pair[0], *grads] + [pair[0] for pair in small_pairs]
    updated = [stem_pair[1], *orthos] + [pair[1] for pair in small_pairs]
    head_new, head_first, head_second = adam(
        head_weight, head_moment, head_square, head_grad * factor, HEAD_RATE, WEIGHT_DECAY
    )
    affine_new, affine_first, affine_second = adam(
        affine, affine_moment, affine_square, affine_grad * factor, AFFINE_RATE, 0.0
    )
    return (
        *carried,
        *updated,
        head_new,
        head_first,
        head_second,
        affine_new,
        affine_first,
        affine_second,
        loss_total,
        clip_count,
        grad_norm,
    )


def solution(mesh):
    in_specs = (
        P("batch", "tm", None, None, None),
        P("batch"),
        P("batch"),
        P("batch"),
        P("batch"),
        P("batch", None),
        P("batch", None),
        P("batch", None),
        P("batch", None),
        P("batch", None),
        P("batch", None),
        P("batch", None),
        P("batch", None),
        P("batch", None),
        P("batch", None),
        P("batch", None),
        P("batch", None),
        P("batch", None),
        P("batch", None),
        P("batch", None),
        P("batch", None),
        P("batch", None),
        P("batch", None),
        P("batch", None),
        P(),
        P(),
        P(),
    )
    out_specs = (
        P("batch", None),
        P("batch", None),
        P("batch", None),
        P("batch", None),
        P("batch", None),
        P("batch", None),
        P("batch", None),
        P("batch", None),
        P("batch", None),
        P("batch", None),
        P("batch", None),
        P("batch", None),
        P("batch", None),
        P("batch", None),
        P("batch", None),
        P("batch", None),
        P("batch", None),
        P("batch", None),
        P("batch", None),
        P(),
        P(),
        P(),
        P(),
        P(),
        P(),
    )
    return jax.shard_map(
        per_device, mesh=mesh, in_specs=in_specs, out_specs=out_specs, check_vma=False
    )
```
